32 devices in a mesh: replica: 8 (over y, x, core), dp: 4 (over z).
Axes of the slice: x: 2, y: 2, z: 4, core: 2. Of those that a mesh axis runs over, the one named last changes fastest.
Arguments:
- block_input: bfloat16 [64, 288, 680], P(('replica', 'dp')), may hold values from -40 to 40
- time_shift: bfloat16 [64, 680], P(('replica', 'dp')), may hold values from -4 to 4
- out_grad: bfloat16 [64, 288, 680], P(('replica', 'dp')), may hold values from -6 to 6
- params: float32 [8, 680, 680], P('replica', 'dp'), may hold values from -0.21875 to 0.21875
- first_moment: float32 [8, 680, 680], P('replica', 'dp'), may hold values from -8 to 8
- second_moment: float32 [8, 680, 680], P('replica', 'dp'), may hold values from 1 to 20
- push_weight: float32 [8], P('replica'), may hold values from 0.5 to 2
- step: int32 [1], replicated, may hold values from 0 to 999
Outputs:
- grad_input: bfloat16 [64, 288, 680], P(('replica', 'dp'))
- new_params: float32 [8, 680, 680], P('replica', 'dp')
- new_first: float32 [8, 680, 680], P('replica', 'dp')
- new_second: float32 [8, 680, 680], P('replica', 'dp')
- new_weight: float32 [8], P('replica')
The draws below stay inside these ranges and needn't reach their ends.
All inputs are finite; a program needn't handle non-finite values.
Results may differ from the reference program's by a relative error of at most 0.006.
Values may be sent and summed in bfloat16 or wider, within the bound.
No kernel may reach another device: no remote copies, remote signals or barrier semaphores. Data moves between devices by JAX's collectives and lax.ppermute only.
A program may use at most 64 MiB of HBM per device.

```python
import math
import jax
import jax.numpy as jnp
from jax import lax

C = 680
GSIZE = 40
POS = 288
SAMPLES = 2
BATCH = 64
N_REPLICA = 8
N_DP = 4


def draw_block_input(key, part):
    key_rows, key_chans, key_base = jax.random.split(key, 3)
    row_scale = jnp.exp(jax.random.uniform(key_rows, (BATCH, POS, 1), jnp.float32, 0.0, math.log(10.0)))
    channel_scale = jnp.exp(jax.random.uniform(key_chans, (1, 1, C), jnp.float32, 0.0, math.log(10.0)))
    multiplier = row_scale * channel_scale / 10.0
    drawn = jax.random.truncated_normal(key_base, -4.0, 4.0, (BATCH, POS, C), jnp.float32) * multiplier
    return drawn.astype(jnp.bfloat16)


def block_levels(stream_key, dims, shards, least, high):
    loudness = 1.0
    for position, blocks in shards:
        heights = jax.random.uniform(jax.random.fold_in(jax.random.fold_in(stream_key, 6), position), (blocks,), jnp.float32, least / len(shards), high / len(shards))
        loudness = loudness * jnp.repeat(jnp.exp(heights), dims[position] // blocks).reshape((-1,) + (1,) * (len(dims) - 1 - position))
    return loudness


def bell_draw(stream_key, shape, width, bound, cuts=(), kind=jnp.bfloat16):
    gain = block_levels(stream_key, shape, cuts, -0.22, 0.18) if cuts else 1.0
    entries = jax.random.normal(stream_key, shape, jnp.float32) * width * gain
    return jnp.minimum(jnp.maximum(entries, -bound), bound).astype(kind)


def setup_inputs(seed: int = 0) -> dict:
    streams_of = jax.random.split(jax.random.key(seed), 9)
    block_input = draw_block_input(jax.random.fold_in(streams_of[8], 71), 0)
    time_shift = bell_draw(streams_of[1], (BATCH, C), 1.0, 4.0, ((0, 32),))
    out_grad = bell_draw(streams_of[2], (BATCH, POS, C), 1.0, 6.0, ((0, 32),))
    params = bell_draw(streams_of[3], (N_REPLICA, C, C), C ** -0.5, 0.21875, ((0, 8), (1, 4)), jnp.float32)
    first_moment = bell_draw(streams_of[4], (N_REPLICA, C, C), 2.0, 8.0, ((0, 8), (1, 4)), jnp.float32)
    second_moment = jnp.clip(jnp.exp(math.log(20.0) - 2.9957323 * jax.random.uniform(streams_of[5], (N_REPLICA, C, C), jnp.float32) ** block_levels(streams_of[5], (N_REPLICA, C, C), ((0, 8), (1, 4)), -0.2, 0.2)), 1.0, 20.0)
    push_weight = jnp.clip(jnp.exp(math.log(2.0) - 1.3862944 * jax.random.uniform(streams_of[6], (N_REPLICA,), jnp.float32) ** block_levels(streams_of[6], (N_REPLICA,), ((0, 8),), -0.2, 0.2)), 0.5, 2.0)
    step = jax.random.randint(streams_of[7], (1,), 0, 1000).astype(jnp.int32)
    return dict(block_input=block_input, time_shift=time_shift, out_grad=out_grad, params=params, first_moment=first_moment, second_moment=second_moment, push_weight=push_weight, step=step)


NORM_EPS = 1e-05
BETA_ONE = 0.9
BETA_TWO = 0.999
LEARN_RATE = 0.002
ADAM_EPS = 1e-08

def norm_stats(values):
    grouped = values.reshape(values.shape[0], values.shape[1], -1, GSIZE)
    average = lax.optimization_barrier(jnp.mean(grouped, axis=(1, 3), keepdims=True))
    centered = grouped - average
    variance = lax.optimization_barrier(jnp.mean(centered * centered, axis=(1, 3), keepdims=True))
    inverse = lax.rsqrt(variance + NORM_EPS)
    return ((centered * inverse).reshape(values.shape), inverse)

def norm_back(grad_val, normed, inverse):
    shape_full = grad_val.shape
    grouped = grad_val.reshape(shape_full[0], shape_full[1], -1, GSIZE)
    normed_grp = normed.reshape(grouped.shape)
    first_mean = lax.optimization_barrier(jnp.mean(grouped, axis=(1, 3), keepdims=True))
    second_mean = lax.optimization_barrier(jnp.mean(grouped * normed_grp, axis=(1, 3), keepdims=True))
    return (inverse * (grouped - first_mean - normed_grp * second_mean)).reshape(shape_full)

def silu_grad(values):
    sigmoid_v = jax.nn.sigmoid(values)
    return sigmoid_v * (1.0 + values * (1.0 - sigmoid_v))

def reference(block_input, time_shift, out_grad, params, first_moment, second_moment, push_weight, step):
    replica_samples = SAMPLES * N_DP

    def per_replica(replica):
        first_row = (replica * replica_samples).astype(jnp.int32)
        inputs = lax.dynamic_slice_in_dim(block_input, first_row, replica_samples, 0)
        shifts = lax.dynamic_slice_in_dim(time_shift, first_row, replica_samples, 0)
        out_grads = lax.dynamic_slice_in_dim(out_grad, first_row, replica_samples, 0)
        weight = (params[replica] / push_weight[replica]).astype(jnp.bfloat16)
        normed_in, inverse_in = norm_stats(inputs.astype(jnp.float32))
        activation = jax.nn.silu(normed_in).astype(jnp.bfloat16)
        flat_act = activation.reshape(-1, C)
        hidden = jnp.dot(flat_act, weight, preferred_element_type=jnp.float32).reshape(inputs.shape)
        hidden = hidden + shifts.astype(jnp.float32)[:, None, :]
        normed_mid, inverse_mid = norm_stats(hidden)
        grad_mid = out_grads.astype(jnp.float32) * silu_grad(normed_mid)
        grad_hidden = norm_back(grad_mid, normed_mid, inverse_mid).astype(jnp.bfloat16).reshape(-1, C)
        weight_grad = lax.dot_general(flat_act, grad_hidden, (((0,), (0,)), ((), ())), preferred_element_type=jnp.float32)
        grad_act = jnp.dot(grad_hidden, weight.T, preferred_element_type=jnp.float32).reshape(inputs.shape)
        grad_input = norm_back(grad_act * silu_grad(normed_in), normed_in, inverse_in).astype(jnp.bfloat16)
        return (grad_input, weight_grad / N_DP)
    grad_input, grad = lax.map(per_replica, jnp.arange(N_REPLICA, dtype=jnp.int32))
    grad_input = grad_input.reshape(BATCH, POS, C)
    step_count = (step[0] + 1).astype(jnp.float32)
    first_new = BETA_ONE * first_moment + (1.0 - BETA_ONE) * grad
    second_new = BETA_TWO * second_moment + (1.0 - BETA_TWO) * grad * grad
    update = LEARN_RATE * (first_new / (1.0 - jnp.power(BETA_ONE, step_count)))
    update = update / (jnp.sqrt(second_new / (1.0 - jnp.power(BETA_TWO, step_count))) + ADAM_EPS)
    moved = params - update
    level_count = N_REPLICA.bit_length() - 1
    distance = jnp.left_shift(jnp.ones((), jnp.int32), step[0] % level_count)
    source = (jnp.arange(N_REPLICA, dtype=jnp.int32) - distance) % N_REPLICA
    new_params = 0.5 * (moved + jnp.take(moved, source, axis=0))
    new_weight = 0.5 * (push_weight + jnp.take(push_weight, source, axis=0))
    return (grad_input, new_params, first_new, second_new, new_weight)
```

```python
import functools

import jax
import jax.numpy as jnp
from jax import lax
from jax.experimental import pallas as pl
from jax.experimental.pallas import tpu as pltpu
from jax.sharding import PartitionSpec as P

GSIZE = 40

NORM_EPS = 1e-05
BETA_ONE = 0.9
BETA_TWO = 0.999
LEARN_RATE = 0.002
ADAM_EPS = 1e-08

VMEM_BYTES = 48 * 1024 * 1024


def whole_in_vmem(count):
    return [pl.BlockSpec(memory_space=pltpu.VMEM)] * count


def group_sums(rows, same_group):
    high = rows.astype(jnp.bfloat16)
    rest = rows - high.astype(jnp.float32)
    middle = rest.astype(jnp.bfloat16)
    low = (rest - middle.astype(jnp.float32)).astype(jnp.bfloat16)
    count = rows.shape[0]
    stacked = jnp.concatenate([high.astype(jnp.float32), middle.astype(jnp.float32), low.astype(jnp.float32)], axis=0)
    sums = jnp.dot(stacked.astype(jnp.bfloat16), same_group, preferred_element_type=jnp.float32)
    return sums[:count] + (sums[count : 2 * count] + sums[2 * count :])


def position_sums(parts):
    return jnp.concatenate([jnp.sum(part, axis=0, keepdims=True) for part in parts], axis=0)


def sigmoid(values):
    return 0.5 * jnp.tanh(0.5 * values) + 0.5


def silu_grad(values):
    gate = sigmoid(values)
    return gate * (1.0 + values * (1.0 - gate))


def norm_in_kernel(x_ref, same_group_ref, act_ref, mean_ref, inverse_ref):
    samples, positions, channels = x_ref.shape
    entries = positions * GSIZE
    same_group = same_group_ref[...]
    parts = [x_ref[i].astype(jnp.float32) for i in range(samples)]
    mean = group_sums(position_sums(parts), same_group) / entries
    centered = [parts[i] - mean[i : i + 1] for i in range(samples)]
    variance = group_sums(position_sums([part * part for part in centered]), same_group) / entries
    inverse = lax.rsqrt(variance + NORM_EPS)
    mean_ref[...] = mean
    inverse_ref[...] = inverse
    for i in range(samples):
        normed = centered[i] * inverse[i : i + 1]
        act_ref[i * positions : (i + 1) * positions, :] = (normed * sigmoid(normed)).astype(jnp.bfloat16)


def mix_kernel(shards, me_ref, act_ref, act_t_ref, shift_ref, out_grad_ref, same_group_ref, *refs):
    weight_refs, refs = refs[:shards], refs[shards:]
    grad_hidden_ref, weight_ref, own_ref = refs[:3]
    send_refs, rows_ref = refs[3 : 2 + shards], refs[2 + shards]
    samples, positions, columns = out_grad_ref.shape
    rows = own_ref.shape[0]
    entries = positions * GSIZE
    turn = me_ref[0] * rows
    for slot, shard_ref in enumerate(weight_refs):
        rows_ref[slot * rows : (slot + 1) * rows, :] = shard_ref[...].astype(jnp.float32)
    weight = pltpu.roll(rows_ref[...], turn, 0).astype(jnp.bfloat16)
    weight_ref[...] = weight
    same_group = same_group_ref[:columns, :columns]
    hidden = jnp.dot(act_ref[...], weight, preferred_element_type=jnp.float32)
    parts = [
        hidden[i * positions : (i + 1) * positions] + shift_ref[i : i + 1, :].astype(jnp.float32)
        for i in range(samples)
    ]
    mean = group_sums(position_sums(parts), same_group) / entries
    parts = [parts[i] - mean[i : i + 1] for i in range(samples)]
    variance = group_sums(position_sums([part * part for part in parts]), same_group) / entries
    inverse = lax.rsqrt(variance + NORM_EPS)
    normed = [parts[i] * inverse[i : i + 1] for i in range(samples)]
    grads = [out_grad_ref[i].astype(jnp.float32) * silu_grad(normed[i]) for i in range(samples)]
    means = group_sums(
        jnp.concatenate(
            [position_sums(grads), position_sums([g * n for g, n in zip(grads, normed)])], axis=0
        ),
        same_group,
    ) / entries
    for i in range(samples):
        first, second = means[i : i + 1], means[samples + i : samples + i + 1]
        grad_hidden_ref[i * positions : (i + 1) * positions, :] = (
            inverse[i : i + 1] * (grads[i] - first - normed[i] * second)
        ).astype(jnp.bfloat16)
    grad = jnp.dot(act_t_ref[...], grad_hidden_ref[...], preferred_element_type=jnp.float32)
    rows_ref[...] = pltpu.roll(grad, rows * shards - turn, 0)
    own_ref[...] = rows_ref[:rows, :]
    for slot, send_ref in enumerate(send_refs, 1):
        send_ref[...] = rows_ref[slot * rows : (slot + 1) * rows, :].astype(jnp.bfloat16)


def input_grad_kernel(pieces, x_ref, mean_ref, inverse_ref, same_group_ref, *refs):
    grad_refs, weight_refs, out_ref = refs[:pieces], refs[pieces : 2 * pieces], refs[2 * pieces]
    samples, positions, channels = x_ref.shape
    entries = positions * GSIZE
    grad_act = sum(
        lax.dot_general(
            grad_ref[...], weight_ref[...], (((1,), (1,)), ((), ())), preferred_element_type=jnp.float32
        )
        for grad_ref, weight_ref in zip(grad_refs, weight_refs)
    )
    inverse = inverse_ref[...]
    normed = [
        (x_ref[i].astype(jnp.float32) - mean_ref[i : i + 1, :]) * inverse[i : i + 1] for i in range(samples)
    ]
    grads = [grad_act[i * positions : (i + 1) * positions] * silu_grad(normed[i]) for i in range(samples)]
    means = group_sums(
        jnp.concatenate(
            [position_sums(grads), position_sums([g * n for g, n in zip(grads, normed)])], axis=0
        ),
        same_group_ref[...],
    ) / entries
    for i in range(samples):
        first, second = means[i : i + 1], means[samples + i : samples + i + 1]
        out_ref[i] = (inverse[i : i + 1] * (grads[i] - first - normed[i] * second)).astype(jnp.bfloat16)


def kernel_options():
    return pltpu.CompilerParams(vmem_limit_bytes=VMEM_BYTES)


def work(tokens, deep, wide, products=1):
    return pl.CostEstimate(
        flops=2 * products * tokens * deep * wide, bytes_accessed=8 * tokens * wide, transcendentals=tokens * wide
    )


def norm_in(block_input, same_group):
    samples, positions, channels = block_input.shape
    return pl.pallas_call(
        norm_in_kernel,
        out_shape=(
            jax.ShapeDtypeStruct((samples * positions, channels), jnp.bfloat16),
            jax.ShapeDtypeStruct((samples, channels), jnp.float32),
            jax.ShapeDtypeStruct((samples, channels), jnp.float32),
        ),
        in_specs=whole_in_vmem(2),
        out_specs=tuple(whole_in_vmem(3)),
        compiler_params=kernel_options(),
        cost_estimate=work(samples * positions, 8, channels),
        name="norm_in",
    )(block_input, same_group)


def mix(me, activation, activation_t, shift, out_grad, same_group, weights):
    shards = len(weights)
    rows, columns = weights[0].shape
    tokens, channels = activation.shape
    return pl.pallas_call(
        functools.partial(mix_kernel, shards),
        out_shape=(
            jax.ShapeDtypeStruct((tokens, columns), jnp.bfloat16),
            jax.ShapeDtypeStruct((channels, columns), jnp.bfloat16),
            jax.ShapeDtypeStruct((rows, columns), jnp.float32),
        )
        + (jax.ShapeDtypeStruct((rows, columns), jnp.bfloat16),) * (shards - 1),
        in_specs=[pl.BlockSpec(memory_space=pltpu.SMEM)] + whole_in_vmem(5 + shards),
        out_specs=tuple(whole_in_vmem(2 + shards)),
        scratch_shapes=[pltpu.VMEM((channels, columns), jnp.float32)],
        compiler_params=kernel_options(),
        cost_estimate=work(tokens, channels, columns, 2),
        name="mix",
    )(me, activation, activation_t, shift, out_grad, same_group, *weights)


def input_grad(block_input, mean, inverse, same_group, grads, weights):
    samples, positions, channels = block_input.shape
    return pl.pallas_call(
        functools.partial(input_grad_kernel, len(grads)),
        out_shape=jax.ShapeDtypeStruct(block_input.shape, jnp.bfloat16),
        in_specs=whole_in_vmem(4 + 2 * len(grads)),
        out_specs=pl.BlockSpec(memory_space=pltpu.VMEM),
        compiler_params=kernel_options(),
        cost_estimate=work(samples * positions, channels, channels),
        name="input_grad",
    )(block_input, mean, inverse, same_group, *grads, *weights)


def moved_on(block, axis, distance):
    size = lax.axis_size(axis)
    return lax.ppermute(block, axis, [(i, (i + distance) % size) for i in range(size)])


def column_cuts(channels):
    groups = channels // GSIZE
    half = (groups + 1) // 2 * GSIZE
    return [(0, half), (half, channels)]


def local(
    block_input, time_shift, out_grad, params, first_moment, second_moment, push_weight, step
):
    samples, positions, channels = block_input.shape
    shards = lax.axis_size("dp")
    me = lax.axis_index("dp").astype(jnp.int32).reshape(1)
    cuts = column_cuts(channels)
    group_of = jnp.arange(channels, dtype=jnp.int32) // GSIZE
    same_group = (group_of[:, None] == group_of[None, :]).astype(jnp.bfloat16)

    scaled_rows = (params[0] / push_weight[0]).astype(jnp.bfloat16)
    weights = []
    for start, stop in cuts:
        piece = scaled_rows[:, start:stop]
        weights.append([piece] + [moved_on(piece, "dp", -slot) for slot in range(1, shards)])

    level_count = lax.axis_size("replica").bit_length() - 1
    distance_bits = step[0] % level_count

    def from_behind(block):
        branches = [
            functools.partial(moved_on, axis="replica", distance=1 << power) for power in range(level_count)
        ]
        return lax.switch(distance_bits, branches, block)

    activation, mean_in, inverse_in = norm_in(block_input, same_group)
    activation_t = activation.T

    step_count = (step[0] + 1).astype(jnp.float32)
    first_scale = LEARN_RATE / (1.0 - jnp.power(BETA_ONE, step_count))
    second_scale = 1.0 / (1.0 - jnp.power(BETA_TWO, step_count))

    hidden_grads, full_weights, arrived = [], [], []
    for (start, stop), shard_list in zip(cuts, weights):
        grad_hidden, full_weight, own, *sends = mix(
            me,
            activation,
            activation_t,
            time_shift[:, start:stop],
            out_grad[:, :, start:stop],
            same_group,
            shard_list,
        )
        hidden_grads.append(grad_hidden)
        full_weights.append(full_weight)
        arrived.append(
            (own, [moved_on(send, "dp", slot) for slot, send in zip(range(1, shards), sends)])
        )
    grad_input = input_grad(block_input, mean_in, inverse_in, same_group, hidden_grads, full_weights)

    outs = []
    for (start, stop), (own, others) in zip(cuts, arrived):
        grad = (own + sum(other.astype(jnp.float32) for other in others)) / shards
        first_new = BETA_ONE * first_moment[0, :, start:stop] + (1.0 - BETA_ONE) * grad
        second_new = BETA_TWO * second_moment[0, :, start:stop] + (1.0 - BETA_TWO) * grad * grad
        update = (first_scale * first_new) / (jnp.sqrt(second_scale * second_new) + ADAM_EPS)
        moved = params[0, :, start:stop] - update
        neighbour = from_behind(moved.astype(jnp.bfloat16))
        outs.append((0.5 * (moved + neighbour.astype(jnp.float32)), first_new, second_new))
    averaged, first_new, second_new = (jnp.concatenate(pieces, axis=1) for pieces in zip(*outs))
    neighbour_weight = from_behind(push_weight.astype(jnp.bfloat16)).astype(jnp.float32)
    new_weight = 0.5 * (push_weight + neighbour_weight)
    return (grad_input, averaged[None], first_new[None], second_new[None], new_weight)


def solution(mesh):
    placed = (
        P(("replica", "dp"), None, None),
        P(("replica", "dp"), None),
        P(("replica", "dp"), None, None),
        P("replica", "dp", None),
        P("replica", "dp", None),
        P("replica", "dp", None),
        P("replica"),
        P(),
    )
    return jax.shard_map(
        local,
        mesh=mesh,
        in_specs=placed,
        out_specs=(
            P(("replica", "dp"), None, None),
            P("replica", "dp", None),
            P("replica", "dp", None),
            P("replica", "dp", None),
            P("replica"),
        ),
        check_vma=False,
    )
```

```python
import functools

import jax
import jax.numpy as jnp
from jax import lax
from jax.experimental import pallas as pl
from jax.experimental.pallas import tpu as pltpu
from jax.sharding import PartitionSpec as P

GSIZE = 40

NORM_EPS = 1e-05
BETA_ONE = 0.9
BETA_TWO = 0.999
LEARN_RATE = 0.002
ADAM_EPS = 1e-08

LANES = 128
TILE_ROWS = 16
VMEM_BYTES = 20 * 1024 * 1024


def padded(rows):
    return -(-rows // TILE_ROWS) * TILE_ROWS


class Packing:
    def __init__(self, rows, start, stop):
        self.rows, self.start, self.stop = rows, start, stop
        self.columns = stop - start
        self.deep = padded(rows)
        self.tiles, self.rest = divmod(self.columns, LANES)
        fold = LANES // self.rest if self.rest else 1
        self.fold_rows = padded(-(-self.deep // fold))
        self.folds = [
            (first, min(self.fold_rows, self.deep - first)) for first in range(0, self.deep, self.fold_rows)
        ]
        self.height = self.tiles * self.deep + (self.fold_rows if self.rest else 0)

    def write(self, ref, block):
        for tile in range(self.tiles):
            ref[tile * self.deep : (tile + 1) * self.deep, :] = block[
                :, tile * LANES : (tile + 1) * LANES
            ].astype(ref.dtype)
        if self.rest:
            left = block[:, self.tiles * LANES :]
            parts = []
            for first, count in self.folds:
                part = left[first : first + count]
                if count < self.fold_rows:
                    part = jnp.concatenate(
                        [part, jnp.zeros((self.fold_rows - count, self.rest), part.dtype)], axis=0
                    )
                parts.append(part)
            spare = LANES - self.rest * len(parts)
            if spare:
                parts.append(jnp.zeros((self.fold_rows, spare), left.dtype))
            ref[self.tiles * self.deep :, :] = jnp.concatenate(parts, axis=1).astype(ref.dtype)

    def read(self, ref):
        pieces = [
            ref[tile * self.deep : (tile + 1) * self.deep, :].astype(jnp.float32) for tile in range(self.tiles)
        ]
        if self.rest:
            left = ref[self.tiles * self.deep :, :].astype(jnp.float32)
            parts = [
                left[:count, i * self.rest : (i + 1) * self.rest] for i, (_, count) in enumerate(self.folds)
            ]
            pieces.append(jnp.concatenate(parts, axis=0) if len(parts) > 1 else parts[0])
        return jnp.concatenate(pieces, axis=1) if len(pieces) > 1 else pieces[0]

    def payload(self):
        return jax.ShapeDtypeStruct((self.height, LANES), jnp.bfloat16)

    def block(self):
        return jax.ShapeDtypeStruct((self.deep, self.columns), jnp.float32)


def group_sums(rows, same_group):
    high = rows.astype(jnp.bfloat16).astype(jnp.float32)
    rest = rows - high
    middle = rest.astype(jnp.bfloat16).astype(jnp.float32)
    count = rows.shape[0]
    stacked = jnp.concatenate([high, middle, rest - middle], axis=0).astype(jnp.bfloat16)
    sums = jnp.dot(stacked, same_group, preferred_element_type=jnp.float32)
    return sums[:count] + (sums[count : 2 * count] + sums[2 * count :])


def position_sums(parts):
    return jnp.concatenate([jnp.sum(part, axis=0, keepdims=True) for part in parts], axis=0)


def sigmoid(values):
    return 0.5 * jnp.tanh(0.5 * values) + 0.5


def silu_grad(values):
    gate = sigmoid(values)
    return gate * (1.0 + values * (1.0 - gate))


def cast_kernel(packs, push_ref, params_ref, *refs):
    out_refs, rows_ref = refs[:-1], refs[-1]
    rows = params_ref.shape[0]
    rows_ref[rows // 8 * 8 :, :] = jnp.zeros((rows_ref.shape[0] - rows // 8 * 8, rows_ref.shape[1]), jnp.float32)
    rows_ref[:rows, :] = params_ref[:, 0, :] / push_ref[0]
    for pack, out_ref in zip(packs, out_refs):
        pack.write(out_ref, rows_ref[:, pack.start : pack.stop])


def norm_in_kernel(shards, me_ref, x_ref, same_group_ref, act_ref, mean_ref, inverse_ref):
    samples, positions, channels = x_ref.shape
    rows = channels // shards
    deep = act_ref.shape[0] // shards
    entries = positions * GSIZE
    same_group = same_group_ref[...]
    parts = [x_ref[i].astype(jnp.float32) for i in range(samples)]
    mean = group_sums(position_sums(parts), same_group) / entries
    centered = [parts[i] - mean[i : i + 1] for i in range(samples)]
    variance = group_sums(position_sums([part * part for part in centered]), same_group) / entries
    inverse = lax.rsqrt(variance + NORM_EPS)
    mean_ref[...] = mean
    inverse_ref[...] = inverse
    normed = [centered[i] * inverse[i : i + 1] for i in range(samples)]
    act = jnp.concatenate([part * sigmoid(part) for part in normed], axis=0)
    turned = pltpu.roll(act.T, channels - me_ref[0] * rows, 0)
    act_ref[...] = jnp.zeros_like(act_ref)
    for slot in range(shards):
        act_ref[slot * deep : slot * deep + rows, :] = turned[slot * rows : (slot + 1) * rows].astype(jnp.bfloat16)


def mix_kernel(shards, pack, act_ref, shift_ref, out_grad_ref, same_group_ref, *refs):
    weight_refs, token_ref, refs = refs[:shards], refs[shards], refs[shards + 1 :]
    grad_hidden_ref, own_ref = refs[:2]
    send_refs, weight_ref = refs[2 : 1 + shards], refs[1 + shards]
    samples, positions, columns = out_grad_ref.shape
    entries = positions * GSIZE
    deep = pack.deep
    for slot, shard_ref in enumerate(weight_refs):
        weight_ref[slot * deep : (slot + 1) * deep, :] = pack.read(shard_ref).astype(jnp.bfloat16)
    same_group = same_group_ref[:columns, :columns]
    hidden = lax.dot_general(
        act_ref[...], weight_ref[...], (((0,), (0,)), ((), ())), preferred_element_type=jnp.float32
    )
    parts = [
        hidden[i * positions : (i + 1) * positions] + shift_ref[i : i + 1, :].astype(jnp.float32)
        for i in range(samples)
    ]
    mean = group_sums(position_sums(parts), same_group) / entries
    parts = [parts[i] - mean[i : i + 1] for i in range(samples)]
    variance = group_sums(position_sums([part * part for part in parts]), same_group) / entries
    inverse = lax.rsqrt(variance + NORM_EPS)
    normed = [parts[i] * inverse[i : i + 1] for i in range(samples)]
    grads = [out_grad_ref[i].astype(jnp.float32) * silu_grad(normed[i]) for i in range(samples)]
    means = group_sums(
        jnp.concatenate(
            [position_sums(grads), position_sums([g * n for g, n in zip(grads, normed)])], axis=0
        ),
        same_group,
    ) / entries
    for i in range(samples):
        first, second = means[i : i + 1], means[samples + i : samples + i + 1]
        grad_hidden_ref[i * positions : (i + 1) * positions, :] = (
            inverse[i : i + 1] * (grads[i] - first - normed[i] * second)
        ).astype(jnp.bfloat16)
    grad = jnp.dot(act_ref[...], grad_hidden_ref[...], preferred_element_type=jnp.float32)
    for slot, send_ref in enumerate(send_refs, 1):
        pack.write(send_ref, grad[slot * deep : (slot + 1) * deep])
    own_ref[...] = grad[:deep]


def input_grad_kernel(shards, packs, me_ref, x_ref, mean_ref, inverse_ref, same_group_ref, *refs):
    grad_refs, refs = refs[: len(packs)], refs[len(packs) :]
    weight_refs, out_ref, rows_ref = refs[:-2], refs[-2], refs[-1]
    samples, positions, channels = x_ref.shape
    entries = positions * GSIZE
    rows = channels // shards
    grad_act = 0.0
    for index, (pack, grad_ref) in enumerate(zip(packs, grad_refs)):
        for slot in range(shards):
            block = pack.read(weight_refs[index * shards + slot])
            rows_ref[slot * rows : (slot + 1) * rows, : pack.columns] = block[:rows]
        weight = pltpu.roll(rows_ref[:, : pack.columns], me_ref[0] * rows, 0).astype(jnp.bfloat16)
        grad_act += lax.dot_general(
            grad_ref[...], weight, (((1,), (1,)), ((), ())), preferred_element_type=jnp.float32
        )
    inverse = inverse_ref[...]
    normed = [
        (x_ref[i].astype(jnp.float32) - mean_ref[i : i + 1, :]) * inverse[i : i + 1] for i in range(samples)
    ]
    grads = [grad_act[i * positions : (i + 1) * positions] * silu_grad(normed[i]) for i in range(samples)]
    means = group_sums(
        jnp.concatenate(
            [position_sums(grads), position_sums([g * n for g, n in zip(grads, normed)])], axis=0
        ),
        same_group_ref[...],
    ) / entries
    for i in range(samples):
        first, second = means[i : i + 1], means[samples + i : samples + i + 1]
        out_ref[i] = (inverse[i : i + 1] * (grads[i] - first - normed[i] * second)).astype(jnp.bfloat16)


def adam_kernel(shards, pack, scales_ref, own_ref, *refs):
    other_refs, refs = refs[: shards - 1], refs[shards - 1 :]
    params_ref, first_ref, second_ref, token_ref, grad_ref, moved_ref, sent_ref = refs
    rows = pack.rows
    total = own_ref[...]
    for other_ref in other_refs:
        total = total + pack.read(other_ref)
    grad_ref[...] = total / shards
    grad = grad_ref[:rows, :]
    columns = slice(pack.start, pack.stop)
    first_new = BETA_ONE * first_ref[:, 0, columns] + (1.0 - BETA_ONE) * grad
    second_new = BETA_TWO * second_ref[:, 0, columns] + (1.0 - BETA_TWO) * grad * grad
    update = (scales_ref[0] * first_new) / (jnp.sqrt(second_new * scales_ref[1]) + ADAM_EPS)
    if rows < pack.deep:
        moved_ref[rows // 8 * 8 :, :] = jnp.zeros((pack.deep - rows // 8 * 8, pack.columns), jnp.float32)
    moved_ref[:rows, :] = params_ref[:, 0, columns] - update
    pack.write(sent_ref, moved_ref[...])


def moments_kernel(packs, first_ref, second_ref, *refs):
    grad_refs, (first_out, second_out) = refs[: len(packs)], refs[len(packs) :]
    rows = first_ref.shape[0]
    grad = jnp.concatenate([grad_ref[:rows, :] for grad_ref in grad_refs], axis=1)
    first_out[:, 0, :] = BETA_ONE * first_ref[:, 0, :] + (1.0 - BETA_ONE) * grad
    second_out[:, 0, :] = BETA_TWO * second_ref[:, 0, :] + (1.0 - BETA_TWO) * grad * grad


def average_kernel(packs, *refs):
    moved_refs, other_refs, out_ref = refs[: len(packs)], refs[len(packs) : -1], refs[-1]
    rows = out_ref.shape[0]
    pieces = [
        0.5 * (moved_ref[...] + pack.read(other_ref))
        for pack, moved_ref, other_ref in zip(packs, moved_refs, other_refs)
    ]
    out_ref[:, 0, :] = jnp.concatenate(pieces, axis=1)[:rows]


SCALARS = pl.BlockSpec(memory_space=pltpu.SMEM)
BLOCKS = pl.BlockSpec(memory_space=pltpu.VMEM)
TOKEN = pl.BlockSpec(memory_space=pl.ANY)


def call(kernel, name, outs, specs, operands, scratch=(), flops=0, elements=0):
    return pl.pallas_call(
        kernel,
        out_shape=outs,
        in_specs=specs,
        out_specs=jax.tree.map(lambda _: BLOCKS, outs),
        scratch_shapes=list(scratch),
        compiler_params=pltpu.CompilerParams(vmem_limit_bytes=VMEM_BYTES),
        cost_estimate=pl.CostEstimate(flops=flops, bytes_accessed=8 * elements, transcendentals=elements),
        name=name,
    )(*operands)


def moved_on(block, axis, distance):
    size = lax.axis_size(axis)
    return lax.ppermute(block, axis, [(i, (i + distance) % size) for i in range(size)])


def column_cuts(channels):
    half = (channels // GSIZE + 1) // 2 * GSIZE
    return [(0, half), (half, channels)]


def local(
    block_input, time_shift, out_grad, params, first_moment, second_moment, push_weight, step
):
    samples, positions, channels = block_input.shape
    tokens = samples * positions
    shards = lax.axis_size("dp")
    rows = params.shape[1]
    deep = padded(rows)
    me = lax.axis_index("dp").astype(jnp.int32).reshape(1)
    packs = [Packing(rows, start, stop) for start, stop in column_cuts(channels)]
    params, first_moment, second_moment = (
        jnp.transpose(array, (1, 0, 2)) for array in (params, first_moment, second_moment)
    )
    group_of = jnp.arange(channels, dtype=jnp.int32) // GSIZE
    same_group = (group_of[:, None] == group_of[None, :]).astype(jnp.bfloat16)

    shard_list = call(
        functools.partial(cast_kernel, packs),
        "cast",
        tuple(pack.payload() for pack in packs),
        [SCALARS, BLOCKS],
        (push_weight, params),
        scratch=[pltpu.VMEM((deep, channels), jnp.float32)],
        elements=rows * channels,
    )
    weights = [
        [piece] + [moved_on(piece, "dp", -slot) for slot in range(1, shards)] for piece in shard_list
    ]

    level_count = lax.axis_size("replica").bit_length() - 1
    distance_bits = step[0] % level_count
    step_count = (step[0] + 1).astype(jnp.float32)
    scales = jnp.stack(
        [LEARN_RATE / (1.0 - jnp.power(BETA_ONE, step_count)), 1.0 / (1.0 - jnp.power(BETA_TWO, step_count))]
    )

    activation, mean_in, inverse_in = call(
        functools.partial(norm_in_kernel, shards),
        "norm_in",
        (
            jax.ShapeDtypeStruct((shards * deep, tokens), jnp.bfloat16),
            jax.ShapeDtypeStruct((samples, channels), jnp.float32),
            jax.ShapeDtypeStruct((samples, channels), jnp.float32),
        ),
        [SCALARS, BLOCKS, BLOCKS],
        (me, block_input, same_group),
        elements=tokens * channels,
    )

    hidden_grads, owns, arrived = [], [], []
    token = mean_in
    for pack, pieces in zip(packs, weights):
        columns = slice(pack.start, pack.stop)
        grad_hidden, own, *sends = call(
            functools.partial(mix_kernel, shards, pack),
            "mix",
            (jax.ShapeDtypeStruct((tokens, pack.columns), jnp.bfloat16), pack.block())
            + (pack.payload(),) * (shards - 1),
            [BLOCKS] * (4 + shards) + [TOKEN],
            (activation, time_shift[:, columns], out_grad[:, :, columns], same_group, *pieces, token),
            scratch=[pltpu.VMEM((shards * deep, pack.columns), jnp.bfloat16)],
            flops=4 * tokens * channels * pack.columns,
            elements=tokens * pack.columns,
        )
        token = own
        hidden_grads.append(grad_hidden)
        owns.append(own)
        arrived.append([moved_on(send, "dp", slot) for slot, send in enumerate(sends, 1)])

    grad_input = call(
        functools.partial(input_grad_kernel, shards, packs),
        "input_grad",
        jax.ShapeDtypeStruct(block_input.shape, jnp.bfloat16),
        [SCALARS] + [BLOCKS] * (4 + len(packs) * (1 + shards)),
        (me, block_input, mean_in, inverse_in, same_group, *hidden_grads, *weights[0], *weights[1]),
        scratch=[pltpu.VMEM((channels, max(pack.columns for pack in packs)), jnp.float32)],
        flops=2 * tokens * channels * channels,
        elements=tokens * channels,
    )

    def adam(pack, own, others, token):
        return call(
            functools.partial(adam_kernel, shards, pack),
            "adam",
            (pack.block(), pack.block(), pack.payload()),
            [SCALARS] + [BLOCKS] * (3 + shards) + [TOKEN],
            (scales, own, *others, params, first_moment, second_moment, token),
            elements=rows * pack.columns,
        )

    def moments(*grads):
        return call(
            functools.partial(moments_kernel, packs),
            "moments",
            (jax.ShapeDtypeStruct(params.shape, jnp.float32),) * 2,
            [BLOCKS] * (2 + len(packs)),
            (first_moment, second_moment, *grads),
            elements=rows * channels,
        )

    def from_behind(finish, *operands):
        def branch(distance):
            return lambda *values: finish(lambda block: moved_on(block, "replica", distance), *values)

        return lax.switch(distance_bits, [branch(1 << power) for power in range(level_count)], *operands)

    grad_a, moved_a, sent_a = adam(packs[0], owns[0], arrived[0], token)
    other_a, other_weight = from_behind(
        lambda move, sent, weight: (move(sent), move(weight)), sent_a, push_weight.astype(jnp.bfloat16)
    )
    grad_b, moved_b, sent_b = adam(packs[1], owns[1], arrived[1], other_a)
    other_b, first_new, second_new = from_behind(
        lambda move, sent, *grads: (move(sent), *moments(*grads)), sent_b, grad_a, grad_b
    )
    averaged = call(
        functools.partial(average_kernel, packs),
        "average",
        jax.ShapeDtypeStruct(params.shape, jnp.float32),
        [BLOCKS] * (2 * len(packs)),
        (moved_a, moved_b, other_a, other_b),
        elements=rows * channels,
    )
    new_weight = 0.5 * (push_weight + other_weight.astype(jnp.float32))
    return (
        grad_input,
        *(jnp.transpose(array, (1, 0, 2)) for array in (averaged, first_new, second_new)),
        new_weight,
    )


def solution(mesh):
    placed = (
        P(("replica", "dp"), None, None),
        P(("replica", "dp"), None),
        P(("replica", "dp"), None, None),
        P("replica", "dp", None),
        P("replica", "dp", None),
        P("replica", "dp", None),
        P("replica"),
        P(),
    )
    return jax.shard_map(
        local,
        mesh=mesh,
        in_specs=placed,
        out_specs=(
            P(("replica", "dp"), None, None),
            P("replica", "dp", None),
            P("replica", "dp", None),
            P("replica", "dp", None),
            P("replica"),
        ),
        check_vma=False,
    )
```

```python
import functools

import jax
import jax.numpy as jnp
from jax import lax
from jax.experimental import pallas as pl
from jax.experimental.pallas import tpu as pltpu
from jax.sharding import PartitionSpec as P

GSIZE = 40

NORM_EPS = 1e-05
BETA_ONE = 0.9
BETA_TWO = 0.999
LEARN_RATE = 0.002
ADAM_EPS = 1e-08

LANES = 128
TILE_ROWS = 16
VMEM_BYTES = 16 * 1024 * 1024


def padded(rows):
    return -(-rows // TILE_ROWS) * TILE_ROWS


class Packing:
    def __init__(self, rows, start, stop):
        self.rows, self.start, self.stop = rows, start, stop
        self.columns = stop - start
        self.deep = padded(rows)
        self.tiles, self.rest = divmod(self.columns, LANES)
        fold = LANES // self.rest if self.rest else 1
        self.fold_rows = padded(-(-self.deep // fold))
        self.folds = [
            (first, min(self.fold_rows, self.deep - first)) for first in range(0, self.deep, self.fold_rows)
        ]
        self.height = self.tiles * self.deep + (self.fold_rows if self.rest else 0)

    def write(self, ref, block):
        for tile in range(self.tiles):
            ref[tile * self.deep : (tile + 1) * self.deep, :] = block[
                :, tile * LANES : (tile + 1) * LANES
            ].astype(ref.dtype)
        if self.rest:
            left = block[:, self.tiles * LANES :]
            parts = []
            for first, count in self.folds:
                part = left[first : first + count]
                if count < self.fold_rows:
                    part = jnp.concatenate(
                        [part, jnp.zeros((self.fold_rows - count, self.rest), part.dtype)], axis=0
                    )
                parts.append(part)
            spare = LANES - self.rest * len(parts)
            if spare:
                parts.append(jnp.zeros((self.fold_rows, spare), left.dtype))
            ref[self.tiles * self.deep :, :] = jnp.concatenate(parts, axis=1).astype(ref.dtype)

    def read(self, ref):
        pieces = [
            ref[tile * self.deep : (tile + 1) * self.deep, :].astype(jnp.float32) for tile in range(self.tiles)
        ]
        if self.rest:
            left = ref[self.tiles * self.deep :, :].astype(jnp.float32)
            parts = [
                left[:count, i * self.rest : (i + 1) * self.rest] for i, (_, count) in enumerate(self.folds)
            ]
            pieces.append(jnp.concatenate(parts, axis=0) if len(parts) > 1 else parts[0])
        return jnp.concatenate(pieces, axis=1) if len(pieces) > 1 else pieces[0]

    def unpack(self, ref, out_ref, first_row):
        for tile in range(self.tiles):
            out_ref[first_row : first_row + self.deep, tile * LANES : (tile + 1) * LANES] = ref[
                tile * self.deep : (tile + 1) * self.deep, :
            ]
        if self.rest:
            left = ref[self.tiles * self.deep :, :]
            for i, (first, count) in enumerate(self.folds):
                out_ref[first_row + first : first_row + first + count, self.tiles * LANES :] = left[
                    :count, i * self.rest : (i + 1) * self.rest
                ]

    def payload(self):
        return jax.ShapeDtypeStruct((self.height, LANES), jnp.bfloat16)

    def block(self):
        return jax.ShapeDtypeStruct((self.deep, self.columns), jnp.float32)


def group_sums(rows, same_group):
    high = rows.astype(jnp.bfloat16).astype(jnp.float32)
    rest = rows - high
    middle = rest.astype(jnp.bfloat16).astype(jnp.float32)
    count = rows.shape[0]
    stacked = jnp.concatenate([high, middle, rest - middle], axis=0).astype(jnp.bfloat16)
    sums = jnp.dot(stacked, same_group, preferred_element_type=jnp.float32)
    return sums[:count] + (sums[count : 2 * count] + sums[2 * count :])


def table_sums(packs, rows, same_group):
    return jnp.concatenate(
        [
            group_sums(rows[:, pack.start : pack.stop], same_group[: pack.columns, : pack.columns])
            for pack in packs
        ],
        axis=1,
    )


def position_sums(parts):
    return jnp.concatenate([jnp.sum(part, axis=0, keepdims=True) for part in parts], axis=0)


def sigmoid(values):
    return 0.5 * jnp.tanh(0.5 * values) + 0.5


def silu_grad(values):
    gate = sigmoid(values)
    return gate * (1.0 + values * (1.0 - gate))


def cast_kernel(packs, push_ref, params_ref, *refs):
    out_refs, rows_ref = refs[:-1], refs[-1]
    rows = params_ref.shape[0]
    rows_ref[rows // 8 * 8 :, :] = jnp.zeros((rows_ref.shape[0] - rows // 8 * 8, rows_ref.shape[1]), jnp.float32)
    rows_ref[:rows, :] = params_ref[:, 0, :] / push_ref[0]
    for pack, out_ref in zip(packs, out_refs):
        pack.write(out_ref, rows_ref[:, pack.start : pack.stop])


def norm_in_kernel(shards, packs, me_ref, scales_ref, x_ref, shift_ref, out_grad_ref, *refs):
    act_ref, mean_ref, inverse_ref, same_group_ref = refs[:4]
    shift_refs, out_grad_refs = refs[4 : 4 + len(packs)], refs[4 + len(packs) :]
    samples, positions, channels = x_ref.shape
    for pack, shift_out, out_grad_out in zip(packs, shift_refs, out_grad_refs):
        shift_out[...] = shift_ref[...].astype(jnp.float32)[:, pack.start : pack.stop]
        for i in range(samples):
            out_grad_out[i] = out_grad_ref[i][:, pack.start : pack.stop]
    group_of_row = lax.broadcasted_iota(jnp.int32, same_group_ref.shape, 0) // GSIZE
    group_of_column = lax.broadcasted_iota(jnp.int32, same_group_ref.shape, 1) // GSIZE
    same_group_ref[...] = (group_of_row == group_of_column).astype(jnp.float32).astype(jnp.bfloat16)
    rows = channels // shards
    deep = act_ref.shape[0] // shards
    entries = positions * GSIZE
    same_group = same_group_ref[...]
    parts = [x_ref[i].astype(jnp.float32) for i in range(samples)]
    mean = table_sums(packs, position_sums(parts), same_group) / entries
    centered = [parts[i] - mean[i : i + 1] for i in range(samples)]
    variance = table_sums(packs, position_sums([part * part for part in centered]), same_group) / entries
    inverse = lax.rsqrt(variance + NORM_EPS)
    mean_ref[...] = mean
    inverse_ref[...] = inverse
    normed = [centered[i] * inverse[i : i + 1] for i in range(samples)]
    act = jnp.concatenate([part * sigmoid(part) for part in normed], axis=0)
    turned = pltpu.roll(act.T, channels - me_ref[0] * rows, 0)
    act_ref[...] = jnp.zeros_like(act_ref)
    for slot in range(shards):
        act_ref[slot * deep : slot * deep + rows, :] = turned[slot * rows : (slot + 1) * rows].astype(jnp.bfloat16)


def mix_kernel(shards, pack, act_ref, shift_ref, out_grad_ref, same_group_ref, *refs):
    weight_refs, token_ref, refs = refs[:shards], refs[shards], refs[shards + 1 :]
    grad_hidden_ref, own_ref = refs[:2]
    send_refs, (weight_ref, kept_ref, sem) = refs[2 : 1 + shards], refs[1 + shards :]
    samples, positions, columns = out_grad_ref.shape
    entries = positions * GSIZE
    deep = pack.deep
    for slot, shard_ref in enumerate(weight_refs):
        pack.unpack(shard_ref, weight_ref, slot * deep)
    same_group = same_group_ref[:columns, :columns]
    hidden = lax.dot_general(
        act_ref[...], weight_ref[...], (((0,), (0,)), ((), ())), preferred_element_type=jnp.float32
    )
    parts = [
        hidden[i * positions : (i + 1) * positions] + shift_ref[i : i + 1, :]
        for i in range(samples)
    ]
    mean = group_sums(position_sums(parts), same_group) / entries
    parts = [parts[i] - mean[i : i + 1] for i in range(samples)]
    variance = group_sums(position_sums([part * part for part in parts]), same_group) / entries
    inverse = lax.rsqrt(variance + NORM_EPS)
    normed = [parts[i] * inverse[i : i + 1] for i in range(samples)]
    grads = [out_grad_ref[i].astype(jnp.float32) * silu_grad(normed[i]) for i in range(samples)]
    means = group_sums(
        jnp.concatenate(
            [position_sums(grads), position_sums([g * n for g, n in zip(grads, normed)])], axis=0
        ),
        same_group,
    ) / entries
    for i in range(samples):
        first, second = means[i : i + 1], means[samples + i : samples + i + 1]
        kept_ref[i * positions : (i + 1) * positions, :] = (
            inverse[i : i + 1] * (grads[i] - first - normed[i] * second)
        ).astype(jnp.bfloat16)
    copy = pltpu.make_async_copy(kept_ref, grad_hidden_ref, sem)
    copy.start()
    grad = jnp.dot(act_ref[...], kept_ref[...], preferred_element_type=jnp.float32)
    for slot, send_ref in enumerate(send_refs, 1):
        pack.write(send_ref, grad[slot * deep : (slot + 1) * deep])
    own_ref[...] = grad[:deep]
    copy.wait()


def input_grad_kernel(shards, packs, me_ref, x_ref, mean_ref, inverse_ref, same_group_ref, *refs):
    grad_refs, refs = refs[: len(packs)], refs[len(packs) :]
    weight_refs, out_ref, rows_ref = refs[:-2], refs[-2], refs[-1]
    samples, positions, channels = x_ref.shape
    entries = positions * GSIZE
    rows = channels // shards
    grad_act = 0.0
    for index, (pack, grad_ref) in enumerate(zip(packs, grad_refs)):
        for slot in range(shards):
            block = pack.read(weight_refs[index * shards + slot])
            rows_ref[slot * rows : (slot + 1) * rows, : pack.columns] = block[:rows]
        weight = pltpu.roll(rows_ref[:, : pack.columns], me_ref[0] * rows, 0).astype(jnp.bfloat16)
        grad_act += lax.dot_general(
            grad_ref[...], weight, (((1,), (1,)), ((), ())), preferred_element_type=jnp.float32
        )
    inverse = inverse_ref[...]
    normed = [
        (x_ref[i].astype(jnp.float32) - mean_ref[i : i + 1, :]) * inverse[i : i + 1] for i in range(samples)
    ]
    grads = [grad_act[i * positions : (i + 1) * positions] * silu_grad(normed[i]) for i in range(samples)]
    means = table_sums(
        packs,
        jnp.concatenate(
            [position_sums(grads), position_sums([g * n for g, n in zip(grads, normed)])], axis=0
        ),
        same_group_ref[...],
    ) / entries
    for i in range(samples):
        first, second = means[i : i + 1], means[samples + i : samples + i + 1]
        out_ref[i] = (inverse[i : i + 1] * (grads[i] - first - normed[i] * second)).astype(jnp.bfloat16)


def adam_kernel(shards, pack, scales_ref, own_ref, *refs):
    other_refs, refs = refs[: shards - 1], refs[shards - 1 :]
    params_ref, first_ref, second_ref, token_ref, grad_ref, moved_ref, sent_ref = refs
    rows = pack.rows
    total = own_ref[...]
    for other_ref in other_refs:
        total = total + pack.read(other_ref)
    grad_ref[...] = total / shards
    grad = grad_ref[:rows, :]
    columns = slice(pack.start, pack.stop)
    first_new = BETA_ONE * first_ref[:, 0, columns] + (1.0 - BETA_ONE) * grad
    second_new = BETA_TWO * second_ref[:, 0, columns] + (1.0 - BETA_TWO) * grad * grad
    update = (scales_ref[0] * first_new) / (jnp.sqrt(second_new * scales_ref[1]) + ADAM_EPS)
    if rows < pack.deep:
        moved_ref[rows // 8 * 8 :, :] = jnp.zeros((pack.deep - rows // 8 * 8, pack.columns), jnp.float32)
    moved_ref[:rows, :] = params_ref[:, 0, columns] - update
    pack.write(sent_ref, moved_ref[...])


def moments_kernel(packs, first_ref, second_ref, *refs):
    grad_refs, (first_out, second_out) = refs[: len(packs)], refs[len(packs) :]
    rows = first_ref.shape[0]
    grad = jnp.concatenate([grad_ref[:rows, :] for grad_ref in grad_refs], axis=1)
    first_out[:, 0, :] = BETA_ONE * first_ref[:, 0, :] + (1.0 - BETA_ONE) * grad
    second_out[:, 0, :] = BETA_TWO * second_ref[:, 0, :] + (1.0 - BETA_TWO) * grad * grad


def average_kernel(packs, *refs):
    moved_refs, other_refs = refs[: len(packs)], refs[len(packs) : -3]
    out_ref, rows_ref, sem = refs[-3:]
    rows = out_ref.shape[0]
    pieces = [
        0.5 * (moved_ref[...] + pack.read(other_ref))
        for pack, moved_ref, other_ref in zip(packs, moved_refs, other_refs)
    ]
    rows_ref[:, 0, :] = jnp.concatenate(pieces, axis=1)[:rows]
    copy = pltpu.make_async_copy(rows_ref, out_ref, sem)
    copy.start()
    copy.wait()


SCALARS = pl.BlockSpec(memory_space=pltpu.SMEM)
BLOCKS = pl.BlockSpec(memory_space=pltpu.VMEM)
TOKEN = pl.BlockSpec(memory_space=pl.ANY)
IN_HBM = pl.BlockSpec(memory_space=pltpu.HBM)


def call(kernel, name, outs, specs, operands, scratch=(), out_specs=None, flops=0, elements=0):
    return pl.pallas_call(
        kernel,
        out_shape=outs,
        in_specs=specs,
        out_specs=out_specs or jax.tree.map(lambda _: BLOCKS, outs),
        scratch_shapes=list(scratch),
        compiler_params=pltpu.CompilerParams(vmem_limit_bytes=VMEM_BYTES),
        cost_estimate=pl.CostEstimate(flops=flops, bytes_accessed=8 * elements, transcendentals=elements),
        name=name,
    )(*operands)


def moved_on(block, axis, distance):
    size = lax.axis_size(axis)
    return lax.ppermute(block, axis, [(i, (i + distance) % size) for i in range(size)])


def column_cuts(channels):
    half = (channels // GSIZE + 1) // 2 * GSIZE
    return [(0, half), (half, channels)]


def local(
    block_input, time_shift, out_grad, params, first_moment, second_moment, push_weight, step
):
    samples, positions, channels = block_input.shape
    tokens = samples * positions
    shards = lax.axis_size("dp")
    rows = params.shape[1]
    deep = padded(rows)
    me = lax.axis_index("dp").astype(jnp.int32).reshape(1)
    packs = [Packing(rows, start, stop) for start, stop in column_cuts(channels)]
    params, first_moment, second_moment = (
        jnp.transpose(array, (1, 0, 2)) for array in (params, first_moment, second_moment)
    )
    shard_list = call(
        functools.partial(cast_kernel, packs),
        "cast",
        tuple(pack.payload() for pack in packs),
        [SCALARS, BLOCKS],
        (push_weight, params),
        scratch=[pltpu.VMEM((deep, channels), jnp.float32)],
        elements=rows * channels,
    )
    weights = [
        [piece] + [moved_on(piece, "dp", -slot) for slot in range(1, shards)] for piece in shard_list
    ]

    level_count = lax.axis_size("replica").bit_length() - 1
    distance_bits = step[0] % level_count
    step_count = (step[0] + 1).astype(jnp.float32)
    scales = jnp.stack(
        [LEARN_RATE / (1.0 - jnp.power(BETA_ONE, step_count)), 1.0 / (1.0 - jnp.power(BETA_TWO, step_count))]
    )

    activation, mean_in, inverse_in, same_group, *pieces = call(
        functools.partial(norm_in_kernel, shards, packs),
        "norm_in",
        (
            jax.ShapeDtypeStruct((shards * deep, tokens), jnp.bfloat16),
            jax.ShapeDtypeStruct((samples, channels), jnp.float32),
            jax.ShapeDtypeStruct((samples, channels), jnp.float32),
            jax.ShapeDtypeStruct((max(pack.columns for pack in packs),) * 2, jnp.bfloat16),
            *(jax.ShapeDtypeStruct((samples, pack.columns), jnp.float32) for pack in packs),
            *(jax.ShapeDtypeStruct((samples, positions, pack.columns), jnp.bfloat16) for pack in packs),
        ),
        [SCALARS, SCALARS, BLOCKS, BLOCKS, BLOCKS],
        (me, scales, block_input, time_shift, out_grad),
        elements=tokens * channels,
    )

    hidden_grads, owns, arrived = [], [], []
    token = mean_in
    shifts, out_grads = pieces[: len(packs)], pieces[len(packs) :]
    for pack, shard_list, shift, out_grad_piece in zip(packs, weights, shifts, out_grads):
        grad_hidden, own, *sends = call(
            functools.partial(mix_kernel, shards, pack),
            "mix",
            (pltpu.HBM((tokens, pack.columns), jnp.bfloat16), pack.block())
            + (pack.payload(),) * (shards - 1),
            [BLOCKS] * (4 + shards) + [TOKEN],
            (activation, shift, out_grad_piece, same_group, *shard_list, token),
            scratch=[
                pltpu.VMEM((shards * deep, pack.columns), jnp.bfloat16),
                pltpu.VMEM((tokens, pack.columns), jnp.bfloat16),
                pltpu.SemaphoreType.DMA,
            ],
            out_specs=(IN_HBM,) + (BLOCKS,) * shards,
            flops=4 * tokens * channels * pack.columns,
            elements=tokens * pack.columns,
        )
        token = own
        hidden_grads.append(grad_hidden)
        owns.append(own)
        arrived.append([moved_on(send, "dp", slot) for slot, send in enumerate(sends, 1)])

    grad_input = call(
        functools.partial(input_grad_kernel, shards, packs),
        "input_grad",
        jax.ShapeDtypeStruct(block_input.shape, jnp.bfloat16),
        [SCALARS] + [BLOCKS] * (4 + len(packs) * (1 + shards)),
        (me, block_input, mean_in, inverse_in, same_group, *hidden_grads, *weights[0], *weights[1]),
        scratch=[pltpu.VMEM((channels, max(pack.columns for pack in packs)), jnp.float32)],
        flops=2 * tokens * channels * channels,
        elements=tokens * channels,
    )

    def adam(pack, own, others, token):
        return call(
            functools.partial(adam_kernel, shards, pack),
            "adam",
            (pack.block(), pack.block(), pack.payload()),
            [SCALARS] + [BLOCKS] * (3 + shards) + [TOKEN],
            (scales, own, *others, params, first_moment, second_moment, token),
            elements=rows * pack.columns,
        )

    def moments(*grads):
        return call(
            functools.partial(moments_kernel, packs),
            "moments",
            (jax.ShapeDtypeStruct(params.shape, jnp.float32),) * 2,
            [BLOCKS] * (2 + len(packs)),
            (first_moment, second_moment, *grads),
            elements=rows * channels,
        )

    def average(*blocks):
        return call(
            functools.partial(average_kernel, packs),
            "average",
            pltpu.HBM(params.shape, jnp.float32),
            [BLOCKS] * (2 * len(packs)),
            blocks,
            scratch=[pltpu.VMEM(params.shape, jnp.float32), pltpu.SemaphoreType.DMA],
            out_specs=IN_HBM,
            elements=rows * channels,
        )

    def from_behind(finish, *operands):
        def branch(distance):
            return lambda *values: finish(lambda block: moved_on(block, "replica", distance), *values)

        return lax.switch(distance_bits, [branch(1 << power) for power in range(level_count)], *operands)

    grad_a, moved_a, sent_a = adam(packs[0], owns[0], arrived[0], token)
    other_a, other_weight = from_behind(
        lambda move, sent, weight: (move(sent), move(weight)), sent_a, push_weight.astype(jnp.bfloat16)
    )
    grad_b, moved_b, sent_b = adam(packs[1], owns[1], arrived[1], other_a)

    def finish(move, sent, *values):
        grads, moved, other_first = values[:2], values[2:4], values[4]
        other = move(sent)
        return (*moments(*grads), average(*moved, other_first, other))

    first_new, second_new, averaged = from_behind(finish, sent_b, grad_a, grad_b, moved_a, moved_b, other_a)
    new_weight = 0.5 * (push_weight + other_weight.astype(jnp.float32))
    return (
        grad_input,
        *(jnp.transpose(array, (1, 0, 2)) for array in (averaged, first_new, second_new)),
        new_weight,
    )


def solution(mesh):
    placed = (
        P(("replica", "dp"), None, None),
        P(("replica", "dp"), None),
        P(("replica", "dp"), None, None),
        P("replica", "dp", None),
        P("replica", "dp", None),
        P("replica", "dp", None),
        P("replica"),
        P(),
    )
    return jax.shard_map(
        local,
        mesh=mesh,
        in_specs=placed,
        out_specs=(
            P(("replica", "dp"), None, None),
            P("replica", "dp", None),
            P("replica", "dp", None),
            P("replica", "dp", None),
            P("replica"),
        ),
        check_vma=False,
    )
```

```python
import functools

import jax
import jax.numpy as jnp
from jax import lax
from jax.experimental import pallas as pl
from jax.experimental.pallas import tpu as pltpu
from jax.sharding import PartitionSpec as P

GSIZE = 40

NORM_EPS = 1e-05
BETA_ONE = 0.9
BETA_TWO = 0.999
LEARN_RATE = 0.002
ADAM_EPS = 1e-08

LANES = 128
TILE_ROWS = 16
VMEM_BYTES = 16 * 1024 * 1024


def padded(rows):
    return -(-rows // TILE_ROWS) * TILE_ROWS


class Packing:
    def __init__(self, rows, start, stop):
        self.rows, self.start, self.stop = rows, start, stop
        self.columns = stop - start
        self.deep = padded(rows)
        self.tiles, self.rest = divmod(self.columns, LANES)
        fold = LANES // self.rest if self.rest else 1
        self.fold_rows = padded(-(-self.deep // fold))
        self.folds = [
            (first, min(self.fold_rows, self.deep - first)) for first in range(0, self.deep, self.fold_rows)
        ]
        self.height = self.tiles * self.deep + (self.fold_rows if self.rest else 0)

    def write(self, ref, block):
        for tile in range(self.tiles):
            ref[tile * self.deep : (tile + 1) * self.deep, :] = block[
                :, tile * LANES : (tile + 1) * LANES
            ].astype(ref.dtype)
        if self.rest:
            left = block[:, self.tiles * LANES :]
            parts = []
            for first, count in self.folds:
                part = left[first : first + count]
                if count < self.fold_rows:
                    part = jnp.concatenate(
                        [part, jnp.zeros((self.fold_rows - count, self.rest), part.dtype)], axis=0
                    )
                parts.append(part)
            spare = LANES - self.rest * len(parts)
            if spare:
                parts.append(jnp.zeros((self.fold_rows, spare), left.dtype))
            ref[self.tiles * self.deep :, :] = jnp.concatenate(parts, axis=1).astype(ref.dtype)

    def read(self, ref):
        pieces = [
            ref[tile * self.deep : (tile + 1) * self.deep, :].astype(jnp.float32) for tile in range(self.tiles)
        ]
        if self.rest:
            left = ref[self.tiles * self.deep :, :].astype(jnp.float32)
            parts = [
                left[:count, i * self.rest : (i + 1) * self.rest] for i, (_, count) in enumerate(self.folds)
            ]
            pieces.append(jnp.concatenate(parts, axis=0) if len(parts) > 1 else parts[0])
        return jnp.concatenate(pieces, axis=1) if len(pieces) > 1 else pieces[0]

    def unpack(self, ref, out_ref, first_row):
        for tile in range(self.tiles):
            out_ref[first_row : first_row + self.deep, tile * LANES : (tile + 1) * LANES] = ref[
                tile * self.deep : (tile + 1) * self.deep, :
            ]
        if self.rest:
            left = ref[self.tiles * self.deep :, :]
            for i, (first, count) in enumerate(self.folds):
                out_ref[first_row + first : first_row + first + count, self.tiles * LANES :] = left[
                    :count, i * self.rest : (i + 1) * self.rest
                ]

    def payload(self):
        return jax.ShapeDtypeStruct((self.height, LANES), jnp.bfloat16)

    def block(self):
        return jax.ShapeDtypeStruct((self.deep, self.columns), jnp.float32)


def group_sums(rows, same_group):
    high = rows.astype(jnp.bfloat16).astype(jnp.float32)
    rest = rows - high
    middle = rest.astype(jnp.bfloat16).astype(jnp.float32)
    count = rows.shape[0]
    stacked = jnp.concatenate([high, middle, rest - middle], axis=0).astype(jnp.bfloat16)
    sums = jnp.dot(stacked, same_group, preferred_element_type=jnp.float32)
    return sums[:count] + (sums[count : 2 * count] + sums[2 * count :])


def table_sums(packs, rows, same_group):
    return jnp.concatenate(
        [
            group_sums(rows[:, pack.start : pack.stop], same_group[: pack.columns, : pack.columns])
            for pack in packs
        ],
        axis=1,
    )


def position_sums(parts):
    return jnp.concatenate([jnp.sum(part, axis=0, keepdims=True) for part in parts], axis=0)


def sigmoid(values):
    return 0.5 * jnp.tanh(0.5 * values) + 0.5


def silu_grad(values):
    gate = sigmoid(values)
    return gate * (1.0 + values * (1.0 - gate))


def cast_kernel(packs, push_ref, params_ref, *refs):
    out_refs, rows_ref = refs[:-1], refs[-1]
    rows = params_ref.shape[0]
    rows_ref[rows // 8 * 8 :, :] = jnp.zeros((rows_ref.shape[0] - rows // 8 * 8, rows_ref.shape[1]), jnp.float32)
    rows_ref[:rows, :] = params_ref[:, 0, :] / push_ref[0]
    for pack, out_ref in zip(packs, out_refs):
        pack.write(out_ref, rows_ref[:, pack.start : pack.stop])


def norm_in_kernel(shards, packs, me_ref, scales_ref, x_ref, shift_ref, out_grad_ref, *refs):
    act_ref, mean_ref, inverse_ref, same_group_ref = refs[:4]
    shift_refs, out_grad_refs = refs[4 : 4 + len(packs)], refs[4 + len(packs) :]
    samples, positions, channels = x_ref.shape
    for pack, shift_out, out_grad_out in zip(packs, shift_refs, out_grad_refs):
        shift_out[...] = shift_ref[...].astype(jnp.float32)[:, pack.start : pack.stop]
        for i in range(samples):
            out_grad_out[i] = out_grad_ref[i][:, pack.start : pack.stop]
    group_of_row = lax.broadcasted_iota(jnp.int32, same_group_ref.shape, 0) // GSIZE
    group_of_column = lax.broadcasted_iota(jnp.int32, same_group_ref.shape, 1) // GSIZE
    same_group_ref[...] = (group_of_row == group_of_column).astype(jnp.float32).astype(jnp.bfloat16)
    rows = channels // shards
    deep = act_ref.shape[0] // shards
    entries = positions * GSIZE
    same_group = same_group_ref[...]
    parts = [x_ref[i].astype(jnp.float32) for i in range(samples)]
    mean = table_sums(packs, position_sums(parts), same_group) / entries
    centered = [parts[i] - mean[i : i + 1] for i in range(samples)]
    variance = table_sums(packs, position_sums([part * part for part in centered]), same_group) / entries
    inverse = lax.rsqrt(variance + NORM_EPS)
    mean_ref[...] = mean
    inverse_ref[...] = inverse
    normed = [centered[i] * inverse[i : i + 1] for i in range(samples)]
    act = jnp.concatenate([part * sigmoid(part) for part in normed], axis=0)
    turned = pltpu.roll(act.T, channels - me_ref[0] * rows, 0)
    act_ref[...] = jnp.zeros_like(act_ref)
    for slot in range(shards):
        act_ref[slot * deep : slot * deep + rows, :] = turned[slot * rows : (slot + 1) * rows].astype(jnp.bfloat16)


def for_each_slot(shards, me, refs, use):
    for slot in range(shards):
        if len(refs) == shards or slot not in (1, shards - 1):
            use(slot, refs[slot])
            continue
        edge = shards - 1 if slot == 1 else 0
        pl.when(me == edge)(functools.partial(use, slot, refs[shards]))
        pl.when(me != edge)(functools.partial(use, slot, refs[slot]))


def mix_kernel(shards, held, pack, me_ref, act_ref, shift_ref, out_grad_ref, same_group_ref, *refs):
    weight_refs, token_ref, refs = refs[:held], refs[held], refs[held + 1 :]
    grad_hidden_ref, own_ref = refs[:2]
    send_refs, (weight_ref, kept_ref, sem) = refs[2 : 1 + shards], refs[1 + shards :]
    samples, positions, columns = out_grad_ref.shape
    entries = positions * GSIZE
    deep = pack.deep
    for_each_slot(
        shards, me_ref[0], weight_refs, lambda slot, ref: pack.unpack(ref, weight_ref, slot * deep)
    )
    same_group = same_group_ref[:columns, :columns]
    hidden = lax.dot_general(
        act_ref[...], weight_ref[...], (((0,), (0,)), ((), ())), preferred_element_type=jnp.float32
    )
    parts = [
        hidden[i * positions : (i + 1) * positions] + shift_ref[i : i + 1, :]
        for i in range(samples)
    ]
    mean = group_sums(position_sums(parts), same_group) / entries
    parts = [parts[i] - mean[i : i + 1] for i in range(samples)]
    variance = group_sums(position_sums([part * part for part in parts]), same_group) / entries
    inverse = lax.rsqrt(variance + NORM_EPS)
    normed = [parts[i] * inverse[i : i + 1] for i in range(samples)]
    grads = [out_grad_ref[i].astype(jnp.float32) * silu_grad(normed[i]) for i in range(samples)]
    means = group_sums(
        jnp.concatenate(
            [position_sums(grads), position_sums([g * n for g, n in zip(grads, normed)])], axis=0
        ),
        same_group,
    ) / entries
    for i in range(samples):
        first, second = means[i : i + 1], means[samples + i : samples + i + 1]
        kept_ref[i * positions : (i + 1) * positions, :] = (
            inverse[i : i + 1] * (grads[i] - first - normed[i] * second)
        ).astype(jnp.bfloat16)
    copy = pltpu.make_async_copy(kept_ref, grad_hidden_ref, sem)
    copy.start()
    grad = jnp.dot(act_ref[...], kept_ref[...], preferred_element_type=jnp.float32)
    for slot, send_ref in enumerate(send_refs, 1):
        pack.write(send_ref, grad[slot * deep : (slot + 1) * deep])
    own_ref[...] = grad[:deep]
    copy.wait()


def input_grad_kernel(shards, held, packs, me_ref, x_ref, mean_ref, inverse_ref, same_group_ref, *refs):
    grad_refs, refs = refs[: len(packs)], refs[len(packs) :]
    weight_refs, out_ref, rows_ref = refs[:-2], refs[-2], refs[-1]
    samples, positions, channels = x_ref.shape
    entries = positions * GSIZE
    rows = channels // shards
    grad_act = 0.0
    for index, (pack, grad_ref) in enumerate(zip(packs, grad_refs)):

        def place(slot, ref, pack=pack):
            rows_ref[slot * rows : (slot + 1) * rows, : pack.columns] = pack.read(ref)[:rows]

        for_each_slot(shards, me_ref[0], weight_refs[index * held : (index + 1) * held], place)
        weight = pltpu.roll(rows_ref[:, : pack.columns], me_ref[0] * rows, 0).astype(jnp.bfloat16)
        grad_act += lax.dot_general(
            grad_ref[...], weight, (((1,), (1,)), ((), ())), preferred_element_type=jnp.float32
        )
    inverse = inverse_ref[...]
    normed = [
        (x_ref[i].astype(jnp.float32) - mean_ref[i : i + 1, :]) * inverse[i : i + 1] for i in range(samples)
    ]
    grads = [grad_act[i * positions : (i + 1) * positions] * silu_grad(normed[i]) for i in range(samples)]
    means = table_sums(
        packs,
        jnp.concatenate(
            [position_sums(grads), position_sums([g * n for g, n in zip(grads, normed)])], axis=0
        ),
        same_group_ref[...],
    ) / entries
    for i in range(samples):
        first, second = means[i : i + 1], means[samples + i : samples + i + 1]
        out_ref[i] = (inverse[i : i + 1] * (grads[i] - first - normed[i] * second)).astype(jnp.bfloat16)


def adam_kernel(shards, pack, scales_ref, own_ref, *refs):
    other_refs, refs = refs[: shards - 1], refs[shards - 1 :]
    params_ref, first_ref, second_ref, token_ref, grad_ref, moved_ref, sent_ref = refs
    rows = pack.rows
    total = own_ref[...]
    for other_ref in other_refs:
        total = total + pack.read(other_ref)
    grad_ref[...] = total / shards
    grad = grad_ref[:rows, :]
    columns = slice(pack.start, pack.stop)
    first_new = BETA_ONE * first_ref[:, 0, columns] + (1.0 - BETA_ONE) * grad
    second_new = BETA_TWO * second_ref[:, 0, columns] + (1.0 - BETA_TWO) * grad * grad
    update = (scales_ref[0] * first_new) / (jnp.sqrt(second_new * scales_ref[1]) + ADAM_EPS)
    if rows < pack.deep:
        moved_ref[rows // 8 * 8 :, :] = jnp.zeros((pack.deep - rows // 8 * 8, pack.columns), jnp.float32)
    moved_ref[:rows, :] = params_ref[:, 0, columns] - update
    pack.write(sent_ref, moved_ref[...])


def moments_kernel(packs, first_ref, second_ref, *refs):
    grad_refs, (first_out, second_out) = refs[: len(packs)], refs[len(packs) :]
    rows = first_ref.shape[0]
    grad = jnp.concatenate([grad_ref[:rows, :] for grad_ref in grad_refs], axis=1)
    first_out[:, 0, :] = BETA_ONE * first_ref[:, 0, :] + (1.0 - BETA_ONE) * grad
    second_out[:, 0, :] = BETA_TWO * second_ref[:, 0, :] + (1.0 - BETA_TWO) * grad * grad


def average_kernel(packs, *refs):
    moved_refs, other_refs = refs[: len(packs)], refs[len(packs) : -3]
    out_ref, rows_ref, sem = refs[-3:]
    rows = out_ref.shape[0]
    pieces = [
        0.5 * (moved_ref[...] + pack.read(other_ref))
        for pack, moved_ref, other_ref in zip(packs, moved_refs, other_refs)
    ]
    rows_ref[:, 0, :] = jnp.concatenate(pieces, axis=1)[:rows]
    copy = pltpu.make_async_copy(rows_ref, out_ref, sem)
    copy.start()
    copy.wait()


SCALARS = pl.BlockSpec(memory_space=pltpu.SMEM)
BLOCKS = pl.BlockSpec(memory_space=pltpu.VMEM)
TOKEN = pl.BlockSpec(memory_space=pl.ANY)
IN_HBM = pl.BlockSpec(memory_space=pltpu.HBM)


def call(kernel, name, outs, specs, operands, scratch=(), out_specs=None, flops=0, elements=0):
    return pl.pallas_call(
        kernel,
        out_shape=outs,
        in_specs=specs,
        out_specs=out_specs or jax.tree.map(lambda _: BLOCKS, outs),
        scratch_shapes=list(scratch),
        compiler_params=pltpu.CompilerParams(vmem_limit_bytes=VMEM_BYTES),
        cost_estimate=pl.CostEstimate(flops=flops, bytes_accessed=8 * elements, transcendentals=elements),
        name=name,
    )(*operands)


def moved_on(block, axis, distance):
    size = lax.axis_size(axis)
    return lax.ppermute(block, axis, [(i, (i + distance) % size) for i in range(size)])


def gathered(piece, shards):
    if shards != 4:
        return [piece] + [moved_on(piece, "dp", -slot) for slot in range(1, shards)]
    two = moved_on(piece, "dp", -2)
    above = lax.ppermute(piece, "dp", [(i + 1, i) for i in range(shards - 1)])
    below = lax.ppermute(piece, "dp", [(i, i + 1) for i in range(shards - 1)])
    far = lax.ppermute(two, "dp", [(1, 0), (shards - 2, shards - 1)])
    return [piece, above, two, below, far]


def column_cuts(channels):
    half = (channels // GSIZE + 1) // 2 * GSIZE
    return [(0, half), (half, channels)]


def local(
    block_input, time_shift, out_grad, params, first_moment, second_moment, push_weight, step
):
    samples, positions, channels = block_input.shape
    tokens = samples * positions
    shards = lax.axis_size("dp")
    rows = params.shape[1]
    deep = padded(rows)
    me = lax.axis_index("dp").astype(jnp.int32).reshape(1)
    packs = [Packing(rows, start, stop) for start, stop in column_cuts(channels)]
    params, first_moment, second_moment = (
        jnp.transpose(array, (1, 0, 2)) for array in (params, first_moment, second_moment)
    )
    shard_list = call(
        functools.partial(cast_kernel, packs),
        "cast",
        tuple(pack.payload() for pack in packs),
        [SCALARS, BLOCKS],
        (push_weight, params),
        scratch=[pltpu.VMEM((deep, channels), jnp.float32)],
        elements=rows * channels,
    )
    weights = [gathered(piece, shards) for piece in shard_list]
    held = len(weights[0])

    level_count = lax.axis_size("replica").bit_length() - 1
    distance_bits = step[0] % level_count
    step_count = (step[0] + 1).astype(jnp.float32)
    scales = jnp.stack(
        [LEARN_RATE / (1.0 - jnp.power(BETA_ONE, step_count)), 1.0 / (1.0 - jnp.power(BETA_TWO, step_count))]
    )

    activation, mean_in, inverse_in, same_group, *pieces = call(
        functools.partial(norm_in_kernel, shards, packs),
        "norm_in",
        (
            jax.ShapeDtypeStruct((shards * deep, tokens), jnp.bfloat16),
            jax.ShapeDtypeStruct((samples, channels), jnp.float32),
            jax.ShapeDtypeStruct((samples, channels), jnp.float32),
            jax.ShapeDtypeStruct((max(pack.columns for pack in packs),) * 2, jnp.bfloat16),
            *(jax.ShapeDtypeStruct((samples, pack.columns), jnp.float32) for pack in packs),
            *(jax.ShapeDtypeStruct((samples, positions, pack.columns), jnp.bfloat16) for pack in packs),
        ),
        [SCALARS, SCALARS, BLOCKS, BLOCKS, BLOCKS],
        (me, scales, block_input, time_shift, out_grad),
        elements=tokens * channels,
    )

    hidden_grads, owns, arrived = [], [], []
    token = mean_in
    shifts, out_grads = pieces[: len(packs)], pieces[len(packs) :]
    for pack, shard_list, shift, out_grad_piece in zip(packs, weights, shifts, out_grads):
        grad_hidden, own, *sends = call(
            functools.partial(mix_kernel, shards, held, pack),
            "mix",
            (pltpu.HBM((tokens, pack.columns), jnp.bfloat16), pack.block())
            + (pack.payload(),) * (shards - 1),
            [SCALARS] + [BLOCKS] * (4 + held) + [TOKEN],
            (me, activation, shift, out_grad_piece, same_group, *shard_list, token),
            scratch=[
                pltpu.VMEM((shards * deep, pack.columns), jnp.bfloat16),
                pltpu.VMEM((tokens, pack.columns), jnp.bfloat16),
                pltpu.SemaphoreType.DMA,
            ],
            out_specs=(IN_HBM,) + (BLOCKS,) * shards,
            flops=4 * tokens * channels * pack.columns,
            elements=tokens * pack.columns,
        )
        token = own
        hidden_grads.append(grad_hidden)
        owns.append(own)
        arrived.append([moved_on(send, "dp", slot) for slot, send in enumerate(sends, 1)])

    grad_input = call(
        functools.partial(input_grad_kernel, shards, held, packs),
        "input_grad",
        jax.ShapeDtypeStruct(block_input.shape, jnp.bfloat16),
        [SCALARS] + [BLOCKS] * (4 + len(packs) * (1 + held)),
        (me, block_input, mean_in, inverse_in, same_group, *hidden_grads, *weights[0], *weights[1]),
        scratch=[pltpu.VMEM((channels, max(pack.columns for pack in packs)), jnp.float32)],
        flops=2 * tokens * channels * channels,
        elements=tokens * channels,
    )

    def adam(pack, own, others, token):
        return call(
            functools.partial(adam_kernel, shards, pack),
            "adam",
            (pack.block(), pack.block(), pack.payload()),
            [SCALARS] + [BLOCKS] * (3 + shards) + [TOKEN],
            (scales, own, *others, params, first_moment, second_moment, token),
            elements=rows * pack.columns,
        )

    def moments(*grads):
        return call(
            functools.partial(moments_kernel, packs),
            "moments",
            (jax.ShapeDtypeStruct(params.shape, jnp.float32),) * 2,
            [BLOCKS] * (2 + len(packs)),
            (first_moment, second_moment, *grads),
            elements=rows * channels,
        )

    def average(*blocks):
        return call(
            functools.partial(average_kernel, packs),
            "average",
            pltpu.HBM(params.shape, jnp.float32),
            [BLOCKS] * (2 * len(packs)),
            blocks,
            scratch=[pltpu.VMEM(params.shape, jnp.float32), pltpu.SemaphoreType.DMA],
            out_specs=IN_HBM,
            elements=rows * channels,
        )

    def from_behind(finish, *operands):
        def branch(distance):
            return lambda *values: finish(lambda block: moved_on(block, "replica", distance), *values)

        return lax.switch(distance_bits, [branch(1 << power) for power in range(level_count)], *operands)

    grad_a, moved_a, sent_a = adam(packs[0], owns[0], arrived[0], token)
    other_a, other_weight = from_behind(
        lambda move, sent, weight: (move(sent), move(weight)), sent_a, push_weight.astype(jnp.bfloat16)
    )
    grad_b, moved_b, sent_b = adam(packs[1], owns[1], arrived[1], other_a)

    def finish(move, sent, *values):
        grads, moved, other_first = values[:2], values[2:4], values[4]
        other = move(sent)
        return (*moments(*grads), average(*moved, other_first, other))

    first_new, second_new, averaged = from_behind(finish, sent_b, grad_a, grad_b, moved_a, moved_b, other_a)
    new_weight = 0.5 * (push_weight + other_weight.astype(jnp.float32))
    return (
        grad_input,
        *(jnp.transpose(array, (1, 0, 2)) for array in (averaged, first_new, second_new)),
        new_weight,
    )


def solution(mesh):
    placed = (
        P(("replica", "dp"), None, None),
        P(("replica", "dp"), None),
        P(("replica", "dp"), None, None),
        P("replica", "dp", None),
        P("replica", "dp", None),
        P("replica", "dp", None),
        P("replica"),
        P(),
    )
    return jax.shard_map(
        local,
        mesh=mesh,
        in_specs=placed,
        out_specs=(
            P(("replica", "dp"), None, None),
            P("replica", "dp", None),
            P("replica", "dp", None),
            P("replica", "dp", None),
            P("replica"),
        ),
        check_vma=False,
    )
```

```python
import functools

import jax
import jax.numpy as jnp
from jax import lax
from jax.experimental import pallas as pl
from jax.experimental.pallas import tpu as pltpu
from jax.sharding import PartitionSpec as P

GSIZE = 40

NORM_EPS = 1e-05
BETA_ONE = 0.9
BETA_TWO = 0.999
LEARN_RATE = 0.002
ADAM_EPS = 1e-08

LANES = 128
TILE_ROWS = 16
VMEM_BYTES = 16 * 1024 * 1024


def padded(rows):
    return -(-rows // TILE_ROWS) * TILE_ROWS


def packed_rows(rows):
    return padded(rows + 1)


class Packing:
    def __init__(self, rows, start, stop):
        self.rows, self.start, self.stop = rows, start, stop
        self.columns = stop - start
        self.deep = packed_rows(rows)
        self.tiles, self.rest = divmod(self.columns, LANES)
        fold = LANES // self.rest if self.rest else 1
        self.fold_rows = padded(-(-self.deep // fold))
        self.folds = [
            (first, min(self.fold_rows, self.deep - first)) for first in range(0, self.deep, self.fold_rows)
        ]
        self.height = self.tiles * self.deep + (self.fold_rows if self.rest else 0)

    def write(self, ref, block):
        for tile in range(self.tiles):
            ref[tile * self.deep : (tile + 1) * self.deep, :] = block[
                :, tile * LANES : (tile + 1) * LANES
            ].astype(ref.dtype)
        if self.rest:
            left = block[:, self.tiles * LANES :]
            parts = []
            for first, count in self.folds:
                part = left[first : first + count]
                if count < self.fold_rows:
                    part = jnp.concatenate(
                        [part, jnp.zeros((self.fold_rows - count, self.rest), part.dtype)], axis=0
                    )
                parts.append(part)
            spare = LANES - self.rest * len(parts)
            if spare:
                parts.append(jnp.zeros((self.fold_rows, spare), left.dtype))
            ref[self.tiles * self.deep :, :] = jnp.concatenate(parts, axis=1).astype(ref.dtype)

    def read(self, ref):
        pieces = [
            ref[tile * self.deep : (tile + 1) * self.deep, :].astype(jnp.float32) for tile in range(self.tiles)
        ]
        if self.rest:
            left = ref[self.tiles * self.deep :, :].astype(jnp.float32)
            parts = [
                left[:count, i * self.rest : (i + 1) * self.rest] for i, (_, count) in enumerate(self.folds)
            ]
            pieces.append(jnp.concatenate(parts, axis=0) if len(parts) > 1 else parts[0])
        return jnp.concatenate(pieces, axis=1) if len(pieces) > 1 else pieces[0]

    def unpack(self, ref, out_ref, first_row):
        for tile in range(self.tiles):
            out_ref[first_row : first_row + self.deep, tile * LANES : (tile + 1) * LANES] = ref[
                tile * self.deep : (tile + 1) * self.deep, :
            ]
        if self.rest:
            left = ref[self.tiles * self.deep :, :]
            for i, (first, count) in enumerate(self.folds):
                out_ref[first_row + first : first_row + first + count, self.tiles * LANES :] = left[
                    :count, i * self.rest : (i + 1) * self.rest
                ]

    def payload(self):
        return jax.ShapeDtypeStruct((self.height, LANES), jnp.bfloat16)

    def block(self):
        return jax.ShapeDtypeStruct((self.deep, self.columns), jnp.float32)


def group_sums(rows, same_group):
    high = rows.astype(jnp.bfloat16).astype(jnp.float32)
    rest = rows - high
    middle = rest.astype(jnp.bfloat16).astype(jnp.float32)
    count = rows.shape[0]
    stacked = jnp.concatenate([high, middle, rest - middle], axis=0).astype(jnp.bfloat16)
    sums = jnp.dot(stacked, same_group, preferred_element_type=jnp.float32)
    return sums[:count] + (sums[count : 2 * count] + sums[2 * count :])


def table_sums(packs, rows, same_group):
    return jnp.concatenate(
        [
            group_sums(rows[:, pack.start : pack.stop], same_group[: pack.columns, : pack.columns])
            for pack in packs
        ],
        axis=1,
    )


def position_sums(parts):
    return jnp.concatenate([jnp.sum(part, axis=0, keepdims=True) for part in parts], axis=0)


def sigmoid(values):
    return 0.5 * jnp.tanh(0.5 * values) + 0.5


def silu_grad(values):
    gate = sigmoid(values)
    return gate * (1.0 + values * (1.0 - gate))


def cast_kernel(packs, push_ref, params_ref, *refs):
    out_refs, rows_ref = refs[:-1], refs[-1]
    rows = params_ref.shape[0]
    rows_ref[rows // 8 * 8 :, :] = jnp.zeros((rows_ref.shape[0] - rows // 8 * 8, rows_ref.shape[1]), jnp.float32)
    rows_ref[:rows, :] = params_ref[:, 0, :] / push_ref[0]
    for pack, out_ref in zip(packs, out_refs):
        pack.write(out_ref, rows_ref[:, pack.start : pack.stop])


def norm_in_kernel(shards, packs, me_ref, scales_ref, x_ref, shift_ref, out_grad_ref, *refs):
    act_ref, mean_ref, inverse_ref, same_group_ref = refs[:4]
    shift_refs, out_grad_refs = refs[4 : 4 + len(packs)], refs[4 + len(packs) :]
    samples, positions, channels = x_ref.shape
    for pack, shift_out, out_grad_out in zip(packs, shift_refs, out_grad_refs):
        shift_out[...] = shift_ref[...].astype(jnp.float32)[:, pack.start : pack.stop]
        for i in range(samples):
            out_grad_out[i] = out_grad_ref[i][:, pack.start : pack.stop]
    group_of_row = lax.broadcasted_iota(jnp.int32, same_group_ref.shape, 0) // GSIZE
    group_of_column = lax.broadcasted_iota(jnp.int32, same_group_ref.shape, 1) // GSIZE
    same_group_ref[...] = (group_of_row == group_of_column).astype(jnp.float32).astype(jnp.bfloat16)
    rows = channels // shards
    deep = act_ref.shape[0] // shards
    entries = positions * GSIZE
    same_group = same_group_ref[...]
    parts = [x_ref[i].astype(jnp.float32) for i in range(samples)]
    mean = table_sums(packs, position_sums(parts), same_group) / entries
    centered = [parts[i] - mean[i : i + 1] for i in range(samples)]
    variance = table_sums(packs, position_sums([part * part for part in centered]), same_group) / entries
    inverse = lax.rsqrt(variance + NORM_EPS)
    mean_ref[...] = mean
    inverse_ref[...] = inverse
    normed = [centered[i] * inverse[i : i + 1] for i in range(samples)]
    act = jnp.concatenate([part * sigmoid(part) for part in normed], axis=0)
    turned = pltpu.roll(act.T, channels - me_ref[0] * rows, 0)
    act_ref[...] = jnp.zeros_like(act_ref)
    for slot in range(shards):
        act_ref[slot * deep : slot * deep + rows, :] = turned[slot * rows : (slot + 1) * rows].astype(jnp.bfloat16)


def mix_kernel(shards, pack, act_ref, shift_ref, out_grad_ref, same_group_ref, *refs):
    weight_refs, token_ref, refs = refs[:shards], refs[shards], refs[shards + 1 :]
    grad_hidden_ref, weight_out_ref, own_ref = refs[:3]
    send_refs, (weight_ref, kept_ref, sems) = refs[3 : 2 + shards], refs[2 + shards :]
    samples, positions, columns = out_grad_ref.shape
    entries = positions * GSIZE
    deep = pack.deep
    for slot, shard_ref in enumerate(weight_refs):
        pack.unpack(shard_ref, weight_ref, slot * deep)
    weight_copy = pltpu.make_async_copy(weight_ref, weight_out_ref, sems.at[0])
    weight_copy.start()
    same_group = same_group_ref[:columns, :columns]
    hidden = lax.dot_general(
        act_ref[...], weight_ref[...], (((0,), (0,)), ((), ())), preferred_element_type=jnp.float32
    )
    parts = [
        hidden[i * positions : (i + 1) * positions] + shift_ref[i : i + 1, :]
        for i in range(samples)
    ]
    mean = group_sums(position_sums(parts), same_group) / entries
    parts = [parts[i] - mean[i : i + 1] for i in range(samples)]
    variance = group_sums(position_sums([part * part for part in parts]), same_group) / entries
    inverse = lax.rsqrt(variance + NORM_EPS)
    normed = [parts[i] * inverse[i : i + 1] for i in range(samples)]
    grads = [out_grad_ref[i].astype(jnp.float32) * silu_grad(normed[i]) for i in range(samples)]
    means = group_sums(
        jnp.concatenate(
            [position_sums(grads), position_sums([g * n for g, n in zip(grads, normed)])], axis=0
        ),
        same_group,
    ) / entries
    for i in range(samples):
        first, second = means[i : i + 1], means[samples + i : samples + i + 1]
        kept_ref[i * positions : (i + 1) * positions, :] = (
            inverse[i : i + 1] * (grads[i] - first - normed[i] * second)
        ).astype(jnp.bfloat16)
    copy = pltpu.make_async_copy(kept_ref, grad_hidden_ref, sems.at[1])
    copy.start()
    grad = jnp.dot(act_ref[...], kept_ref[...], preferred_element_type=jnp.float32)
    for slot, send_ref in enumerate(send_refs, 1):
        pack.write(send_ref, grad[slot * deep : (slot + 1) * deep])
    own_ref[...] = grad[:deep]
    weight_copy.wait()
    copy.wait()


def input_grad_kernel(shards, packs, me_ref, mean_ref, inverse_ref, same_group_ref, x_hbm, *refs):
    count = len(packs)
    grad_hbms, weight_hbms, out_ref = refs[:count], refs[count : 2 * count], refs[2 * count]
    rows_ref, x_ref, sems = refs[2 * count + 1 : 2 * count + 4]
    grad_refs, weight_refs = refs[2 * count + 4 : 3 * count + 4], refs[3 * count + 4 :]
    copies = [
        pltpu.make_async_copy(source, target, sems.at[i])
        for i, (source, target) in enumerate(
            zip((*weight_hbms, *grad_hbms, x_hbm), (*weight_refs, *grad_refs, x_ref))
        )
    ]
    for copy in copies:
        copy.start()
    samples, positions, channels = x_ref.shape
    entries = positions * GSIZE
    rows = channels // shards
    weights = []
    for index, (pack, weight_ref) in enumerate(zip(packs, weight_refs)):
        copies[index].wait()
        for slot in range(shards):
            rows_ref[slot * rows : (slot + 1) * rows, : pack.columns] = weight_ref[
                slot * pack.deep : (slot + 1) * pack.deep, :
            ].astype(jnp.float32)[:rows]
        weights.append(pltpu.roll(rows_ref[:, : pack.columns], me_ref[0] * rows, 0).astype(jnp.bfloat16))
    grad_act = 0.0
    for index, (grad_ref, weight) in enumerate(zip(grad_refs, weights)):
        copies[count + index].wait()
        grad_act += lax.dot_general(
            grad_ref[...], weight, (((1,), (1,)), ((), ())), preferred_element_type=jnp.float32
        )
    copies[-1].wait()
    inverse = inverse_ref[...]
    normed = [
        (x_ref[i].astype(jnp.float32) - mean_ref[i : i + 1, :]) * inverse[i : i + 1] for i in range(samples)
    ]
    grads = [grad_act[i * positions : (i + 1) * positions] * silu_grad(normed[i]) for i in range(samples)]
    means = table_sums(
        packs,
        jnp.concatenate(
            [position_sums(grads), position_sums([g * n for g, n in zip(grads, normed)])], axis=0
        ),
        same_group_ref[...],
    ) / entries
    for i in range(samples):
        first, second = means[i : i + 1], means[samples + i : samples + i + 1]
        out_ref[i] = (inverse[i : i + 1] * (grads[i] - first - normed[i] * second)).astype(jnp.bfloat16)


def adam_step(shards, pack, scales_ref, own_ref, other_refs, blocks, grad_ref, moved_ref):
    rows = pack.rows
    total = own_ref[...]
    for other_ref in other_refs:
        total = total + pack.read(other_ref)
    grad_ref[...] = total / shards
    grad = grad_ref[:rows, :]
    params, first, second = blocks()
    first_new = BETA_ONE * first + (1.0 - BETA_ONE) * grad
    second_new = BETA_TWO * second + (1.0 - BETA_TWO) * grad * grad
    update = (scales_ref[0] * first_new) / (jnp.sqrt(second_new * scales_ref[1]) + ADAM_EPS)
    moved_ref[rows // 8 * 8 :, :] = jnp.zeros((pack.deep - rows // 8 * 8, pack.columns), jnp.float32)
    moved_ref[:rows, :] = params - update


def first_adam_kernel(shards, packs, scales_ref, push_ref, own_ref, *refs):
    pack, later = packs
    other_refs, refs = refs[: shards - 1], refs[shards - 1 :]
    hbm_refs, token_ref, (grad_ref, moved_ref, sent_ref), later_refs = refs[:3], refs[3], refs[4:7], refs[7:10]
    row_refs, sems = refs[10:13], refs[13]
    copies = [
        pltpu.make_async_copy(source, target, sems.at[i])
        for i, (source, target) in enumerate(zip(hbm_refs, row_refs))
    ]
    for copy in copies:
        copy.start()

    def blocks():
        for copy in copies:
            copy.wait()
        return [row_ref[:, 0, pack.start : pack.stop] for row_ref in row_refs]

    adam_step(shards, pack, scales_ref, own_ref, other_refs, blocks, grad_ref, moved_ref)
    moved = moved_ref[...]
    spare = lax.broadcasted_iota(jnp.int32, moved.shape, 0) == pack.rows
    pack.write(sent_ref, jnp.where(spare, push_ref[0], moved))
    for row_ref, later_ref in zip(row_refs, later_refs):
        later_ref[...] = row_ref[:, 0, later.start : later.stop]


def second_adam_kernel(shards, pack, scales_ref, own_ref, *refs):
    other_refs, refs = refs[: shards - 1], refs[shards - 1 :]
    block_refs, token_ref, (grad_ref, moved_ref, sent_ref) = refs[:3], refs[3], refs[4:]
    adam_step(
        shards, pack, scales_ref, own_ref, other_refs, lambda: [ref[...] for ref in block_refs], grad_ref, moved_ref
    )
    pack.write(sent_ref, moved_ref[...])


def half_average_kernel(pack, push_ref, moved_ref, other_ref, mean_ref, push_out_ref):
    other = pack.read(other_ref)
    mean_ref[...] = 0.5 * (moved_ref[...] + other)
    push_out_ref[0:1, :] = 0.5 * (push_ref[0] + other[pack.rows : pack.rows + 1, :LANES])


def moments_kernel(packs, first_ref, second_ref, *refs):
    grad_refs, (first_out, second_out) = refs[: len(packs)], refs[len(packs) :]
    rows = first_ref.shape[0]
    grad = jnp.concatenate([grad_ref[:rows, :] for grad_ref in grad_refs], axis=1)
    first_out[:, 0, :] = BETA_ONE * first_ref[:, 0, :] + (1.0 - BETA_ONE) * grad
    second_out[:, 0, :] = BETA_TWO * second_ref[:, 0, :] + (1.0 - BETA_TWO) * grad * grad


def average_kernel(pack, mean_ref, moved_ref, other_ref, out_ref, rows_ref, sem):
    rows = out_ref.shape[0]
    later = 0.5 * (moved_ref[...] + pack.read(other_ref))
    rows_ref[:, 0, :] = jnp.concatenate([mean_ref[...], later], axis=1)[:rows]
    copy = pltpu.make_async_copy(rows_ref, out_ref, sem)
    copy.start()
    copy.wait()


SCALARS = pl.BlockSpec(memory_space=pltpu.SMEM)
BLOCKS = pl.BlockSpec(memory_space=pltpu.VMEM)
TOKEN = pl.BlockSpec(memory_space=pl.ANY)
IN_HBM = pl.BlockSpec(memory_space=pltpu.HBM)


def call(kernel, name, outs, specs, operands, scratch=(), out_specs=None, flops=0, elements=0):
    return pl.pallas_call(
        kernel,
        out_shape=outs,
        in_specs=specs,
        out_specs=out_specs or jax.tree.map(lambda _: BLOCKS, outs),
        scratch_shapes=list(scratch),
        compiler_params=pltpu.CompilerParams(vmem_limit_bytes=VMEM_BYTES),
        cost_estimate=pl.CostEstimate(flops=flops, bytes_accessed=8 * elements, transcendentals=elements),
        name=name,
    )(*operands)


def stay(array):
    return pltpu.with_memory_space_constraint(array, pltpu.HBM)


def moved_on(block, axis, distance):
    size = lax.axis_size(axis)
    return lax.ppermute(block, axis, [(i, (i + distance) % size) for i in range(size)])


def column_cuts(channels):
    half = (channels // GSIZE + 1) // 2 * GSIZE
    return [(0, half), (half, channels)]


def local(
    block_input, time_shift, out_grad, params, first_moment, second_moment, push_weight, step
):
    samples, positions, channels = block_input.shape
    tokens = samples * positions
    shards = lax.axis_size("dp")
    rows = params.shape[1]
    deep = packed_rows(rows)
    me = lax.axis_index("dp").astype(jnp.int32).reshape(1)
    packs = [Packing(rows, start, stop) for start, stop in column_cuts(channels)]
    params, first_moment, second_moment = (
        jnp.transpose(array, (1, 0, 2)) for array in (params, first_moment, second_moment)
    )
    shard_list = call(
        functools.partial(cast_kernel, packs),
        "cast",
        tuple(pack.payload() for pack in packs),
        [SCALARS, BLOCKS],
        (push_weight, params),
        scratch=[pltpu.VMEM((deep, channels), jnp.float32)],
        elements=rows * channels,
    )
    weights = [
        [piece] + [moved_on(piece, "dp", -slot) for slot in range(1, shards)] for piece in shard_list
    ]

    level_count = lax.axis_size("replica").bit_length() - 1
    distance_bits = step[0] % level_count
    step_count = (step[0] + 1).astype(jnp.float32)
    scales = jnp.stack(
        [LEARN_RATE / (1.0 - jnp.power(BETA_ONE, step_count)), 1.0 / (1.0 - jnp.power(BETA_TWO, step_count))]
    )

    activation, mean_in, inverse_in, same_group, *pieces = call(
        functools.partial(norm_in_kernel, shards, packs),
        "norm_in",
        (
            jax.ShapeDtypeStruct((shards * deep, tokens), jnp.bfloat16),
            jax.ShapeDtypeStruct((samples, channels), jnp.float32),
            jax.ShapeDtypeStruct((samples, channels), jnp.float32),
            jax.ShapeDtypeStruct((max(pack.columns for pack in packs),) * 2, jnp.bfloat16),
            *(jax.ShapeDtypeStruct((samples, pack.columns), jnp.float32) for pack in packs),
            *(jax.ShapeDtypeStruct((samples, positions, pack.columns), jnp.bfloat16) for pack in packs),
        ),
        [SCALARS, SCALARS, BLOCKS, BLOCKS, BLOCKS],
        (me, scales, block_input, time_shift, out_grad),
        elements=tokens * channels,
    )

    hidden_grads, full_weights, owns, arrived = [], [], [], []
    token = mean_in
    shifts, out_grads = pieces[: len(packs)], pieces[len(packs) :]
    for pack, shard_list, shift, out_grad_piece in zip(packs, weights, shifts, out_grads):
        grad_hidden, full_weight, own, *sends = call(
            functools.partial(mix_kernel, shards, pack),
            "mix",
            (
                pltpu.HBM((tokens, pack.columns), jnp.bfloat16),
                pltpu.HBM((shards * deep, pack.columns), jnp.bfloat16),
                pack.block(),
            )
            + (pack.payload(),) * (shards - 1),
            [BLOCKS] * (4 + shards) + [TOKEN],
            (activation, shift, out_grad_piece, same_group, *shard_list, token),
            scratch=[
                pltpu.VMEM((shards * deep, pack.columns), jnp.bfloat16),
                pltpu.VMEM((tokens, pack.columns), jnp.bfloat16),
                pltpu.SemaphoreType.DMA((2,)),
            ],
            out_specs=(IN_HBM,) * 2 + (BLOCKS,) * shards,
            flops=4 * tokens * channels * pack.columns,
            elements=tokens * pack.columns,
        )
        token = own
        hidden_grads.append(grad_hidden)
        full_weights.append(full_weight)
        owns.append(own)
        arrived.append([moved_on(send, "dp", slot) for slot, send in enumerate(sends, 1)])

    grad_input = call(
        functools.partial(input_grad_kernel, shards, packs),
        "input_grad",
        jax.ShapeDtypeStruct(block_input.shape, jnp.bfloat16),
        [SCALARS] + [BLOCKS] * 3 + [IN_HBM] * (1 + 2 * len(packs)),
        (me, mean_in, inverse_in, same_group, *map(stay, (block_input, *hidden_grads, *full_weights))),
        scratch=[
            pltpu.VMEM((channels, max(pack.columns for pack in packs)), jnp.float32),
            pltpu.VMEM(block_input.shape, jnp.bfloat16),
            pltpu.SemaphoreType.DMA((1 + 2 * len(packs),)),
            *(pltpu.VMEM((tokens, pack.columns), jnp.bfloat16) for pack in packs),
            *(pltpu.VMEM((shards * deep, pack.columns), jnp.bfloat16) for pack in packs),
        ],
        flops=2 * tokens * channels * channels,
        elements=tokens * channels,
    )

    def moments(*grads):
        return call(
            functools.partial(moments_kernel, packs),
            "moments",
            (jax.ShapeDtypeStruct(params.shape, jnp.float32),) * 2,
            [BLOCKS] * (2 + len(packs)),
            (first_moment, second_moment, *grads),
            elements=rows * channels,
        )

    def from_behind(finish, *operands):
        def branch(distance):
            return lambda *values: finish(lambda block: moved_on(block, "replica", distance), *values)

        return lax.switch(distance_bits, [branch(1 << power) for power in range(level_count)], *operands)

    early, late = packs
    rows_kept = jax.ShapeDtypeStruct((rows, late.columns), jnp.float32)
    grad_a, moved_a, sent_a, *late_blocks = call(
        functools.partial(first_adam_kernel, shards, packs),
        "adam",
        (early.block(), early.block(), early.payload()) + (rows_kept,) * 3,
        [SCALARS] * 2 + [BLOCKS] * shards + [IN_HBM] * 3 + [TOKEN],
        (scales, push_weight, owns[0], *arrived[0], stay(params), stay(first_moment), stay(second_moment), token),
        scratch=[pltpu.VMEM(params.shape, jnp.float32)] * 3 + [pltpu.SemaphoreType.DMA((3,))],
        elements=rows * channels,
    )

    def finish_early(move, sent, moved):
        return call(
            functools.partial(half_average_kernel, early),
            "half_average",
            (early.block(), jax.ShapeDtypeStruct((8, LANES), jnp.float32)),
            [SCALARS] + [BLOCKS] * 2,
            (push_weight, moved, move(sent)),
            elements=rows * early.columns,
        )

    mean_a, weight_tile = from_behind(finish_early, sent_a, moved_a)
    grad_b, moved_b, sent_b = call(
        functools.partial(second_adam_kernel, shards, late),
        "adam",
        (late.block(), late.block(), late.payload()),
        [SCALARS] + [BLOCKS] * (3 + shards) + [TOKEN],
        (scales, owns[1], *arrived[1], *late_blocks, mean_a),
        elements=rows * late.columns,
    )

    def finish_late(move, sent, grad_a, grad_b, mean_a, moved_b):
        other = move(sent)
        averaged = call(
            functools.partial(average_kernel, late),
            "average",
            pltpu.HBM(params.shape, jnp.float32),
            [BLOCKS] * 3,
            (mean_a, moved_b, other),
            scratch=[pltpu.VMEM(params.shape, jnp.float32), pltpu.SemaphoreType.DMA],
            out_specs=IN_HBM,
            elements=rows * channels,
        )
        return (*moments(grad_a, grad_b), averaged)

    first_new, second_new, averaged = from_behind(finish_late, sent_b, grad_a, grad_b, mean_a, moved_b)
    new_weight = weight_tile[0, :1]
    return (
        grad_input,
        *(jnp.transpose(array, (1, 0, 2)) for array in (averaged, first_new, second_new)),
        new_weight,
    )


def solution(mesh):
    placed = (
        P(("replica", "dp"), None, None),
        P(("replica", "dp"), None),
        P(("replica", "dp"), None, None),
        P("replica", "dp", None),
        P("replica", "dp", None),
        P("replica", "dp", None),
        P("replica"),
        P(),
    )
    return jax.shard_map(
        local,
        mesh=mesh,
        in_specs=placed,
        out_specs=(
            P(("replica", "dp"), None, None),
            P("replica", "dp", None),
            P("replica", "dp", None),
            P("replica", "dp", None),
            P("replica"),
        ),
        check_vma=False,
    )
```

```python
import functools

import jax
import jax.numpy as jnp
from jax import lax
from jax.experimental import pallas as pl
from jax.experimental.pallas import tpu as pltpu
from jax.sharding import PartitionSpec as P

GSIZE = 40

NORM_EPS = 1e-05
BETA_ONE = 0.9
BETA_TWO = 0.999
LEARN_RATE = 0.002
ADAM_EPS = 1e-08

LANES = 128
TILE_ROWS = 16
VMEM_BYTES = 16 * 1024 * 1024


def padded(rows):
    return -(-rows // TILE_ROWS) * TILE_ROWS


def packed_rows(rows):
    return padded(rows + 1)


class Packing:
    def __init__(self, rows, start, stop):
        self.rows, self.start, self.stop = rows, start, stop
        self.columns = stop - start
        self.deep = packed_rows(rows)
        self.tiles, self.rest = divmod(self.columns, LANES)
        fold = LANES // self.rest if self.rest else 1
        self.fold_rows = padded(-(-self.deep // fold))
        self.folds = [
            (first, min(self.fold_rows, self.deep - first)) for first in range(0, self.deep, self.fold_rows)
        ]
        self.height = self.tiles * self.deep + (self.fold_rows if self.rest else 0)

    def write(self, ref, block):
        for tile in range(self.tiles):
            ref[tile * self.deep : (tile + 1) * self.deep, :] = block[
                :, tile * LANES : (tile + 1) * LANES
            ].astype(ref.dtype)
        if self.rest:
            left = block[:, self.tiles * LANES :]
            parts = []
            for first, count in self.folds:
                part = left[first : first + count]
                if count < self.fold_rows:
                    part = jnp.concatenate(
                        [part, jnp.zeros((self.fold_rows - count, self.rest), part.dtype)], axis=0
                    )
                parts.append(part)
            spare = LANES - self.rest * len(parts)
            if spare:
                parts.append(jnp.zeros((self.fold_rows, spare), left.dtype))
            ref[self.tiles * self.deep :, :] = jnp.concatenate(parts, axis=1).astype(ref.dtype)

    def read(self, ref):
        pieces = [
            ref[tile * self.deep : (tile + 1) * self.deep, :].astype(jnp.float32) for tile in range(self.tiles)
        ]
        if self.rest:
            left = ref[self.tiles * self.deep :, :].astype(jnp.float32)
            parts = [
                left[:count, i * self.rest : (i + 1) * self.rest] for i, (_, count) in enumerate(self.folds)
            ]
            pieces.append(jnp.concatenate(parts, axis=0) if len(parts) > 1 else parts[0])
        return jnp.concatenate(pieces, axis=1) if len(pieces) > 1 else pieces[0]

    def unpack(self, ref, out_ref, first_row):
        for tile in range(self.tiles):
            out_ref[first_row : first_row + self.deep, tile * LANES : (tile + 1) * LANES] = ref[
                tile * self.deep : (tile + 1) * self.deep, :
            ]
        if self.rest:
            left = ref[self.tiles * self.deep :, :]
            for i, (first, count) in enumerate(self.folds):
                out_ref[first_row + first : first_row + first + count, self.tiles * LANES :] = left[
                    :count, i * self.rest : (i + 1) * self.rest
                ]

    def payload(self):
        return jax.ShapeDtypeStruct((self.height, LANES), jnp.bfloat16)

    def block(self):
        return jax.ShapeDtypeStruct((self.deep, self.columns), jnp.float32)


def group_sums(rows, same_group):
    high = rows.astype(jnp.bfloat16).astype(jnp.float32)
    rest = rows - high
    middle = rest.astype(jnp.bfloat16).astype(jnp.float32)
    count = rows.shape[0]
    stacked = jnp.concatenate([high, middle, rest - middle], axis=0).astype(jnp.bfloat16)
    sums = jnp.dot(stacked, same_group, preferred_element_type=jnp.float32)
    return sums[:count] + (sums[count : 2 * count] + sums[2 * count :])


def table_sums(packs, rows, same_group):
    return jnp.concatenate(
        [
            group_sums(rows[:, pack.start : pack.stop], same_group[: pack.columns, : pack.columns])
            for pack in packs
        ],
        axis=1,
    )


def position_sums(parts):
    return jnp.concatenate([jnp.sum(part, axis=0, keepdims=True) for part in parts], axis=0)


def sigmoid(values):
    return 0.5 * jnp.tanh(0.5 * values) + 0.5


def silu_grad(values):
    gate = sigmoid(values)
    return gate * (1.0 + values * (1.0 - gate))


def cast_kernel(packs, push_ref, params_ref, *refs):
    out_refs, rows_ref = refs[:-1], refs[-1]
    rows = params_ref.shape[0]
    rows_ref[rows // 8 * 8 :, :] = jnp.zeros((rows_ref.shape[0] - rows // 8 * 8, rows_ref.shape[1]), jnp.float32)
    rows_ref[:rows, :] = params_ref[:, 0, :] / push_ref[0]
    for pack, out_ref in zip(packs, out_refs):
        pack.write(out_ref, rows_ref[:, pack.start : pack.stop])


def norm_in_kernel(shards, packs, me_ref, scales_ref, shift_ref, x_hbm, out_grad_hbm, *refs):
    act_ref, mean_ref, inverse_ref, same_group_ref = refs[:4]
    shift_refs, out_grad_refs = refs[4 : 4 + len(packs)], refs[4 + len(packs) : 4 + 2 * len(packs)]
    x_ref, out_grad_ref, sems = refs[4 + 2 * len(packs) :]
    copies = [
        pltpu.make_async_copy(x_hbm, x_ref, sems.at[0]),
        pltpu.make_async_copy(out_grad_hbm, out_grad_ref, sems.at[1]),
    ]
    for copy in copies:
        copy.start()
    samples, positions, channels = x_ref.shape
    rows = channels // shards
    deep = act_ref.shape[0] // shards
    entries = positions * GSIZE
    group_of_row = lax.broadcasted_iota(jnp.int32, same_group_ref.shape, 0) // GSIZE
    group_of_column = lax.broadcasted_iota(jnp.int32, same_group_ref.shape, 1) // GSIZE
    same_group_ref[...] = (group_of_row == group_of_column).astype(jnp.float32).astype(jnp.bfloat16)
    same_group = same_group_ref[...]
    for pack, shift_out in zip(packs, shift_refs):
        shift_out[...] = shift_ref[...].astype(jnp.float32)[:, pack.start : pack.stop]
    copies[0].wait()
    parts = [x_ref[i].astype(jnp.float32) for i in range(samples)]
    mean = table_sums(packs, position_sums(parts), same_group) / entries
    centered = [parts[i] - mean[i : i + 1] for i in range(samples)]
    variance = table_sums(packs, position_sums([part * part for part in centered]), same_group) / entries
    inverse = lax.rsqrt(variance + NORM_EPS)
    mean_ref[...] = mean
    inverse_ref[...] = inverse
    normed = [centered[i] * inverse[i : i + 1] for i in range(samples)]
    act = jnp.concatenate([part * sigmoid(part) for part in normed], axis=0).T
    for block in range(shards):
        slot = lax.rem(block + shards - me_ref[0], shards)
        act_ref[pl.ds(pl.multiple_of(slot * deep, TILE_ROWS), deep), :] = jnp.concatenate(
            [act[block * rows : (block + 1) * rows], jnp.zeros((deep - rows, act.shape[1]), jnp.float32)], axis=0
        ).astype(jnp.bfloat16)
    copies[1].wait()
    for pack, out_grad_out in zip(packs, out_grad_refs):
        for i in range(samples):
            out_grad_out[i] = out_grad_ref[i][:, pack.start : pack.stop]


def mix_kernel(shards, pack, act_ref, shift_ref, out_grad_ref, same_group_ref, *refs):
    weight_refs, token_ref, refs = refs[:shards], refs[shards], refs[shards + 1 :]
    grad_hidden_ref, weight_out_ref, own_ref = refs[:3]
    send_refs, (weight_ref, kept_ref, sems) = refs[3 : 2 + shards], refs[2 + shards :]
    samples, positions, columns = out_grad_ref.shape
    entries = positions * GSIZE
    deep = pack.deep
    for slot, shard_ref in enumerate(weight_refs):
        pack.unpack(shard_ref, weight_ref, slot * deep)
    weight_copy = pltpu.make_async_copy(weight_ref, weight_out_ref, sems.at[0])
    weight_copy.start()
    same_group = same_group_ref[:columns, :columns]
    hidden = lax.dot_general(
        act_ref[...], weight_ref[...], (((0,), (0,)), ((), ())), preferred_element_type=jnp.float32
    )
    parts = [
        hidden[i * positions : (i + 1) * positions] + shift_ref[i : i + 1, :]
        for i in range(samples)
    ]
    mean = group_sums(position_sums(parts), same_group) / entries
    parts = [parts[i] - mean[i : i + 1] for i in range(samples)]
    variance = group_sums(position_sums([part * part for part in parts]), same_group) / entries
    inverse = lax.rsqrt(variance + NORM_EPS)
    normed = [parts[i] * inverse[i : i + 1] for i in range(samples)]
    grads = [out_grad_ref[i].astype(jnp.float32) * silu_grad(normed[i]) for i in range(samples)]
    means = group_sums(
        jnp.concatenate(
            [position_sums(grads), position_sums([g * n for g, n in zip(grads, normed)])], axis=0
        ),
        same_group,
    ) / entries
    for i in range(samples):
        first, second = means[i : i + 1], means[samples + i : samples + i + 1]
        kept_ref[i * positions : (i + 1) * positions, :] = (
            inverse[i : i + 1] * (grads[i] - first - normed[i] * second)
        ).astype(jnp.bfloat16)
    copy = pltpu.make_async_copy(kept_ref, grad_hidden_ref, sems.at[1])
    copy.start()
    grad = jnp.dot(act_ref[...], kept_ref[...], preferred_element_type=jnp.float32)
    for slot, send_ref in enumerate(send_refs, 1):
        pack.write(send_ref, grad[slot * deep : (slot + 1) * deep])
    own_ref[...] = grad[:deep]
    weight_copy.wait()
    copy.wait()


def input_grad_kernel(shards, packs, me_ref, mean_ref, inverse_ref, same_group_ref, x_hbm, *refs):
    count = len(packs)
    grad_hbms, weight_hbms, out_ref = refs[:count], refs[count : 2 * count], refs[2 * count]
    rows_ref, x_ref, made_ref, sems = refs[2 * count + 1 : 2 * count + 5]
    grad_refs, weight_refs = refs[2 * count + 5 : 3 * count + 5], refs[3 * count + 5 :]
    copies = [
        pltpu.make_async_copy(source, target, sems.at[i])
        for i, (source, target) in enumerate(
            zip((*weight_hbms, *grad_hbms, x_hbm), (*weight_refs, *grad_refs, x_ref))
        )
    ]
    for copy in copies:
        copy.start()
    samples, positions, channels = x_ref.shape
    entries = positions * GSIZE
    rows = channels // shards
    weights = []
    for index, (pack, weight_ref) in enumerate(zip(packs, weight_refs)):
        copies[index].wait()
        for block in range(shards):
            slot = lax.rem(block + shards - me_ref[0], shards)
            rows_ref[block * rows : (block + 1) * rows, : pack.columns] = weight_ref[
                pl.ds(pl.multiple_of(slot * pack.deep, TILE_ROWS), pack.deep), :
            ].astype(jnp.float32)[:rows]
        weights.append(rows_ref[:, : pack.columns].astype(jnp.bfloat16))
    grad_act = 0.0
    for index, (grad_ref, weight) in enumerate(zip(grad_refs, weights)):
        copies[count + index].wait()
        grad_act += lax.dot_general(
            grad_ref[...], weight, (((1,), (1,)), ((), ())), preferred_element_type=jnp.float32
        )
    copies[-1].wait()
    inverse = inverse_ref[...]
    normed = [
        (x_ref[i].astype(jnp.float32) - mean_ref[i : i + 1, :]) * inverse[i : i + 1] for i in range(samples)
    ]
    grads = [grad_act[i * positions : (i + 1) * positions] * silu_grad(normed[i]) for i in range(samples)]
    means = table_sums(
        packs,
        jnp.concatenate(
            [position_sums(grads), position_sums([g * n for g, n in zip(grads, normed)])], axis=0
        ),
        same_group_ref[...],
    ) / entries
    for i in range(samples):
        first, second = means[i : i + 1], means[samples + i : samples + i + 1]
        made_ref[i] = (inverse[i : i + 1] * (grads[i] - first - normed[i] * second)).astype(jnp.bfloat16)
        copies.append(pltpu.make_async_copy(made_ref.at[i], out_ref.at[i], sems.at[len(copies)]))
        copies[-1].start()
    for copy in copies[-samples:]:
        copy.wait()


def adam_step(shards, pack, scales_ref, own_ref, other_refs, blocks, grad_ref, moved_ref):
    rows = pack.rows
    total = own_ref[...]
    for other_ref in other_refs:
        total = total + pack.read(other_ref)
    grad_ref[...] = total / shards
    grad = grad_ref[:rows, :]
    params, first, second = blocks()
    first_new = BETA_ONE * first + (1.0 - BETA_ONE) * grad
    second_new = BETA_TWO * second + (1.0 - BETA_TWO) * grad * grad
    update = (scales_ref[0] * first_new) / (jnp.sqrt(second_new * scales_ref[1]) + ADAM_EPS)
    moved_ref[rows // 8 * 8 :, :] = jnp.zeros((pack.deep - rows // 8 * 8, pack.columns), jnp.float32)
    moved_ref[:rows, :] = params - update


def fetch(hbm_refs, row_refs, sems):
    copies = [
        pltpu.make_async_copy(source, target, sems.at[i])
        for i, (source, target) in enumerate(zip(hbm_refs, row_refs))
    ]
    for copy in copies:
        copy.start()
    return copies


def first_adam_kernel(shards, pack, scales_ref, push_ref, own_ref, *refs):
    other_refs, refs = refs[: shards - 1], refs[shards - 1 :]
    hbm_refs, token_ref, (grad_ref, moved_ref, sent_ref) = refs[:3], refs[3], refs[4:7]
    row_refs, sems = refs[7:10], refs[10]
    copies = fetch(hbm_refs, row_refs, sems)

    def blocks():
        for copy in copies:
            copy.wait()
        return [row_ref[:, 0, pack.start : pack.stop] for row_ref in row_refs]

    adam_step(shards, pack, scales_ref, own_ref, other_refs, blocks, grad_ref, moved_ref)
    moved = moved_ref[...]
    spare = lax.broadcasted_iota(jnp.int32, moved.shape, 0) == pack.rows
    pack.write(sent_ref, jnp.where(spare, push_ref[0], moved))


def cut_kernel(pack, *refs):
    hbm_refs, out_refs, row_refs, sems = refs[:3], refs[3:6], refs[6:9], refs[9]
    for copy, row_ref, out_ref in zip(fetch(hbm_refs, row_refs, sems), row_refs, out_refs):
        copy.wait()
        out_ref[...] = row_ref[:, 0, pack.start : pack.stop]


def second_adam_kernel(shards, pack, scales_ref, own_ref, *refs):
    other_refs, refs = refs[: shards - 1], refs[shards - 1 :]
    block_refs, token_ref, (grad_ref, moved_ref, sent_ref) = refs[:3], refs[3], refs[4:]
    adam_step(
        shards, pack, scales_ref, own_ref, other_refs, lambda: [ref[...] for ref in block_refs], grad_ref, moved_ref
    )
    pack.write(sent_ref, moved_ref[...])


def half_average_kernel(pack, push_ref, moved_ref, other_ref, mean_ref, push_out_ref):
    other = pack.read(other_ref)
    mean_ref[...] = 0.5 * (moved_ref[...] + other)
    place = other[pack.rows : pack.rows + 1, :LANES]
    first = lax.broadcasted_iota(jnp.int32, place.shape, 1) == 0
    push_out_ref[0] = 0.5 * (push_ref[0] + jnp.sum(jnp.where(first, place, 0.0)))


def moments_kernel(packs, first_ref, second_ref, *refs):
    grad_refs, (first_out, second_out) = refs[: len(packs)], refs[len(packs) :]
    rows = first_ref.shape[0]
    grad = jnp.concatenate([grad_ref[:rows, :] for grad_ref in grad_refs], axis=1)
    first_out[:, 0, :] = BETA_ONE * first_ref[:, 0, :] + (1.0 - BETA_ONE) * grad
    second_out[:, 0, :] = BETA_TWO * second_ref[:, 0, :] + (1.0 - BETA_TWO) * grad * grad


def average_kernel(pack, mean_ref, moved_ref, other_ref, out_ref, rows_ref, sem):
    rows = out_ref.shape[0]
    later = 0.5 * (moved_ref[...] + pack.read(other_ref))
    rows_ref[:, 0, :] = jnp.concatenate([mean_ref[...], later], axis=1)[:rows]
    copy = pltpu.make_async_copy(rows_ref, out_ref, sem)
    copy.start()
    copy.wait()


SCALARS = pl.BlockSpec(memory_space=pltpu.SMEM)
BLOCKS = pl.BlockSpec(memory_space=pltpu.VMEM)
TOKEN = pl.BlockSpec(memory_space=pl.ANY)
IN_HBM = pl.BlockSpec(memory_space=pltpu.HBM)


def call(kernel, name, outs, specs, operands, scratch=(), out_specs=None, flops=0, elements=0):
    return pl.pallas_call(
        kernel,
        out_shape=outs,
        in_specs=specs,
        out_specs=out_specs or jax.tree.map(lambda _: BLOCKS, outs),
        scratch_shapes=list(scratch),
        compiler_params=pltpu.CompilerParams(vmem_limit_bytes=VMEM_BYTES),
        cost_estimate=pl.CostEstimate(flops=flops, bytes_accessed=8 * elements, transcendentals=elements),
        name=name,
    )(*operands)


def stay(array):
    return pltpu.with_memory_space_constraint(array, pltpu.HBM)


def moved_on(block, axis, distance):
    size = lax.axis_size(axis)
    return lax.ppermute(block, axis, [(i, (i + distance) % size) for i in range(size)])


def column_cuts(channels):
    half = (channels // GSIZE + 1) // 2 * GSIZE
    return [(0, half), (half, channels)]


def local(
    block_input, time_shift, out_grad, params, first_moment, second_moment, push_weight, step
):
    samples, positions, channels = block_input.shape
    tokens = samples * positions
    shards = lax.axis_size("dp")
    rows = params.shape[1]
    deep = packed_rows(rows)
    me = lax.axis_index("dp").astype(jnp.int32).reshape(1)
    packs = [Packing(rows, start, stop) for start, stop in column_cuts(channels)]
    params, first_moment, second_moment = (
        jnp.transpose(array, (1, 0, 2)) for array in (params, first_moment, second_moment)
    )
    shard_list = call(
        functools.partial(cast_kernel, packs),
        "cast",
        tuple(pack.payload() for pack in packs),
        [SCALARS, BLOCKS],
        (push_weight, params),
        scratch=[pltpu.VMEM((deep, channels), jnp.float32)],
        elements=rows * channels,
    )
    weights = [
        [piece] + [moved_on(piece, "dp", -slot) for slot in range(1, shards)] for piece in shard_list
    ]

    level_count = lax.axis_size("replica").bit_length() - 1
    distance_bits = step[0] % level_count
    step_count = (step[0] + 1).astype(jnp.float32)
    scales = jnp.stack(
        [LEARN_RATE / (1.0 - jnp.power(BETA_ONE, step_count)), 1.0 / (1.0 - jnp.power(BETA_TWO, step_count))]
    )

    activation, mean_in, inverse_in, same_group, *pieces = call(
        functools.partial(norm_in_kernel, shards, packs),
        "norm_in",
        (
            jax.ShapeDtypeStruct((shards * deep, tokens), jnp.bfloat16),
            jax.ShapeDtypeStruct((samples, channels), jnp.float32),
            jax.ShapeDtypeStruct((samples, channels), jnp.float32),
            jax.ShapeDtypeStruct((max(pack.columns for pack in packs),) * 2, jnp.bfloat16),
            *(jax.ShapeDtypeStruct((samples, pack.columns), jnp.float32) for pack in packs),
            *(jax.ShapeDtypeStruct((samples, positions, pack.columns), jnp.bfloat16) for pack in packs),
        ),
        [SCALARS, SCALARS, BLOCKS, IN_HBM, IN_HBM],
        (me, scales, time_shift, stay(block_input), stay(out_grad)),
        scratch=[
            pltpu.VMEM(block_input.shape, jnp.bfloat16),
            pltpu.VMEM(out_grad.shape, jnp.bfloat16),
            pltpu.SemaphoreType.DMA((2,)),
        ],
        elements=tokens * channels,
    )

    hidden_grads, full_weights, owns, arrived = [], [], [], []
    token = mean_in
    shifts, out_grads = pieces[: len(packs)], pieces[len(packs) :]
    for pack, shard_list, shift, out_grad_piece in zip(packs, weights, shifts, out_grads):
        grad_hidden, full_weight, own, *sends = call(
            functools.partial(mix_kernel, shards, pack),
            "mix",
            (
                pltpu.HBM((tokens, pack.columns), jnp.bfloat16),
                pltpu.HBM((shards * deep, pack.columns), jnp.bfloat16),
                pack.block(),
            )
            + (pack.payload(),) * (shards - 1),
            [BLOCKS] * (4 + shards) + [TOKEN],
            (activation, shift, out_grad_piece, same_group, *shard_list, token),
            scratch=[
                pltpu.VMEM((shards * deep, pack.columns), jnp.bfloat16),
                pltpu.VMEM((tokens, pack.columns), jnp.bfloat16),
                pltpu.SemaphoreType.DMA((2,)),
            ],
            out_specs=(IN_HBM,) * 2 + (BLOCKS,) * shards,
            flops=4 * tokens * channels * pack.columns,
            elements=tokens * pack.columns,
        )
        token = own
        hidden_grads.append(grad_hidden)
        full_weights.append(full_weight)
        owns.append(own)
        arrived.append([moved_on(send, "dp", slot) for slot, send in enumerate(sends, 1)])

    def input_grad(*operands):
        return call(
            functools.partial(input_grad_kernel, shards, packs),
            "input_grad",
            pltpu.HBM(block_input.shape, jnp.bfloat16),
            [SCALARS] + [BLOCKS] * 3 + [IN_HBM] * (1 + 2 * len(packs)),
            operands[:4] + tuple(map(stay, operands[4:])),
            scratch=[
                pltpu.VMEM((channels, max(pack.columns for pack in packs)), jnp.float32),
                pltpu.VMEM(block_input.shape, jnp.bfloat16),
                pltpu.VMEM(block_input.shape, jnp.bfloat16),
                pltpu.SemaphoreType.DMA((1 + 2 * len(packs) + samples,)),
                *(pltpu.VMEM((tokens, pack.columns), jnp.bfloat16) for pack in packs),
                *(pltpu.VMEM((shards * deep, pack.columns), jnp.bfloat16) for pack in packs),
            ],
            out_specs=IN_HBM,
            flops=2 * tokens * channels * channels,
            elements=tokens * channels,
        )

    def moments(*grads):
        return call(
            functools.partial(moments_kernel, packs),
            "moments",
            (jax.ShapeDtypeStruct(params.shape, jnp.float32),) * 2,
            [BLOCKS] * (2 + len(packs)),
            (first_moment, second_moment, *grads),
            elements=rows * channels,
        )

    def from_behind(finish, *operands):
        def branch(distance):
            return lambda *values: finish(lambda block: moved_on(block, "replica", distance), *values)

        return lax.switch(distance_bits, [branch(1 << power) for power in range(level_count)], *operands)

    early, late = packs
    arrays = [stay(params), stay(first_moment), stay(second_moment)]
    array_scratch = [pltpu.VMEM(params.shape, jnp.float32)] * 3 + [pltpu.SemaphoreType.DMA((3,))]
    grad_a, moved_a, sent_a = call(
        functools.partial(first_adam_kernel, shards, early),
        "adam",
        (early.block(), early.block(), early.payload()),
        [SCALARS] * 2 + [BLOCKS] * shards + [IN_HBM] * 3 + [TOKEN],
        (scales, push_weight, owns[0], *arrived[0], *arrays, token),
        scratch=array_scratch,
        elements=rows * early.columns,
    )

    def finish_early(move, sent, moved, params, first_moment, second_moment, *operands):
        other = move(sent)
        grad_input = input_grad(*operands)
        blocks = call(
            functools.partial(cut_kernel, late),
            "cut",
            (jax.ShapeDtypeStruct((rows, late.columns), jnp.float32),) * 3,
            [IN_HBM] * 3,
            (stay(params), stay(first_moment), stay(second_moment)),
            scratch=array_scratch,
            elements=rows * late.columns,
        )
        mean, weight = call(
            functools.partial(half_average_kernel, early),
            "half_average",
            (early.block(), jax.ShapeDtypeStruct((1,), jnp.float32)),
            [SCALARS] + [BLOCKS] * 2,
            (push_weight, moved, other),
            out_specs=(BLOCKS, SCALARS),
            elements=rows * early.columns,
        )
        return (grad_input, mean, weight, *blocks)

    grad_input, mean_a, new_weight, *late_blocks = from_behind(
        finish_early,
        sent_a,
        moved_a,
        params,
        first_moment,
        second_moment,
        me,
        mean_in,
        inverse_in,
        same_group,
        block_input,
        *hidden_grads,
        *full_weights,
    )
    grad_b, moved_b, sent_b = call(
        functools.partial(second_adam_kernel, shards, late),
        "adam",
        (late.block(), late.block(), late.payload()),
        [SCALARS] + [BLOCKS] * (3 + shards) + [TOKEN],
        (scales, owns[1], *arrived[1], *late_blocks, mean_a),
        elements=rows * late.columns,
    )

    def finish_late(move, sent, grad_a, grad_b, mean_a, moved_b):
        other = move(sent)
        averaged = call(
            functools.partial(average_kernel, late),
            "average",
            pltpu.HBM(params.shape, jnp.float32),
            [BLOCKS] * 3,
            (mean_a, moved_b, other),
            scratch=[pltpu.VMEM(params.shape, jnp.float32), pltpu.SemaphoreType.DMA],
            out_specs=IN_HBM,
            elements=rows * channels,
        )
        return (*moments(grad_a, grad_b), averaged)

    first_new, second_new, averaged = from_behind(finish_late, sent_b, grad_a, grad_b, mean_a, moved_b)
    return (
        grad_input,
        *(jnp.transpose(array, (1, 0, 2)) for array in (averaged, first_new, second_new)),
        new_weight,
    )


def solution(mesh):
    placed = (
        P(("replica", "dp"), None, None),
        P(("replica", "dp"), None),
        P(("replica", "dp"), None, None),
        P("replica", "dp", None),
        P("replica", "dp", None),
        P("replica", "dp", None),
        P("replica"),
        P(),
    )
    return jax.shard_map(
        local,
        mesh=mesh,
        in_specs=placed,
        out_specs=(
            P(("replica", "dp"), None, None),
            P("replica", "dp", None),
            P("replica", "dp", None),
            P("replica", "dp", None),
            P("replica"),
        ),
        check_vma=False,
    )
```

```python
import functools

import jax
import jax.numpy as jnp
from jax import lax
from jax.experimental import pallas as pl
from jax.experimental.pallas import tpu as pltpu
from jax.sharding import PartitionSpec as P

GSIZE = 40

NORM_EPS = 1e-05
BETA_ONE = 0.9
BETA_TWO = 0.999
LEARN_RATE = 0.002
ADAM_EPS = 1e-08

LANES = 128
TILE_ROWS = 16
VMEM_BYTES = 16 * 1024 * 1024


def padded(rows):
    return -(-rows // TILE_ROWS) * TILE_ROWS


def packed_rows(rows):
    return padded(rows + 1)


class Packing:
    def __init__(self, rows, start, stop):
        self.rows, self.start, self.stop = rows, start, stop
        self.columns = stop - start
        self.deep = packed_rows(rows)
        self.tiles, self.rest = divmod(self.columns, LANES)
        fold = LANES // self.rest if self.rest else 1
        self.fold_rows = padded(-(-self.deep // fold))
        self.folds = [
            (first, min(self.fold_rows, self.deep - first)) for first in range(0, self.deep, self.fold_rows)
        ]
        self.height = self.tiles * self.deep + (self.fold_rows if self.rest else 0)

    def write(self, ref, block):
        for tile in range(self.tiles):
            ref[tile * self.deep : (tile + 1) * self.deep, :] = block[
                :, tile * LANES : (tile + 1) * LANES
            ].astype(ref.dtype)
        if self.rest:
            left = block[:, self.tiles * LANES :]
            parts = []
            for first, count in self.folds:
                part = left[first : first + count]
                if count < self.fold_rows:
                    part = jnp.concatenate(
                        [part, jnp.zeros((self.fold_rows - count, self.rest), part.dtype)], axis=0
                    )
                parts.append(part)
            spare = LANES - self.rest * len(parts)
            if spare:
                parts.append(jnp.zeros((self.fold_rows, spare), left.dtype))
            ref[self.tiles * self.deep :, :] = jnp.concatenate(parts, axis=1).astype(ref.dtype)

    def read(self, ref):
        pieces = [
            ref[tile * self.deep : (tile + 1) * self.deep, :].astype(jnp.float32) for tile in range(self.tiles)
        ]
        if self.rest:
            left = ref[self.tiles * self.deep :, :].astype(jnp.float32)
            parts = [
                left[:count, i * self.rest : (i + 1) * self.rest] for i, (_, count) in enumerate(self.folds)
            ]
            pieces.append(jnp.concatenate(parts, axis=0) if len(parts) > 1 else parts[0])
        return jnp.concatenate(pieces, axis=1) if len(pieces) > 1 else pieces[0]

    def unpack(self, ref, out_ref, first_row):
        for tile in range(self.tiles):
            out_ref[first_row : first_row + self.deep, tile * LANES : (tile + 1) * LANES] = ref[
                tile * self.deep : (tile + 1) * self.deep, :
            ]
        if self.rest:
            left = ref[self.tiles * self.deep :, :]
            for i, (first, count) in enumerate(self.folds):
                out_ref[first_row + first : first_row + first + count, self.tiles * LANES :] = left[
                    :count, i * self.rest : (i + 1) * self.rest
                ]

    def payload(self):
        return jax.ShapeDtypeStruct((self.height, LANES), jnp.bfloat16)

    def block(self):
        return jax.ShapeDtypeStruct((self.deep, self.columns), jnp.float32)


def group_sums(rows, same_group):
    high = rows.astype(jnp.bfloat16).astype(jnp.float32)
    rest = rows - high
    middle = rest.astype(jnp.bfloat16).astype(jnp.float32)
    count = rows.shape[0]
    stacked = jnp.concatenate([high, middle, rest - middle], axis=0).astype(jnp.bfloat16)
    sums = jnp.dot(stacked, same_group, preferred_element_type=jnp.float32)
    return sums[:count] + (sums[count : 2 * count] + sums[2 * count :])


def table_sums(packs, rows, same_group):
    return jnp.concatenate(
        [
            group_sums(rows[:, pack.start : pack.stop], same_group[: pack.columns, : pack.columns])
            for pack in packs
        ],
        axis=1,
    )


def position_sums(parts):
    return jnp.concatenate([jnp.sum(part, axis=0, keepdims=True) for part in parts], axis=0)


def sigmoid(values):
    return 0.5 * jnp.tanh(0.5 * values) + 0.5


def silu_grad(values):
    gate = sigmoid(values)
    return gate * (1.0 + values * (1.0 - gate))


def cast_kernel(packs, push_ref, params_ref, *refs):
    out_refs, rows_ref = refs[:-1], refs[-1]
    rows = params_ref.shape[0]
    rows_ref[rows // 8 * 8 :, :] = jnp.zeros((rows_ref.shape[0] - rows // 8 * 8, rows_ref.shape[1]), jnp.float32)
    rows_ref[:rows, :] = params_ref[:, 0, :] / push_ref[0]
    for pack, out_ref in zip(packs, out_refs):
        pack.write(out_ref, rows_ref[:, pack.start : pack.stop])


def norm_in_kernel(shards, packs, me_ref, scales_ref, shift_ref, x_hbm, out_grad_hbm, *refs):
    act_ref, mean_ref, inverse_ref, same_group_ref = refs[:4]
    shift_refs, out_grad_refs = refs[4 : 4 + len(packs)], refs[4 + len(packs) : 4 + 2 * len(packs)]
    x_ref, out_grad_ref, sems = refs[4 + 2 * len(packs) :]
    copies = [
        pltpu.make_async_copy(x_hbm, x_ref, sems.at[0]),
        pltpu.make_async_copy(out_grad_hbm, out_grad_ref, sems.at[1]),
    ]
    for copy in copies:
        copy.start()
    samples, positions, channels = x_ref.shape
    rows = channels // shards
    deep = act_ref.shape[0] // shards
    entries = positions * GSIZE
    group_of_row = lax.broadcasted_iota(jnp.int32, same_group_ref.shape, 0) // GSIZE
    group_of_column = lax.broadcasted_iota(jnp.int32, same_group_ref.shape, 1) // GSIZE
    same_group_ref[...] = (group_of_row == group_of_column).astype(jnp.float32).astype(jnp.bfloat16)
    same_group = same_group_ref[...]
    for pack, shift_out in zip(packs, shift_refs):
        shift_out[...] = shift_ref[...].astype(jnp.float32)[:, pack.start : pack.stop]
    copies[0].wait()
    parts = [x_ref[i].astype(jnp.float32) for i in range(samples)]
    mean = table_sums(packs, position_sums(parts), same_group) / entries
    centered = [parts[i] - mean[i : i + 1] for i in range(samples)]
    variance = table_sums(packs, position_sums([part * part for part in centered]), same_group) / entries
    inverse = lax.rsqrt(variance + NORM_EPS)
    mean_ref[...] = mean
    inverse_ref[...] = inverse
    normed = [centered[i] * inverse[i : i + 1] for i in range(samples)]
    act = jnp.concatenate([part * sigmoid(part) for part in normed], axis=0).T
    for block in range(shards):
        slot = jnp.bitwise_xor(me_ref[0], block)
        act_ref[pl.ds(pl.multiple_of(slot * deep, TILE_ROWS), deep), :] = jnp.concatenate(
            [act[block * rows : (block + 1) * rows], jnp.zeros((deep - rows, act.shape[1]), jnp.float32)], axis=0
        ).astype(jnp.bfloat16)
    copies[1].wait()
    for pack, out_grad_out in zip(packs, out_grad_refs):
        for i in range(samples):
            out_grad_out[i] = out_grad_ref[i][:, pack.start : pack.stop]


def mix_kernel(shards, pack, act_ref, shift_ref, out_grad_ref, same_group_ref, *refs):
    weight_refs, token_ref, refs = refs[:shards], refs[shards], refs[shards + 1 :]
    grad_hidden_ref, weight_out_ref, own_ref = refs[:3]
    send_refs, (weight_ref, kept_ref, sems) = refs[3 : 2 + shards], refs[2 + shards :]
    samples, positions, columns = out_grad_ref.shape
    entries = positions * GSIZE
    deep = pack.deep
    for slot, shard_ref in enumerate(weight_refs):
        pack.unpack(shard_ref, weight_ref, slot * deep)
    weight_copy = pltpu.make_async_copy(weight_ref, weight_out_ref, sems.at[0])
    weight_copy.start()
    same_group = same_group_ref[:columns, :columns]
    hidden = lax.dot_general(
        act_ref[...], weight_ref[...], (((0,), (0,)), ((), ())), preferred_element_type=jnp.float32
    )
    parts = [
        hidden[i * positions : (i + 1) * positions] + shift_ref[i : i + 1, :]
        for i in range(samples)
    ]
    mean = group_sums(position_sums(parts), same_group) / entries
    parts = [parts[i] - mean[i : i + 1] for i in range(samples)]
    variance = group_sums(position_sums([part * part for part in parts]), same_group) / entries
    inverse = lax.rsqrt(variance + NORM_EPS)
    normed = [parts[i] * inverse[i : i + 1] for i in range(samples)]
    grads = [out_grad_ref[i].astype(jnp.float32) * silu_grad(normed[i]) for i in range(samples)]
    means = group_sums(
        jnp.concatenate(
            [position_sums(grads), position_sums([g * n for g, n in zip(grads, normed)])], axis=0
        ),
        same_group,
    ) / entries
    for i in range(samples):
        first, second = means[i : i + 1], means[samples + i : samples + i + 1]
        kept_ref[i * positions : (i + 1) * positions, :] = (
            inverse[i : i + 1] * (grads[i] - first - normed[i] * second)
        ).astype(jnp.bfloat16)
    copy = pltpu.make_async_copy(kept_ref, grad_hidden_ref, sems.at[1])
    copy.start()
    grad = jnp.dot(act_ref[...], kept_ref[...], preferred_element_type=jnp.float32)
    for slot, send_ref in enumerate(send_refs, 1):
        pack.write(send_ref, grad[slot * deep : (slot + 1) * deep])
    own_ref[...] = grad[:deep]
    weight_copy.wait()
    copy.wait()


def input_grad_kernel(shards, packs, me_ref, mean_ref, inverse_ref, same_group_ref, x_hbm, *refs):
    count = len(packs)
    grad_hbms, weight_hbms, out_ref = refs[:count], refs[count : 2 * count], refs[2 * count]
    rows_ref, x_ref, made_ref, sems = refs[2 * count + 1 : 2 * count + 5]
    grad_refs, weight_refs = refs[2 * count + 5 : 3 * count + 5], refs[3 * count + 5 :]
    copies = [
        pltpu.make_async_copy(source, target, sems.at[i])
        for i, (source, target) in enumerate(
            zip((*weight_hbms, *grad_hbms, x_hbm), (*weight_refs, *grad_refs, x_ref))
        )
    ]
    for copy in copies:
        copy.start()
    samples, positions, channels = x_ref.shape
    entries = positions * GSIZE
    rows = channels // shards
    weights = []
    for index, (pack, weight_ref) in enumerate(zip(packs, weight_refs)):
        copies[index].wait()
        for block in range(shards):
            slot = jnp.bitwise_xor(me_ref[0], block)
            rows_ref[block * rows : (block + 1) * rows, : pack.columns] = weight_ref[
                pl.ds(pl.multiple_of(slot * pack.deep, TILE_ROWS), pack.deep), :
            ].astype(jnp.float32)[:rows]
        weights.append(rows_ref[:, : pack.columns].astype(jnp.bfloat16))
    grad_act = 0.0
    for index, (grad_ref, weight) in enumerate(zip(grad_refs, weights)):
        copies[count + index].wait()
        grad_act += lax.dot_general(
            grad_ref[...], weight, (((1,), (1,)), ((), ())), preferred_element_type=jnp.float32
        )
    copies[-1].wait()
    inverse = inverse_ref[...]
    normed = [
        (x_ref[i].astype(jnp.float32) - mean_ref[i : i + 1, :]) * inverse[i : i + 1] for i in range(samples)
    ]
    grads = [grad_act[i * positions : (i + 1) * positions] * silu_grad(normed[i]) for i in range(samples)]
    means = table_sums(
        packs,
        jnp.concatenate(
            [position_sums(grads), position_sums([g * n for g, n in zip(grads, normed)])], axis=0
        ),
        same_group_ref[...],
    ) / entries
    for i in range(samples):
        first, second = means[i : i + 1], means[samples + i : samples + i + 1]
        made_ref[i] = (inverse[i : i + 1] * (grads[i] - first - normed[i] * second)).astype(jnp.bfloat16)
        copies.append(pltpu.make_async_copy(made_ref.at[i], out_ref.at[i], sems.at[len(copies)]))
        copies[-1].start()
    for copy in copies[-samples:]:
        copy.wait()


def adam_step(shards, pack, scales_ref, own_ref, other_refs, blocks, grad_ref, moved_ref):
    rows = pack.rows
    total = own_ref[...]
    for other_ref in other_refs:
        total = total + pack.read(other_ref)
    grad_ref[...] = total / shards
    grad = grad_ref[:rows, :]
    params, first, second = blocks()
    first_new = BETA_ONE * first + (1.0 - BETA_ONE) * grad
    second_new = BETA_TWO * second + (1.0 - BETA_TWO) * grad * grad
    update = (scales_ref[0] * first_new) / (jnp.sqrt(second_new * scales_ref[1]) + ADAM_EPS)
    moved_ref[rows // 8 * 8 :, :] = jnp.zeros((pack.deep - rows // 8 * 8, pack.columns), jnp.float32)
    moved_ref[:rows, :] = params - update


def merge_kernel(one_ref, other_ref, out_ref):
    out_ref[...] = (one_ref[...].astype(jnp.float32) + other_ref[...].astype(jnp.float32)).astype(out_ref.dtype)


def fetch(hbm_refs, row_refs, sems):
    copies = [
        pltpu.make_async_copy(source, target, sems.at[i])
        for i, (source, target) in enumerate(zip(hbm_refs, row_refs))
    ]
    for copy in copies:
        copy.start()
    return copies


def first_adam_kernel(shards, count, pack, scales_ref, push_ref, own_ref, *refs):
    other_refs, refs = refs[:count], refs[count:]
    hbm_refs, token_ref, (grad_ref, moved_ref, sent_ref) = refs[:3], refs[3], refs[4:7]
    row_refs, sems = refs[7:10], refs[10]
    copies = fetch(hbm_refs, row_refs, sems)

    def blocks():
        for copy in copies:
            copy.wait()
        return [row_ref[:, 0, pack.start : pack.stop] for row_ref in row_refs]

    adam_step(shards, pack, scales_ref, own_ref, other_refs, blocks, grad_ref, moved_ref)
    moved = moved_ref[...]
    spare = lax.broadcasted_iota(jnp.int32, moved.shape, 0) == pack.rows
    pack.write(sent_ref, jnp.where(spare, push_ref[0], moved))


def cut_kernel(pack, *refs):
    hbm_refs, out_refs, row_refs, sems = refs[:3], refs[4:7], refs[7:10], refs[10]
    for copy, row_ref, out_ref in zip(fetch(hbm_refs, row_refs, sems), row_refs, out_refs):
        copy.wait()
        out_ref[...] = row_ref[:, 0, pack.start : pack.stop]


def second_adam_kernel(shards, count, pack, scales_ref, own_ref, *refs):
    other_refs, refs = refs[:count], refs[count:]
    block_refs, (grad_ref, moved_ref, sent_ref) = refs[:3], refs[3:]
    adam_step(
        shards, pack, scales_ref, own_ref, other_refs, lambda: [ref[...] for ref in block_refs], grad_ref, moved_ref
    )
    pack.write(sent_ref, moved_ref[...])


def half_average_kernel(pack, push_ref, moved_ref, other_ref, mean_ref, push_out_ref):
    other = pack.read(other_ref)
    mean_ref[...] = 0.5 * (moved_ref[...] + other)
    place = other[pack.rows : pack.rows + 1, :LANES]
    first = lax.broadcasted_iota(jnp.int32, place.shape, 1) == 0
    push_out_ref[0] = 0.5 * (push_ref[0] + jnp.sum(jnp.where(first, place, 0.0)))


def moments_kernel(packs, first_ref, second_ref, *refs):
    grad_refs, (first_out, second_out) = refs[: len(packs)], refs[len(packs) :]
    rows = first_ref.shape[0]
    grad = jnp.concatenate([grad_ref[:rows, :] for grad_ref in grad_refs], axis=1)
    first_out[:, 0, :] = BETA_ONE * first_ref[:, 0, :] + (1.0 - BETA_ONE) * grad
    second_out[:, 0, :] = BETA_TWO * second_ref[:, 0, :] + (1.0 - BETA_TWO) * grad * grad


def average_kernel(pack, mean_ref, moved_ref, other_ref, out_ref, rows_ref, sem):
    rows = out_ref.shape[0]
    later = 0.5 * (moved_ref[...] + pack.read(other_ref))
    rows_ref[:, 0, :] = jnp.concatenate([mean_ref[...], later], axis=1)[:rows]
    copy = pltpu.make_async_copy(rows_ref, out_ref, sem)
    copy.start()
    copy.wait()


SCALARS = pl.BlockSpec(memory_space=pltpu.SMEM)
BLOCKS = pl.BlockSpec(memory_space=pltpu.VMEM)
TOKEN = pl.BlockSpec(memory_space=pl.ANY)
IN_HBM = pl.BlockSpec(memory_space=pltpu.HBM)


def call(kernel, name, outs, specs, operands, scratch=(), out_specs=None, flops=0, elements=0):
    return pl.pallas_call(
        kernel,
        out_shape=outs,
        in_specs=specs,
        out_specs=out_specs or jax.tree.map(lambda _: BLOCKS, outs),
        scratch_shapes=list(scratch),
        compiler_params=pltpu.CompilerParams(vmem_limit_bytes=VMEM_BYTES),
        cost_estimate=pl.CostEstimate(flops=flops, bytes_accessed=8 * elements, transcendentals=elements),
        name=name,
    )(*operands)


def stay(array):
    return pltpu.with_memory_space_constraint(array, pltpu.HBM)


def moved_on(block, axis, distance):
    size = lax.axis_size(axis)
    return lax.ppermute(block, axis, [(i, (i + distance) % size) for i in range(size)])


def exchanged(block, axis, bit):
    return lax.ppermute(block, axis, [(i, i ^ bit) for i in range(lax.axis_size(axis))])


def lowest_bit(slot):
    return slot & -slot


def gathered(piece, shards):
    held = [piece]
    for slot in range(1, shards):
        bit = lowest_bit(slot)
        held.append(exchanged(held[slot ^ bit], "dp", bit))
    return held


def scattered(sends, shards):
    held = dict(enumerate(sends, 1))
    arrived = []
    for slot in sorted(held, key=lambda slot: (-slot.bit_count(), slot)):
        bit = lowest_bit(slot)
        other = exchanged(held[slot], "dp", bit)
        if slot == bit:
            arrived.append(other)
        else:
            held[slot ^ bit] = call(
                merge_kernel,
                "merge",
                jax.ShapeDtypeStruct(other.shape, other.dtype),
                [BLOCKS] * 2,
                (held[slot ^ bit], other),
                elements=other.size,
            )
    return arrived


def column_cuts(channels):
    half = (channels // GSIZE + 1) // 2 * GSIZE
    return [(0, half), (half, channels)]


def local(
    block_input, time_shift, out_grad, params, first_moment, second_moment, push_weight, step
):
    samples, positions, channels = block_input.shape
    tokens = samples * positions
    shards = lax.axis_size("dp")
    rows = params.shape[1]
    deep = packed_rows(rows)
    me = lax.axis_index("dp").astype(jnp.int32).reshape(1)
    packs = [Packing(rows, start, stop) for start, stop in column_cuts(channels)]
    params, first_moment, second_moment = (
        jnp.transpose(array, (1, 0, 2)) for array in (params, first_moment, second_moment)
    )
    shard_list = call(
        functools.partial(cast_kernel, packs),
        "cast",
        tuple(pack.payload() for pack in packs),
        [SCALARS, BLOCKS],
        (push_weight, params),
        scratch=[pltpu.VMEM((deep, channels), jnp.float32)],
        elements=rows * channels,
    )
    weights = [gathered(piece, shards) for piece in shard_list]

    level_count = lax.axis_size("replica").bit_length() - 1
    distance_bits = step[0] % level_count
    step_count = (step[0] + 1).astype(jnp.float32)
    scales = jnp.stack(
        [LEARN_RATE / (1.0 - jnp.power(BETA_ONE, step_count)), 1.0 / (1.0 - jnp.power(BETA_TWO, step_count))]
    )

    activation, mean_in, inverse_in, same_group, *pieces = call(
        functools.partial(norm_in_kernel, shards, packs),
        "norm_in",
        (
            jax.ShapeDtypeStruct((shards * deep, tokens), jnp.bfloat16),
            jax.ShapeDtypeStruct((samples, channels), jnp.float32),
            jax.ShapeDtypeStruct((samples, channels), jnp.float32),
            jax.ShapeDtypeStruct((max(pack.columns for pack in packs),) * 2, jnp.bfloat16),
            *(jax.ShapeDtypeStruct((samples, pack.columns), jnp.float32) for pack in packs),
            *(jax.ShapeDtypeStruct((samples, positions, pack.columns), jnp.bfloat16) for pack in packs),
        ),
        [SCALARS, SCALARS, BLOCKS, IN_HBM, IN_HBM],
        (me, scales, time_shift, stay(block_input), stay(out_grad)),
        scratch=[
            pltpu.VMEM(block_input.shape, jnp.bfloat16),
            pltpu.VMEM(out_grad.shape, jnp.bfloat16),
            pltpu.SemaphoreType.DMA((2,)),
        ],
        elements=tokens * channels,
    )

    hidden_grads, full_weights, owns, arrived = [], [], [], []
    token = mean_in
    shifts, out_grads = pieces[: len(packs)], pieces[len(packs) :]
    for pack, shard_list, shift, out_grad_piece in zip(packs, weights, shifts, out_grads):
        grad_hidden, full_weight, own, *sends = call(
            functools.partial(mix_kernel, shards, pack),
            "mix",
            (
                pltpu.HBM((tokens, pack.columns), jnp.bfloat16),
                pltpu.HBM((shards * deep, pack.columns), jnp.bfloat16),
                pack.block(),
            )
            + (pack.payload(),) * (shards - 1),
            [BLOCKS] * (4 + shards) + [TOKEN],
            (activation, shift, out_grad_piece, same_group, *shard_list, token),
            scratch=[
                pltpu.VMEM((shards * deep, pack.columns), jnp.bfloat16),
                pltpu.VMEM((tokens, pack.columns), jnp.bfloat16),
                pltpu.SemaphoreType.DMA((2,)),
            ],
            out_specs=(IN_HBM,) * 2 + (BLOCKS,) * shards,
            flops=4 * tokens * channels * pack.columns,
            elements=tokens * pack.columns,
        )
        token = own
        hidden_grads.append(grad_hidden)
        full_weights.append(full_weight)
        owns.append(own)
        arrived.append(scattered(sends, shards))

    def input_grad(*operands):
        return call(
            functools.partial(input_grad_kernel, shards, packs),
            "input_grad",
            pltpu.HBM(block_input.shape, jnp.bfloat16),
            [SCALARS] + [BLOCKS] * 3 + [IN_HBM] * (1 + 2 * len(packs)),
            operands[:4] + tuple(map(stay, operands[4:])),
            scratch=[
                pltpu.VMEM((channels, max(pack.columns for pack in packs)), jnp.float32),
                pltpu.VMEM(block_input.shape, jnp.bfloat16),
                pltpu.VMEM(block_input.shape, jnp.bfloat16),
                pltpu.SemaphoreType.DMA((1 + 2 * len(packs) + samples,)),
                *(pltpu.VMEM((tokens, pack.columns), jnp.bfloat16) for pack in packs),
                *(pltpu.VMEM((shards * deep, pack.columns), jnp.bfloat16) for pack in packs),
            ],
            out_specs=IN_HBM,
            flops=2 * tokens * channels * channels,
            elements=tokens * channels,
        )

    def moments(*grads):
        return call(
            functools.partial(moments_kernel, packs),
            "moments",
            (jax.ShapeDtypeStruct(params.shape, jnp.float32),) * 2,
            [BLOCKS] * (2 + len(packs)),
            (first_moment, second_moment, *grads),
            elements=rows * channels,
        )

    def from_behind(finish, *operands):
        def branch(distance):
            return lambda *values: finish(lambda block: moved_on(block, "replica", distance), *values)

        return lax.switch(distance_bits, [branch(1 << power) for power in range(level_count)], *operands)

    grad_input = input_grad(
        me, mean_in, inverse_in, same_group, block_input, *hidden_grads, *full_weights
    )
    early, late = packs
    arrays = [stay(params), stay(first_moment), stay(second_moment)]
    array_scratch = [pltpu.VMEM(params.shape, jnp.float32)] * 3 + [pltpu.SemaphoreType.DMA((3,))]
    late_blocks = call(
        functools.partial(cut_kernel, late),
        "cut",
        (jax.ShapeDtypeStruct((rows, late.columns), jnp.float32),) * 3,
        [IN_HBM] * 3 + [TOKEN],
        (*arrays, token),
        scratch=array_scratch,
        elements=rows * late.columns,
    )
    grad_a, moved_a, sent_a = call(
        functools.partial(first_adam_kernel, shards, len(arrived[0]), early),
        "adam",
        (early.block(), early.block(), early.payload()),
        [SCALARS] * 2 + [BLOCKS] * (1 + len(arrived[0])) + [IN_HBM] * 3 + [TOKEN],
        (scales, push_weight, owns[0], *arrived[0], *arrays, token),
        scratch=array_scratch,
        elements=rows * early.columns,
    )

    def finish(move, sent, grad_a, moved_a, own, *operands):
        other_a = move(sent)
        grad_b, moved_b, sent_b = call(
            functools.partial(second_adam_kernel, shards, len(arrived[1]), late),
            "adam",
            (late.block(), late.block(), late.payload()),
            [SCALARS] + [BLOCKS] * (4 + len(arrived[1])),
            (scales, own, *operands),
            elements=rows * late.columns,
        )
        other_b = move(sent_b)
        mean, weight = call(
            functools.partial(half_average_kernel, early),
            "half_average",
            (early.block(), jax.ShapeDtypeStruct((1,), jnp.float32)),
            [SCALARS] + [BLOCKS] * 2,
            (push_weight, moved_a, other_a),
            out_specs=(BLOCKS, SCALARS),
            elements=rows * early.columns,
        )
        averaged = call(
            functools.partial(average_kernel, late),
            "average",
            pltpu.HBM(params.shape, jnp.float32),
            [BLOCKS] * 3,
            (mean, moved_b, other_b),
            scratch=[pltpu.VMEM(params.shape, jnp.float32), pltpu.SemaphoreType.DMA],
            out_specs=IN_HBM,
            elements=rows * channels,
        )
        return (*moments(grad_a, grad_b), averaged, weight)

    first_new, second_new, averaged, new_weight = from_behind(
        finish, sent_a, grad_a, moved_a, owns[1], *arrived[1], *late_blocks
    )
    return (
        grad_input,
        *(jnp.transpose(array, (1, 0, 2)) for array in (averaged, first_new, second_new)),
        new_weight,
    )


def solution(mesh):
    placed = (
        P(("replica", "dp"), None, None),
        P(("replica", "dp"), None),
        P(("replica", "dp"), None, None),
        P("replica", "dp", None),
        P("replica", "dp", None),
        P("replica", "dp", None),
        P("replica"),
        P(),
    )
    return jax.shard_map(
        local,
        mesh=mesh,
        in_specs=placed,
        out_specs=(
            P(("replica", "dp"), None, None),
            P("replica", "dp", None),
            P("replica", "dp", None),
            P("replica", "dp", None),
            P("replica"),
        ),
        check_vma=False,
    )
```

```python
import functools

import jax
import jax.numpy as jnp
from jax import lax
from jax.experimental import pallas as pl
from jax.experimental.pallas import tpu as pltpu
from jax.sharding import PartitionSpec as P

GSIZE = 40

NORM_EPS = 1e-05
BETA_ONE = 0.9
BETA_TWO = 0.999
LEARN_RATE = 0.002
ADAM_EPS = 1e-08

LANES = 128
TILE_ROWS = 16
VMEM_BYTES = 16 * 1024 * 1024


def padded(rows):
    return -(-rows // TILE_ROWS) * TILE_ROWS


def packed_rows(rows):
    return padded(rows + 1)


class Packing:
    def __init__(self, rows, start, stop):
        self.rows, self.start, self.stop = rows, start, stop
        self.columns = stop - start
        self.deep = packed_rows(rows)
        self.tiles, self.rest = divmod(self.columns, LANES)
        fold = LANES // self.rest if self.rest else 1
        self.fold_rows = padded(-(-self.deep // fold))
        self.folds = [
            (first, min(self.fold_rows, self.deep - first)) for first in range(0, self.deep, self.fold_rows)
        ]
        self.height = self.tiles * self.deep + (self.fold_rows if self.rest else 0)

    def write(self, ref, block):
        for tile in range(self.tiles):
            ref[tile * self.deep : (tile + 1) * self.deep, :] = block[
                :, tile * LANES : (tile + 1) * LANES
            ].astype(ref.dtype)
        if self.rest:
            left = block[:, self.tiles * LANES :]
            parts = []
            for first, count in self.folds:
                part = left[first : first + count]
                if count < self.fold_rows:
                    part = jnp.concatenate(
                        [part, jnp.zeros((self.fold_rows - count, self.rest), part.dtype)], axis=0
                    )
                parts.append(part)
            spare = LANES - self.rest * len(parts)
            if spare:
                parts.append(jnp.zeros((self.fold_rows, spare), left.dtype))
            ref[self.tiles * self.deep :, :] = jnp.concatenate(parts, axis=1).astype(ref.dtype)

    def read(self, ref):
        pieces = [
            ref[tile * self.deep : (tile + 1) * self.deep, :].astype(jnp.float32) for tile in range(self.tiles)
        ]
        if self.rest:
            left = ref[self.tiles * self.deep :, :].astype(jnp.float32)
            parts = [
                left[:count, i * self.rest : (i + 1) * self.rest] for i, (_, count) in enumerate(self.folds)
            ]
            pieces.append(jnp.concatenate(parts, axis=0) if len(parts) > 1 else parts[0])
        return jnp.concatenate(pieces, axis=1) if len(pieces) > 1 else pieces[0]

    def unpack(self, ref, out_ref, first_row):
        for tile in range(self.tiles):
            out_ref[first_row : first_row + self.deep, tile * LANES : (tile + 1) * LANES] = ref[
                tile * self.deep : (tile + 1) * self.deep, :
            ]
        if self.rest:
            left = ref[self.tiles * self.deep :, :]
            for i, (first, count) in enumerate(self.folds):
                out_ref[first_row + first : first_row + first + count, self.tiles * LANES :] = left[
                    :count, i * self.rest : (i + 1) * self.rest
                ]

    def payload(self):
        return jax.ShapeDtypeStruct((self.height, LANES), jnp.bfloat16)

    def block(self):
        return jax.ShapeDtypeStruct((self.deep, self.columns), jnp.float32)


def group_sums(rows, same_group):
    high = rows.astype(jnp.bfloat16).astype(jnp.float32)
    rest = rows - high
    middle = rest.astype(jnp.bfloat16).astype(jnp.float32)
    count = rows.shape[0]
    stacked = jnp.concatenate([high, middle, rest - middle], axis=0).astype(jnp.bfloat16)
    sums = jnp.dot(stacked, same_group, preferred_element_type=jnp.float32)
    return sums[:count] + (sums[count : 2 * count] + sums[2 * count :])


def table_sums(packs, rows, same_group):
    return jnp.concatenate(
        [
            group_sums(rows[:, pack.start : pack.stop], same_group[: pack.columns, : pack.columns])
            for pack in packs
        ],
        axis=1,
    )


def position_sums(parts):
    return jnp.concatenate([jnp.sum(part, axis=0, keepdims=True) for part in parts], axis=0)


def sigmoid(values):
    return 0.5 * jnp.tanh(0.5 * values) + 0.5


def silu_grad(values):
    gate = sigmoid(values)
    return gate * (1.0 + values * (1.0 - gate))


def cast_kernel(pack, push_ref, params_ref, token_ref, out_ref, rows_ref):
    rows = pack.rows
    rows_ref[rows // 8 * 8 :, :] = jnp.zeros((pack.deep - rows // 8 * 8, pack.columns), jnp.float32)
    rows_ref[:rows, :] = params_ref[:, 0, pack.start : pack.stop] / push_ref[0]
    pack.write(out_ref, rows_ref[...])


def norm_in_kernel(shards, packs, me_ref, scales_ref, shift_ref, x_hbm, out_grad_hbm, *refs):
    act_ref, mean_ref, inverse_ref, same_group_ref = refs[:4]
    shift_refs, out_grad_refs = refs[4 : 4 + len(packs)], refs[4 + len(packs) : 4 + 2 * len(packs)]
    x_ref, out_grad_ref, sems = refs[4 + 2 * len(packs) :]
    copies = [
        pltpu.make_async_copy(x_hbm, x_ref, sems.at[0]),
        pltpu.make_async_copy(out_grad_hbm, out_grad_ref, sems.at[1]),
    ]
    for copy in copies:
        copy.start()
    samples, positions, channels = x_ref.shape
    rows = channels // shards
    deep = act_ref.shape[0] // shards
    entries = positions * GSIZE
    group_of_row = lax.broadcasted_iota(jnp.int32, same_group_ref.shape, 0) // GSIZE
    group_of_column = lax.broadcasted_iota(jnp.int32, same_group_ref.shape, 1) // GSIZE
    same_group_ref[...] = (group_of_row == group_of_column).astype(jnp.float32).astype(jnp.bfloat16)
    same_group = same_group_ref[...]
    for pack, shift_out in zip(packs, shift_refs):
        shift_out[...] = shift_ref[...].astype(jnp.float32)[:, pack.start : pack.stop]
    copies[0].wait()
    parts = [x_ref[i].astype(jnp.float32) for i in range(samples)]
    mean = table_sums(packs, position_sums(parts), same_group) / entries
    centered = [parts[i] - mean[i : i + 1] for i in range(samples)]
    variance = table_sums(packs, position_sums([part * part for part in centered]), same_group) / entries
    inverse = lax.rsqrt(variance + NORM_EPS)
    mean_ref[...] = mean
    inverse_ref[...] = inverse
    normed = [centered[i] * inverse[i : i + 1] for i in range(samples)]
    act = jnp.concatenate([part * sigmoid(part) for part in normed], axis=0).T
    for block in range(shards):
        slot = jnp.bitwise_xor(me_ref[0], block)
        act_ref[pl.ds(pl.multiple_of(slot * deep, TILE_ROWS), deep), :] = jnp.concatenate(
            [act[block * rows : (block + 1) * rows], jnp.zeros((deep - rows, act.shape[1]), jnp.float32)], axis=0
        ).astype(jnp.bfloat16)
    copies[1].wait()
    for pack, out_grad_out in zip(packs, out_grad_refs):
        for i in range(samples):
            out_grad_out[i] = out_grad_ref[i][:, pack.start : pack.stop]


def mix_kernel(shards, pack, act_ref, shift_ref, out_grad_ref, same_group_ref, *refs):
    weight_refs, token_ref, refs = refs[:shards], refs[shards], refs[shards + 1 :]
    grad_hidden_ref, weight_out_ref, own_ref = refs[:3]
    send_refs, (weight_ref, kept_ref, sems) = refs[3 : 2 + shards], refs[2 + shards :]
    samples, positions, columns = out_grad_ref.shape
    entries = positions * GSIZE
    deep = pack.deep
    for slot, shard_ref in enumerate(weight_refs):
        pack.unpack(shard_ref, weight_ref, slot * deep)
    weight_copy = pltpu.make_async_copy(weight_ref, weight_out_ref, sems.at[0])
    weight_copy.start()
    same_group = same_group_ref[:columns, :columns]
    hidden = lax.dot_general(
        act_ref[...], weight_ref[...], (((0,), (0,)), ((), ())), preferred_element_type=jnp.float32
    )
    parts = [
        hidden[i * positions : (i + 1) * positions] + shift_ref[i : i + 1, :]
        for i in range(samples)
    ]
    mean = group_sums(position_sums(parts), same_group) / entries
    parts = [parts[i] - mean[i : i + 1] for i in range(samples)]
    variance = group_sums(position_sums([part * part for part in parts]), same_group) / entries
    inverse = lax.rsqrt(variance + NORM_EPS)
    normed = [parts[i] * inverse[i : i + 1] for i in range(samples)]
    grads = [out_grad_ref[i].astype(jnp.float32) * silu_grad(normed[i]) for i in range(samples)]
    means = group_sums(
        jnp.concatenate(
            [position_sums(grads), position_sums([g * n for g, n in zip(grads, normed)])], axis=0
        ),
        same_group,
    ) / entries
    for i in range(samples):
        first, second = means[i : i + 1], means[samples + i : samples + i + 1]
        kept_ref[i * positions : (i + 1) * positions, :] = (
            inverse[i : i + 1] * (grads[i] - first - normed[i] * second)
        ).astype(jnp.bfloat16)
    copy = pltpu.make_async_copy(kept_ref, grad_hidden_ref, sems.at[1])
    copy.start()
    grad = jnp.dot(act_ref[...], kept_ref[...], preferred_element_type=jnp.float32)
    for slot, send_ref in enumerate(send_refs, 1):
        pack.write(send_ref, grad[slot * deep : (slot + 1) * deep])
    own_ref[...] = grad[:deep]
    weight_copy.wait()
    copy.wait()


def input_grad_kernel(shards, packs, me_ref, mean_ref, inverse_ref, same_group_ref, x_hbm, *refs):
    count = len(packs)
    grad_hbms, weight_hbms, out_ref = refs[:count], refs[count : 2 * count], refs[2 * count]
    rows_ref, x_ref, made_ref, sems = refs[2 * count + 1 : 2 * count + 5]
    grad_refs, weight_refs = refs[2 * count + 5 : 3 * count + 5], refs[3 * count + 5 :]
    copies = [
        pltpu.make_async_copy(source, target, sems.at[i])
        for i, (source, target) in enumerate(
            zip((*weight_hbms, *grad_hbms, x_hbm), (*weight_refs, *grad_refs, x_ref))
        )
    ]
    for copy in copies:
        copy.start()
    samples, positions, channels = x_ref.shape
    entries = positions * GSIZE
    rows = channels // shards
    weights = []
    for index, (pack, weight_ref) in enumerate(zip(packs, weight_refs)):
        copies[index].wait()
        for block in range(shards):
            slot = jnp.bitwise_xor(me_ref[0], block)
            rows_ref[block * rows : (block + 1) * rows, : pack.columns] = weight_ref[
                pl.ds(pl.multiple_of(slot * pack.deep, TILE_ROWS), pack.deep), :
            ].astype(jnp.float32)[:rows]
        weights.append(rows_ref[:, : pack.columns].astype(jnp.bfloat16))
    grad_act = 0.0
    for index, (grad_ref, weight) in enumerate(zip(grad_refs, weights)):
        copies[count + index].wait()
        grad_act += lax.dot_general(
            grad_ref[...], weight, (((1,), (1,)), ((), ())), preferred_element_type=jnp.float32
        )
    copies[-1].wait()
    inverse = inverse_ref[...]
    normed = [
        (x_ref[i].astype(jnp.float32) - mean_ref[i : i + 1, :]) * inverse[i : i + 1] for i in range(samples)
    ]
    grads = [grad_act[i * positions : (i + 1) * positions] * silu_grad(normed[i]) for i in range(samples)]
    means = table_sums(
        packs,
        jnp.concatenate(
            [position_sums(grads), position_sums([g * n for g, n in zip(grads, normed)])], axis=0
        ),
        same_group_ref[...],
    ) / entries
    for i in range(samples):
        first, second = means[i : i + 1], means[samples + i : samples + i + 1]
        made_ref[i] = (inverse[i : i + 1] * (grads[i] - first - normed[i] * second)).astype(jnp.bfloat16)
        copies.append(pltpu.make_async_copy(made_ref.at[i], out_ref.at[i], sems.at[len(copies)]))
        copies[-1].start()
    for copy in copies[-samples:]:
        copy.wait()


def merge_kernel(one_ref, other_ref, direct_ref, out_ref, direct_out_ref):
    out_ref[...] = (one_ref[...].astype(jnp.float32) + other_ref[...].astype(jnp.float32)).astype(out_ref.dtype)
    direct_out_ref[...] = direct_ref[...]


def cut_kernel(packs, *refs):
    count = 3 * len(packs)
    hbm_refs, out_refs = refs[:3], refs[4 : 4 + count]
    row_refs, block_refs, sems = refs[4 + count : 7 + count], refs[7 + count : -1], refs[-1]
    copies = [
        pltpu.make_async_copy(source, target, sems.at[i])
        for i, (source, target) in enumerate(zip(hbm_refs, row_refs))
    ]
    for copy in copies:
        copy.start()
    out_copies = []
    for i, row_ref in enumerate(row_refs):
        copies[i].wait()
        for index, pack in enumerate(packs):
            place = 3 * index + i
            block_refs[place][...] = row_ref[:, 0, pack.start : pack.stop]
            out_copies.append(pltpu.make_async_copy(block_refs[place], out_refs[place], sems.at[3 + place]))
            out_copies[-1].start()
    for copy in out_copies:
        copy.wait()


def adam_kernel(count, pack, spare_value, scales_ref, push_ref, own_ref, *refs):
    other_refs, refs = refs[:count], refs[count:]
    (params_ref, first_ref, second_ref), (grad_ref, moved_ref, sent_ref) = refs[:3], refs[-3:]
    rows = pack.rows
    total = own_ref[...]
    for other_ref in other_refs:
        total = total + pack.read(other_ref)
    grad_ref[...] = total * scales_ref[2]
    grad = grad_ref[:rows, :]
    first_new = BETA_ONE * first_ref[...] + (1.0 - BETA_ONE) * grad
    second_new = BETA_TWO * second_ref[...] + (1.0 - BETA_TWO) * grad * grad
    update = (scales_ref[0] * first_new) / (jnp.sqrt(second_new * scales_ref[1]) + ADAM_EPS)
    value = push_ref[0] if spare_value else 0.0
    moved_ref[rows // 8 * 8 :, :] = jnp.full((pack.deep - rows // 8 * 8, pack.columns), value, jnp.float32)
    moved_ref[:rows, :] = params_ref[...] - update
    pack.write(sent_ref, moved_ref[...])


def half_average_kernel(pack, push_ref, moved_ref, other_ref, mean_ref, push_out_ref):
    other = pack.read(other_ref)
    mean_ref[...] = 0.5 * (moved_ref[...] + other)
    place = other[pack.rows : pack.rows + 1, :LANES]
    first = lax.broadcasted_iota(jnp.int32, place.shape, 1) == 0
    push_out_ref[0] = 0.5 * (push_ref[0] + jnp.sum(jnp.where(first, place, 0.0)))


def moments_kernel(packs, first_ref, second_ref, *refs):
    grad_refs, (first_out, second_out) = refs[: len(packs)], refs[len(packs) :]
    rows = first_ref.shape[0]
    grad = jnp.concatenate([grad_ref[:rows, :] for grad_ref in grad_refs], axis=1)
    first_out[:, 0, :] = BETA_ONE * first_ref[:, 0, :] + (1.0 - BETA_ONE) * grad
    second_out[:, 0, :] = BETA_TWO * second_ref[:, 0, :] + (1.0 - BETA_TWO) * grad * grad


def average_kernel(pack, mean_ref, moved_ref, other_ref, out_ref, rows_ref, sem):
    rows = out_ref.shape[0]
    later = 0.5 * (moved_ref[...] + pack.read(other_ref))
    rows_ref[:, 0, :] = jnp.concatenate([mean_ref[...], later], axis=1)[:rows]
    copy = pltpu.make_async_copy(rows_ref, out_ref, sem)
    copy.start()
    copy.wait()


SCALARS = pl.BlockSpec(memory_space=pltpu.SMEM)
BLOCKS = pl.BlockSpec(memory_space=pltpu.VMEM)
TOKEN = pl.BlockSpec(memory_space=pl.ANY)
IN_HBM = pl.BlockSpec(memory_space=pltpu.HBM)


def call(kernel, name, outs, specs, operands, scratch=(), out_specs=None, flops=0, elements=0):
    return pl.pallas_call(
        kernel,
        out_shape=outs,
        in_specs=specs,
        out_specs=out_specs or jax.tree.map(lambda _: BLOCKS, outs),
        scratch_shapes=list(scratch),
        compiler_params=pltpu.CompilerParams(vmem_limit_bytes=VMEM_BYTES),
        cost_estimate=pl.CostEstimate(flops=flops, bytes_accessed=8 * elements, transcendentals=elements),
        name=name,
    )(*operands)


def stay(array):
    return pltpu.with_memory_space_constraint(array, pltpu.HBM)


def moved_on(block, axis, distance):
    size = lax.axis_size(axis)
    return lax.ppermute(block, axis, [(i, (i + distance) % size) for i in range(size)])


def exchanged(block, axis, bit):
    return lax.ppermute(block, axis, [(i, i ^ bit) for i in range(lax.axis_size(axis))])


def lowest_bit(slot):
    return slot & -slot


def gathered(piece, shards):
    held = [piece]
    for slot in range(1, shards):
        bit = lowest_bit(slot)
        held.append(exchanged(held[slot ^ bit], "dp", bit))
    return held


def scattered(sends, shards):
    held = dict(enumerate(sends, 1))
    arrived = []
    for slot in sorted(held, key=lambda slot: (-slot.bit_count(), slot)):
        bit = lowest_bit(slot)
        other = exchanged(held[slot], "dp", bit)
        if slot == bit:
            arrived.append(other)
        else:
            shape = jax.ShapeDtypeStruct(other.shape, other.dtype)
            held[slot ^ bit], held[bit] = call(
                merge_kernel, "merge", (shape,) * 2, [BLOCKS] * 3, (held[slot ^ bit], other, held[bit])
            )
    return arrived


def column_cuts(channels):
    half = (channels // GSIZE + 1) // 2 * GSIZE
    return [(0, half), (half, channels)]


def local(
    block_input, time_shift, out_grad, params, first_moment, second_moment, push_weight, step
):
    samples, positions, channels = block_input.shape
    tokens = samples * positions
    shards = lax.axis_size("dp")
    rows = params.shape[1]
    deep = packed_rows(rows)
    me = lax.axis_index("dp").astype(jnp.int32).reshape(1)
    packs = [Packing(rows, start, stop) for start, stop in column_cuts(channels)]
    params, first_moment, second_moment = (
        jnp.transpose(array, (1, 0, 2)) for array in (params, first_moment, second_moment)
    )
    def shards_of(pack, token):
        piece = call(
            functools.partial(cast_kernel, pack),
            "cast",
            pack.payload(),
            [SCALARS, BLOCKS, TOKEN],
            (push_weight, params, token),
            scratch=[pltpu.VMEM((deep, pack.columns), jnp.float32)],
            elements=rows * pack.columns,
        )
        return gathered(piece, shards)

    level_count = lax.axis_size("replica").bit_length() - 1
    distance_bits = step[0] % level_count
    step_count = (step[0] + 1).astype(jnp.float32)
    scales = jnp.stack(
        [
            LEARN_RATE / (1.0 - jnp.power(BETA_ONE, step_count)),
            1.0 / (1.0 - jnp.power(BETA_TWO, step_count)),
            jnp.float32(1.0 / shards),
        ]
    )

    activation, mean_in, inverse_in, same_group, *pieces = call(
        functools.partial(norm_in_kernel, shards, packs),
        "norm_in",
        (
            jax.ShapeDtypeStruct((shards * deep, tokens), jnp.bfloat16),
            jax.ShapeDtypeStruct((samples, channels), jnp.float32),
            jax.ShapeDtypeStruct((samples, channels), jnp.float32),
            jax.ShapeDtypeStruct((max(pack.columns for pack in packs),) * 2, jnp.bfloat16),
            *(jax.ShapeDtypeStruct((samples, pack.columns), jnp.float32) for pack in packs),
            *(jax.ShapeDtypeStruct((samples, positions, pack.columns), jnp.bfloat16) for pack in packs),
        ),
        [SCALARS, SCALARS, BLOCKS, IN_HBM, IN_HBM],
        (me, scales, time_shift, stay(block_input), stay(out_grad)),
        scratch=[
            pltpu.VMEM(block_input.shape, jnp.bfloat16),
            pltpu.VMEM(out_grad.shape, jnp.bfloat16),
            pltpu.SemaphoreType.DMA((2,)),
        ],
        elements=tokens * channels,
    )

    weights = [shards_of(pack, token) for pack, token in zip(packs, (push_weight, mean_in))]
    columns = [pack.columns for pack in packs for _ in range(3)]
    blocks = call(
        functools.partial(cut_kernel, packs),
        "cut",
        tuple(pltpu.HBM((rows, width), jnp.float32) for width in columns),
        [IN_HBM] * 3 + [TOKEN],
        (stay(params), stay(first_moment), stay(second_moment), mean_in),
        scratch=[pltpu.VMEM(params.shape, jnp.float32)] * 3
        + [pltpu.VMEM((rows, width), jnp.float32) for width in columns]
        + [pltpu.SemaphoreType.DMA((3 + len(columns),))],
        out_specs=(IN_HBM,) * len(columns),
        elements=rows * channels,
    )
    hidden_grads, full_weights, owns, arrived = [], [], [], []
    token = blocks[-1]
    shifts, out_grads = pieces[: len(packs)], pieces[len(packs) :]
    for pack, shard_list, shift, out_grad_piece in zip(packs, weights, shifts, out_grads):
        grad_hidden, full_weight, own, *sends = call(
            functools.partial(mix_kernel, shards, pack),
            "mix",
            (
                pltpu.HBM((tokens, pack.columns), jnp.bfloat16),
                pltpu.HBM((shards * deep, pack.columns), jnp.bfloat16),
                pack.block(),
            )
            + (pack.payload(),) * (shards - 1),
            [BLOCKS] * (4 + shards) + [TOKEN],
            (activation, shift, out_grad_piece, same_group, *shard_list, token),
            scratch=[
                pltpu.VMEM((shards * deep, pack.columns), jnp.bfloat16),
                pltpu.VMEM((tokens, pack.columns), jnp.bfloat16),
                pltpu.SemaphoreType.DMA((2,)),
            ],
            out_specs=(IN_HBM,) * 2 + (BLOCKS,) * shards,
            flops=4 * tokens * channels * pack.columns,
            elements=tokens * pack.columns,
        )
        token = own
        hidden_grads.append(grad_hidden)
        full_weights.append(full_weight)
        owns.append(own)
        arrived.append(scattered(sends, shards))

    def input_grad(*operands):
        return call(
            functools.partial(input_grad_kernel, shards, packs),
            "input_grad",
            pltpu.HBM(block_input.shape, jnp.bfloat16),
            [SCALARS] + [BLOCKS] * 3 + [IN_HBM] * (1 + 2 * len(packs)),
            operands[:4] + tuple(map(stay, operands[4:])),
            scratch=[
                pltpu.VMEM((channels, max(pack.columns for pack in packs)), jnp.float32),
                pltpu.VMEM(block_input.shape, jnp.bfloat16),
                pltpu.VMEM(block_input.shape, jnp.bfloat16),
                pltpu.SemaphoreType.DMA((1 + 2 * len(packs) + samples,)),
                *(pltpu.VMEM((tokens, pack.columns), jnp.bfloat16) for pack in packs),
                *(pltpu.VMEM((shards * deep, pack.columns), jnp.bfloat16) for pack in packs),
            ],
            out_specs=IN_HBM,
            flops=2 * tokens * channels * channels,
            elements=tokens * channels,
        )

    def moments(*grads):
        return call(
            functools.partial(moments_kernel, packs),
            "moments",
            (jax.ShapeDtypeStruct(params.shape, jnp.float32),) * 2,
            [BLOCKS] * (2 + len(packs)),
            (first_moment, second_moment, *grads),
            elements=rows * channels,
        )

    def from_behind(finish, *operands):
        def branch(distance):
            return lambda *values: finish(lambda block: moved_on(block, "replica", distance), *values)

        return lax.switch(distance_bits, [branch(1 << power) for power in range(level_count)], *operands)

    grad_input = input_grad(
        me, mean_in, inverse_in, same_group, block_input, *hidden_grads, *full_weights
    )
    early, late = packs

    def adam(pack, own, others, blocks):
        return call(
            functools.partial(adam_kernel, len(others), pack, pack is early),
            "adam",
            (pack.block(), pack.block(), pack.payload()),
            [SCALARS] * 2 + [BLOCKS] * (4 + len(others)),
            (scales, push_weight, own, *others, *blocks),
            elements=rows * pack.columns,
        )

    grad_a, moved_a, sent_a = adam(early, owns[0], arrived[0], blocks[:3])

    def finish(move, sent, grad_a, moved_a, own, *operands):
        other_a = move(sent)
        grad_b, moved_b, sent_b = adam(late, own, operands[:-3], operands[-3:])
        other_b = move(sent_b)
        mean, weight = call(
            functools.partial(half_average_kernel, early),
            "half_average",
            (early.block(), jax.ShapeDtypeStruct((1,), jnp.float32)),
            [SCALARS] + [BLOCKS] * 2,
            (push_weight, moved_a, other_a),
            out_specs=(BLOCKS, SCALARS),
            elements=rows * early.columns,
        )
        averaged = call(
            functools.partial(average_kernel, late),
            "average",
            pltpu.HBM(params.shape, jnp.float32),
            [BLOCKS] * 3,
            (mean, moved_b, other_b),
            scratch=[pltpu.VMEM(params.shape, jnp.float32), pltpu.SemaphoreType.DMA],
            out_specs=IN_HBM,
            elements=rows * channels,
        )
        return (*moments(grad_a, grad_b), averaged, weight)

    first_new, second_new, averaged, new_weight = from_behind(
        finish, sent_a, grad_a, moved_a, owns[1], *arrived[1], *blocks[3:]
    )
    return (
        grad_input,
        *(jnp.transpose(array, (1, 0, 2)) for array in (averaged, first_new, second_new)),
        new_weight,
    )


def solution(mesh):
    placed = (
        P(("replica", "dp"), None, None),
        P(("replica", "dp"), None),
        P(("replica", "dp"), None, None),
        P("replica", "dp", None),
        P("replica", "dp", None),
        P("replica", "dp", None),
        P("replica"),
        P(),
    )
    return jax.shard_map(
        local,
        mesh=mesh,
        in_specs=placed,
        out_specs=(
            P(("replica", "dp"), None, None),
            P("replica", "dp", None),
            P("replica", "dp", None),
            P("replica", "dp", None),
            P("replica"),
        ),
        check_vma=False,
    )
```

```python
import functools

import jax
import jax.numpy as jnp
from jax import lax
from jax.experimental import pallas as pl
from jax.experimental.pallas import tpu as pltpu
from jax.sharding import PartitionSpec as P

GSIZE = 40

NORM_EPS = 1e-05
BETA_ONE = 0.9
BETA_TWO = 0.999
LEARN_RATE = 0.002
ADAM_EPS = 1e-08

LANES = 128
TILE_ROWS = 16
VMEM_BYTES = 16 * 1024 * 1024


def padded(rows):
    return -(-rows // TILE_ROWS) * TILE_ROWS


def packed_rows(rows):
    return padded(rows + 1)


class Packing:
    def __init__(self, rows, start, stop):
        self.rows, self.start, self.stop = rows, start, stop
        self.columns = stop - start
        self.deep = packed_rows(rows)
        self.tiles, self.rest = divmod(self.columns, LANES)
        fold = LANES // self.rest if self.rest else 1
        self.fold_rows = padded(-(-self.deep // fold))
        self.folds = [
            (first, min(self.fold_rows, self.deep - first)) for first in range(0, self.deep, self.fold_rows)
        ]
        self.height = self.tiles * self.deep + (self.fold_rows if self.rest else 0)

    def write(self, ref, block):
        for tile in range(self.tiles):
            ref[tile * self.deep : (tile + 1) * self.deep, :] = block[
                :, tile * LANES : (tile + 1) * LANES
            ].astype(ref.dtype)
        if self.rest:
            left = block[:, self.tiles * LANES :]
            parts = []
            for first, count in self.folds:
                part = left[first : first + count]
                if count < self.fold_rows:
                    part = jnp.concatenate(
                        [part, jnp.zeros((self.fold_rows - count, self.rest), part.dtype)], axis=0
                    )
                parts.append(part)
            spare = LANES - self.rest * len(parts)
            if spare:
                parts.append(jnp.zeros((self.fold_rows, spare), left.dtype))
            ref[self.tiles * self.deep :, :] = jnp.concatenate(parts, axis=1).astype(ref.dtype)

    def read(self, ref):
        pieces = [
            ref[tile * self.deep : (tile + 1) * self.deep, :].astype(jnp.float32) for tile in range(self.tiles)
        ]
        if self.rest:
            left = ref[self.tiles * self.deep :, :].astype(jnp.float32)
            parts = [
                left[:count, i * self.rest : (i + 1) * self.rest] for i, (_, count) in enumerate(self.folds)
            ]
            pieces.append(jnp.concatenate(parts, axis=0) if len(parts) > 1 else parts[0])
        return jnp.concatenate(pieces, axis=1) if len(pieces) > 1 else pieces[0]

    def unpack(self, ref, out_ref, first_row):
        for tile in range(self.tiles):
            out_ref[first_row : first_row + self.deep, tile * LANES : (tile + 1) * LANES] = ref[
                tile * self.deep : (tile + 1) * self.deep, :
            ]
        if self.rest:
            left = ref[self.tiles * self.deep :, :]
            for i, (first, count) in enumerate(self.folds):
                out_ref[first_row + first : first_row + first + count, self.tiles * LANES :] = left[
                    :count, i * self.rest : (i + 1) * self.rest
                ]

    def payload(self):
        return jax.ShapeDtypeStruct((self.height, LANES), jnp.bfloat16)

    def block(self):
        return jax.ShapeDtypeStruct((self.deep, self.columns), jnp.float32)


def group_sums(rows, same_group):
    high = rows.astype(jnp.bfloat16).astype(jnp.float32)
    rest = rows - high
    middle = rest.astype(jnp.bfloat16).astype(jnp.float32)
    count = rows.shape[0]
    stacked = jnp.concatenate([high, middle, rest - middle], axis=0).astype(jnp.bfloat16)
    sums = jnp.dot(stacked, same_group, preferred_element_type=jnp.float32)
    return sums[:count] + (sums[count : 2 * count] + sums[2 * count :])


def table_sums(packs, rows, same_group):
    return jnp.concatenate(
        [
            group_sums(rows[:, pack.start : pack.stop], same_group[: pack.columns, : pack.columns])
            for pack in packs
        ],
        axis=1,
    )


def position_sums(parts):
    return jnp.concatenate([jnp.sum(part, axis=0, keepdims=True) for part in parts], axis=0)


def sigmoid(values):
    return 0.5 * jnp.tanh(0.5 * values) + 0.5


def silu_grad(values):
    gate = sigmoid(values)
    return gate * (1.0 + values * (1.0 - gate))


def cast_kernel(pack, push_ref, params_ref, token_ref, other_token_ref, out_ref, rows_ref):
    rows = pack.rows
    rows_ref[rows // 8 * 8 :, :] = jnp.zeros((pack.deep - rows // 8 * 8, pack.columns), jnp.float32)
    rows_ref[:rows, :] = params_ref[:, 0, pack.start : pack.stop] / push_ref[0]
    pack.write(out_ref, rows_ref[...])


def norm_in_kernel(shards, packs, me_ref, scales_ref, shift_ref, x_hbm, out_grad_hbm, *refs):
    act_ref, mean_ref, inverse_ref, same_group_ref = refs[:4]
    shift_refs, out_grad_refs = refs[4 : 4 + len(packs)], refs[4 + len(packs) : 4 + 2 * len(packs)]
    x_ref, out_grad_ref, sems = refs[4 + 2 * len(packs) :]
    copies = [
        pltpu.make_async_copy(x_hbm, x_ref, sems.at[0]),
        pltpu.make_async_copy(out_grad_hbm, out_grad_ref, sems.at[1]),
    ]
    for copy in copies:
        copy.start()
    samples, positions, channels = x_ref.shape
    rows = channels // shards
    deep = act_ref.shape[0] // shards
    entries = positions * GSIZE
    group_of_row = lax.broadcasted_iota(jnp.int32, same_group_ref.shape, 0) // GSIZE
    group_of_column = lax.broadcasted_iota(jnp.int32, same_group_ref.shape, 1) // GSIZE
    same_group_ref[...] = (group_of_row == group_of_column).astype(jnp.float32).astype(jnp.bfloat16)
    same_group = same_group_ref[...]
    for pack, shift_out in zip(packs, shift_refs):
        shift_out[...] = shift_ref[...].astype(jnp.float32)[:, pack.start : pack.stop]
    copies[0].wait()
    parts = [x_ref[i].astype(jnp.float32) for i in range(samples)]
    mean = table_sums(packs, position_sums(parts), same_group) / entries
    centered = [parts[i] - mean[i : i + 1] for i in range(samples)]
    variance = table_sums(packs, position_sums([part * part for part in centered]), same_group) / entries
    inverse = lax.rsqrt(variance + NORM_EPS)
    mean_ref[...] = mean
    inverse_ref[...] = inverse
    normed = [centered[i] * inverse[i : i + 1] for i in range(samples)]
    act = jnp.concatenate([part * sigmoid(part) for part in normed], axis=0).T
    for block in range(shards):
        slot = jnp.bitwise_xor(me_ref[0], block)
        act_ref[pl.ds(pl.multiple_of(slot * deep, TILE_ROWS), deep), :] = jnp.concatenate(
            [act[block * rows : (block + 1) * rows], jnp.zeros((deep - rows, act.shape[1]), jnp.float32)], axis=0
        ).astype(jnp.bfloat16)
    copies[1].wait()
    for pack, out_grad_out in zip(packs, out_grad_refs):
        for i in range(samples):
            out_grad_out[i] = out_grad_ref[i][:, pack.start : pack.stop]


def mix_kernel(shards, pack, act_ref, shift_ref, out_grad_ref, same_group_ref, *refs):
    weight_refs, token_ref, refs = refs[:shards], refs[shards], refs[shards + 1 :]
    grad_hidden_ref, weight_out_ref, own_ref = refs[:3]
    send_refs, (weight_ref, kept_ref, sems) = refs[3 : 2 + shards], refs[2 + shards :]
    samples, positions, columns = out_grad_ref.shape
    entries = positions * GSIZE
    deep = pack.deep
    for slot, shard_ref in enumerate(weight_refs):
        pack.unpack(shard_ref, weight_ref, slot * deep)
    weight_copy = pltpu.make_async_copy(weight_ref, weight_out_ref, sems.at[0])
    weight_copy.start()
    same_group = same_group_ref[:columns, :columns]
    hidden = lax.dot_general(
        act_ref[...], weight_ref[...], (((0,), (0,)), ((), ())), preferred_element_type=jnp.float32
    )
    parts = [
        hidden[i * positions : (i + 1) * positions] + shift_ref[i : i + 1, :]
        for i in range(samples)
    ]
    mean = group_sums(position_sums(parts), same_group) / entries
    parts = [parts[i] - mean[i : i + 1] for i in range(samples)]
    variance = group_sums(position_sums([part * part for part in parts]), same_group) / entries
    inverse = lax.rsqrt(variance + NORM_EPS)
    normed = [parts[i] * inverse[i : i + 1] for i in range(samples)]
    grads = [out_grad_ref[i].astype(jnp.float32) * silu_grad(normed[i]) for i in range(samples)]
    means = group_sums(
        jnp.concatenate(
            [position_sums(grads), position_sums([g * n for g, n in zip(grads, normed)])], axis=0
        ),
        same_group,
    ) / entries
    for i in range(samples):
        first, second = means[i : i + 1], means[samples + i : samples + i + 1]
        kept_ref[i * positions : (i + 1) * positions, :] = (
            inverse[i : i + 1] * (grads[i] - first - normed[i] * second)
        ).astype(jnp.bfloat16)
    copy = pltpu.make_async_copy(kept_ref, grad_hidden_ref, sems.at[1])
    copy.start()
    grad = jnp.dot(act_ref[...], kept_ref[...], preferred_element_type=jnp.float32)
    for slot, send_ref in enumerate(send_refs, 1):
        pack.write(send_ref, grad[slot * deep : (slot + 1) * deep])
    own_ref[...] = grad[:deep]
    weight_copy.wait()
    copy.wait()


def input_grad_kernel(shards, packs, me_ref, mean_ref, inverse_ref, same_group_ref, x_hbm, *refs):
    count = len(packs)
    grad_hbms, weight_hbms, out_ref = refs[:count], refs[count : 2 * count], refs[2 * count]
    rows_ref, x_ref, made_ref, sems = refs[2 * count + 1 : 2 * count + 5]
    grad_refs, weight_refs = refs[2 * count + 5 : 3 * count + 5], refs[3 * count + 5 :]
    copies = [
        pltpu.make_async_copy(source, target, sems.at[i])
        for i, (source, target) in enumerate(
            zip((*weight_hbms, *grad_hbms, x_hbm), (*weight_refs, *grad_refs, x_ref))
        )
    ]
    for copy in copies:
        copy.start()
    samples, positions, channels = x_ref.shape
    entries = positions * GSIZE
    rows = channels // shards
    weights = []
    for index, (pack, weight_ref) in enumerate(zip(packs, weight_refs)):
        copies[index].wait()
        for block in range(shards):
            slot = jnp.bitwise_xor(me_ref[0], block)
            rows_ref[block * rows : (block + 1) * rows, : pack.columns] = weight_ref[
                pl.ds(pl.multiple_of(slot * pack.deep, TILE_ROWS), pack.deep), :
            ].astype(jnp.float32)[:rows]
        weights.append(rows_ref[:, : pack.columns].astype(jnp.bfloat16))
    grad_act = 0.0
    for index, (grad_ref, weight) in enumerate(zip(grad_refs, weights)):
        copies[count + index].wait()
        grad_act += lax.dot_general(
            grad_ref[...], weight, (((1,), (1,)), ((), ())), preferred_element_type=jnp.float32
        )
    copies[-1].wait()
    inverse = inverse_ref[...]
    normed = [
        (x_ref[i].astype(jnp.float32) - mean_ref[i : i + 1, :]) * inverse[i : i + 1] for i in range(samples)
    ]
    grads = [grad_act[i * positions : (i + 1) * positions] * silu_grad(normed[i]) for i in range(samples)]
    means = table_sums(
        packs,
        jnp.concatenate(
            [position_sums(grads), position_sums([g * n for g, n in zip(grads, normed)])], axis=0
        ),
        same_group_ref[...],
    ) / entries
    for i in range(samples):
        first, second = means[i : i + 1], means[samples + i : samples + i + 1]
        made_ref[i] = (inverse[i : i + 1] * (grads[i] - first - normed[i] * second)).astype(jnp.bfloat16)
        copies.append(pltpu.make_async_copy(made_ref.at[i], out_ref.at[i], sems.at[len(copies)]))
        copies[-1].start()
    for copy in copies[-samples:]:
        copy.wait()


def merge_kernel(one_ref, other_ref, *refs):
    count = len(refs) // 2
    through_refs, out_ref, through_out_refs = refs[:count], refs[count], refs[count + 1 :]
    out_ref[...] = (one_ref[...].astype(jnp.float32) + other_ref[...].astype(jnp.float32)).astype(out_ref.dtype)
    for through_ref, through_out_ref in zip(through_refs, through_out_refs):
        through_out_ref[...] = through_ref[...]


def cut_kernel(packs, *refs):
    count = 3 * len(packs)
    hbm_refs, out_refs = refs[:3], refs[4 : 4 + count]
    row_refs, block_refs, sems = refs[4 + count : 7 + count], refs[7 + count : -1], refs[-1]
    copies = [
        pltpu.make_async_copy(source, target, sems.at[i])
        for i, (source, target) in enumerate(zip(hbm_refs, row_refs))
    ]
    for copy in copies:
        copy.start()
    out_copies = []
    for i, row_ref in enumerate(row_refs):
        copies[i].wait()
        for index, pack in enumerate(packs):
            place = 3 * index + i
            block_refs[place][...] = row_ref[:, 0, pack.start : pack.stop]
            out_copies.append(pltpu.make_async_copy(block_refs[place], out_refs[place], sems.at[3 + place]))
            out_copies[-1].start()
    for copy in out_copies:
        copy.wait()


def adam_kernel(count, pack, spare_value, scales_ref, push_ref, own_ref, *refs):
    other_refs, refs = refs[:count], refs[count:]
    (params_ref, first_ref, second_ref), (grad_ref, moved_ref, sent_ref) = refs[:3], refs[-3:]
    rows = pack.rows
    total = own_ref[...]
    for other_ref in other_refs:
        total = total + pack.read(other_ref)
    grad_ref[...] = total * scales_ref[2]
    grad = grad_ref[:rows, :]
    first_new = BETA_ONE * first_ref[...] + (1.0 - BETA_ONE) * grad
    second_new = BETA_TWO * second_ref[...] + (1.0 - BETA_TWO) * grad * grad
    update = (scales_ref[0] * first_new) / (jnp.sqrt(second_new * scales_ref[1]) + ADAM_EPS)
    value = push_ref[0] if spare_value else 0.0
    moved_ref[rows // 8 * 8 :, :] = jnp.full((pack.deep - rows // 8 * 8, pack.columns), value, jnp.float32)
    moved_ref[:rows, :] = params_ref[...] - update
    pack.write(sent_ref, moved_ref[...])


def half_average_kernel(pack, push_ref, moved_ref, other_ref, mean_ref, push_out_ref):
    other = pack.read(other_ref)
    mean_ref[...] = 0.5 * (moved_ref[...] + other)
    push_out_ref[...] = 0.5 * (push_ref[0] + other[pack.rows, :1])


def moments_kernel(packs, first_hbm, second_hbm, *refs):
    grad_refs, (first_out, second_out, first_ref, second_ref, sems) = refs[: len(packs)], refs[len(packs) :]
    copies = [
        pltpu.make_async_copy(first_hbm, first_ref, sems.at[0]),
        pltpu.make_async_copy(second_hbm, second_ref, sems.at[1]),
    ]
    for copy in copies:
        copy.start()
    rows = first_ref.shape[0]
    grad = jnp.concatenate([grad_ref[:rows, :] for grad_ref in grad_refs], axis=1)
    copies[0].wait()
    first_out[:, 0, :] = BETA_ONE * first_ref[:, 0, :] + (1.0 - BETA_ONE) * grad
    copies[1].wait()
    second_out[:, 0, :] = BETA_TWO * second_ref[:, 0, :] + (1.0 - BETA_TWO) * grad * grad


def average_kernel(pack, mean_ref, moved_ref, other_ref, out_ref, rows_ref, sem):
    rows = out_ref.shape[0]
    later = 0.5 * (moved_ref[...] + pack.read(other_ref))
    rows_ref[:, 0, :] = jnp.concatenate([mean_ref[...], later], axis=1)[:rows]
    copy = pltpu.make_async_copy(rows_ref, out_ref, sem)
    copy.start()
    copy.wait()


SCALARS = pl.BlockSpec(memory_space=pltpu.SMEM)
BLOCKS = pl.BlockSpec(memory_space=pltpu.VMEM)
TOKEN = pl.BlockSpec(memory_space=pl.ANY)
IN_HBM = pl.BlockSpec(memory_space=pltpu.HBM)


def call(kernel, name, outs, specs, operands, scratch=(), out_specs=None, flops=0, elements=0):
    return pl.pallas_call(
        kernel,
        out_shape=outs,
        in_specs=specs,
        out_specs=out_specs or jax.tree.map(lambda _: BLOCKS, outs),
        scratch_shapes=list(scratch),
        compiler_params=pltpu.CompilerParams(vmem_limit_bytes=VMEM_BYTES),
        cost_estimate=pl.CostEstimate(flops=flops, bytes_accessed=8 * elements, transcendentals=elements),
        name=name,
    )(*operands)


def stay(array):
    return pltpu.with_memory_space_constraint(array, pltpu.HBM)


def moved_on(block, axis, distance):
    size = lax.axis_size(axis)
    return lax.ppermute(block, axis, [(i, (i + distance) % size) for i in range(size)])


def exchanged(block, axis, bit):
    return lax.ppermute(block, axis, [(i, i ^ bit) for i in range(lax.axis_size(axis))])


def lowest_bit(slot):
    return slot & -slot


def hold_kernel(block_ref, token_ref, out_ref):
    out_ref[...] = block_ref[...]


def gathered(piece, shards, token=None):
    held = [piece]
    for slot in range(1, shards):
        bit = lowest_bit(slot)
        held.append(exchanged(held[slot ^ bit], "dp", bit))
        if token is not None and slot == 2:
            shape = jax.ShapeDtypeStruct(piece.shape, piece.dtype)
            held[slot] = call(hold_kernel, "hold", shape, [BLOCKS, IN_HBM], (held[slot], stay(token)))
    return held


def scattered(parts, shards):
    arrived = [[] for _ in parts]
    direct = [sends[0] for sends in parts]
    for part, sends in enumerate(parts):
        held = dict(enumerate(sends, 1))
        slots = sorted(range(2, shards), key=lambda slot: (-slot.bit_count(), -slot))
        for slot in slots:
            bit = lowest_bit(slot)
            other = exchanged(held[slot], "dp", bit)
            if slot == bit:
                arrived[part].append(other)
                continue
            through = direct if part == len(parts) - 1 and slot.bit_count() == 2 else []
            shapes = [jax.ShapeDtypeStruct(array.shape, array.dtype) for array in (other, *through)]
            held[slot ^ bit], *through = call(
                merge_kernel, "merge", tuple(shapes), [BLOCKS] * (2 + len(through)), (held[slot ^ bit], other, *through)
            )
            direct = through or direct
    for part, piece in enumerate(direct):
        arrived[part].append(exchanged(piece, "dp", 1))
    return arrived


def column_cuts(channels):
    half = (channels // GSIZE + 1) // 2 * GSIZE
    return [(0, half), (half, channels)]


def local(
    block_input, time_shift, out_grad, params, first_moment, second_moment, push_weight, step
):
    samples, positions, channels = block_input.shape
    tokens = samples * positions
    shards = lax.axis_size("dp")
    rows = params.shape[1]
    deep = packed_rows(rows)
    me = lax.axis_index("dp").astype(jnp.int32).reshape(1)
    packs = [Packing(rows, start, stop) for start, stop in column_cuts(channels)]
    params, first_moment, second_moment = (
        jnp.transpose(array, (1, 0, 2)) for array in (params, first_moment, second_moment)
    )
    def shards_of(pack, *tokens, late=None):
        piece = call(
            functools.partial(cast_kernel, pack),
            "cast",
            pack.payload(),
            [SCALARS, BLOCKS, TOKEN, TOKEN],
            (push_weight, params, *tokens),
            scratch=[pltpu.VMEM((deep, pack.columns), jnp.float32)],
            elements=rows * pack.columns,
        )
        return gathered(piece, shards, late)

    level_count = lax.axis_size("replica").bit_length() - 1
    distance_bits = step[0] % level_count
    step_count = (step[0] + 1).astype(jnp.float32)
    scales = jnp.stack(
        [
            LEARN_RATE / (1.0 - jnp.power(BETA_ONE, step_count)),
            1.0 / (1.0 - jnp.power(BETA_TWO, step_count)),
            jnp.float32(1.0 / shards),
        ]
    )

    activation, mean_in, inverse_in, same_group, *pieces = call(
        functools.partial(norm_in_kernel, shards, packs),
        "norm_in",
        (
            jax.ShapeDtypeStruct((shards * deep, tokens), jnp.bfloat16),
            jax.ShapeDtypeStruct((samples, channels), jnp.float32),
            jax.ShapeDtypeStruct((samples, channels), jnp.float32),
            jax.ShapeDtypeStruct((max(pack.columns for pack in packs),) * 2, jnp.bfloat16),
            *(jax.ShapeDtypeStruct((samples, pack.columns), jnp.float32) for pack in packs),
            *(jax.ShapeDtypeStruct((samples, positions, pack.columns), jnp.bfloat16) for pack in packs),
        ),
        [SCALARS, SCALARS, BLOCKS, IN_HBM, IN_HBM],
        (me, scales, time_shift, stay(block_input), stay(out_grad)),
        scratch=[
            pltpu.VMEM(block_input.shape, jnp.bfloat16),
            pltpu.VMEM(out_grad.shape, jnp.bfloat16),
            pltpu.SemaphoreType.DMA((2,)),
        ],
        elements=tokens * channels,
    )

    columns = [pack.columns for pack in packs for _ in range(3)]
    blocks = call(
        functools.partial(cut_kernel, packs),
        "cut",
        tuple(pltpu.HBM((rows, width), jnp.float32) for width in columns),
        [IN_HBM] * 3 + [TOKEN],
        (stay(params), stay(first_moment), stay(second_moment), mean_in),
        scratch=[pltpu.VMEM(params.shape, jnp.float32)] * 3
        + [pltpu.VMEM((rows, width), jnp.float32) for width in columns]
        + [pltpu.SemaphoreType.DMA((3 + len(columns),))],
        out_specs=(IN_HBM,) * len(columns),
        elements=rows * channels,
    )
    weights = [shards_of(packs[0], push_weight, push_weight)]
    weights.append(shards_of(packs[1], weights[0][1], mean_in, late=blocks[-1]))
    hidden_grads, full_weights, owns, parts = [], [], [], []
    token = mean_in
    shifts, out_grads = pieces[: len(packs)], pieces[len(packs) :]
    for pack, shard_list, shift, out_grad_piece in zip(packs, weights, shifts, out_grads):
        grad_hidden, full_weight, own, *sends = call(
            functools.partial(mix_kernel, shards, pack),
            "mix",
            (
                pltpu.HBM((tokens, pack.columns), jnp.bfloat16),
                pltpu.HBM((shards * deep, pack.columns), jnp.bfloat16),
                pack.block(),
            )
            + (pack.payload(),) * (shards - 1),
            [BLOCKS] * (4 + shards) + [TOKEN],
            (activation, shift, out_grad_piece, same_group, *shard_list, token),
            scratch=[
                pltpu.VMEM((shards * deep, pack.columns), jnp.bfloat16),
                pltpu.VMEM((tokens, pack.columns), jnp.bfloat16),
                pltpu.SemaphoreType.DMA((2,)),
            ],
            out_specs=(IN_HBM,) * 2 + (BLOCKS,) * shards,
            flops=4 * tokens * channels * pack.columns,
            elements=tokens * pack.columns,
        )
        token = own
        hidden_grads.append(grad_hidden)
        full_weights.append(full_weight)
        owns.append(own)
        parts.append(sends)

    def input_grad(*operands):
        return call(
            functools.partial(input_grad_kernel, shards, packs),
            "input_grad",
            pltpu.HBM(block_input.shape, jnp.bfloat16),
            [SCALARS] + [BLOCKS] * 3 + [IN_HBM] * (1 + 2 * len(packs)),
            operands[:4] + tuple(map(stay, operands[4:])),
            scratch=[
                pltpu.VMEM((channels, max(pack.columns for pack in packs)), jnp.float32),
                pltpu.VMEM(block_input.shape, jnp.bfloat16),
                pltpu.VMEM(block_input.shape, jnp.bfloat16),
                pltpu.SemaphoreType.DMA((1 + 2 * len(packs) + samples,)),
                *(pltpu.VMEM((tokens, pack.columns), jnp.bfloat16) for pack in packs),
                *(pltpu.VMEM((shards * deep, pack.columns), jnp.bfloat16) for pack in packs),
            ],
            out_specs=IN_HBM,
            flops=2 * tokens * channels * channels,
            elements=tokens * channels,
        )

    def moments(*grads):
        return call(
            functools.partial(moments_kernel, packs),
            "moments",
            (jax.ShapeDtypeStruct(params.shape, jnp.float32),) * 2,
            [IN_HBM] * 2 + [BLOCKS] * len(packs),
            (stay(first_moment), stay(second_moment), *grads),
            scratch=[pltpu.VMEM(params.shape, jnp.float32)] * 2 + [pltpu.SemaphoreType.DMA((2,))],
            elements=rows * channels,
        )

    def from_behind(finish, *operands):
        def branch(distance):
            return lambda *values: finish(lambda block: moved_on(block, "replica", distance), *values)

        return lax.switch(distance_bits, [branch(1 << power) for power in range(level_count)], *operands)

    grad_input = input_grad(
        me, mean_in, inverse_in, same_group, block_input, *hidden_grads, *full_weights
    )
    arrived = scattered(parts, shards)
    early, late = packs

    def adam(pack, own, others, blocks):
        return call(
            functools.partial(adam_kernel, len(others), pack, pack is early),
            "adam",
            (pack.block(), pack.block(), pack.payload()),
            [SCALARS] * 2 + [BLOCKS] * (4 + len(others)),
            (scales, push_weight, own, *others, *blocks),
            elements=rows * pack.columns,
        )

    grad_a, moved_a, sent_a = adam(early, owns[0], arrived[0], blocks[:3])

    def finish(move, sent, grad_a, moved_a, own, *operands):
        other_a = move(sent)
        grad_b, moved_b, sent_b = adam(late, own, operands[:-3], operands[-3:])
        other_b = move(sent_b)
        mean, weight = call(
            functools.partial(half_average_kernel, early),
            "half_average",
            (early.block(), jax.ShapeDtypeStruct((1,), jnp.float32)),
            [SCALARS] + [BLOCKS] * 2,
            (push_weight, moved_a, other_a),
            elements=rows * early.columns,
        )
        averaged = call(
            functools.partial(average_kernel, late),
            "average",
            pltpu.HBM(params.shape, jnp.float32),
            [BLOCKS] * 3,
            (mean, moved_b, other_b),
            scratch=[pltpu.VMEM(params.shape, jnp.float32), pltpu.SemaphoreType.DMA],
            out_specs=IN_HBM,
            elements=rows * channels,
        )
        return (*moments(grad_a, grad_b), averaged, weight)

    first_new, second_new, averaged, new_weight = from_behind(
        finish, sent_a, grad_a, moved_a, owns[1], *arrived[1], *blocks[3:]
    )
    return (
        grad_input,
        *(jnp.transpose(array, (1, 0, 2)) for array in (averaged, first_new, second_new)),
        new_weight,
    )


def solution(mesh):
    placed = (
        P(("replica", "dp"), None, None),
        P(("replica", "dp"), None),
        P(("replica", "dp"), None, None),
        P("replica", "dp", None),
        P("replica", "dp", None),
        P("replica", "dp", None),
        P("replica"),
        P(),
    )
    return jax.shard_map(
        local,
        mesh=mesh,
        in_specs=placed,
        out_specs=(
            P(("replica", "dp"), None, None),
            P("replica", "dp", None),
            P("replica", "dp", None),
            P("replica", "dp", None),
            P("replica"),
        ),
        check_vma=False,
    )
```

```python
import functools

import jax
import jax.numpy as jnp
from jax import lax
from jax.experimental import pallas as pl
from jax.experimental.pallas import tpu as pltpu
from jax.sharding import PartitionSpec as P

GSIZE = 40

NORM_EPS = 1e-05
BETA_ONE = 0.9
BETA_TWO = 0.999
LEARN_RATE = 0.002
ADAM_EPS = 1e-08

LANES = 128
ROW_STEP = 32
UNROLL = 3
TILE_ROWS = 16
VMEM_BYTES = 16 * 1024 * 1024


def padded(rows):
    return -(-rows // TILE_ROWS) * TILE_ROWS


def packed_rows(rows):
    return padded(rows + 1)


class Packing:
    def __init__(self, rows, start, stop):
        self.rows, self.start, self.stop = rows, start, stop
        self.columns = stop - start
        self.deep = packed_rows(rows)
        self.tiles, self.rest = divmod(self.columns, LANES)
        fold = LANES // self.rest if self.rest else 1
        self.fold_rows = padded(-(-self.deep // fold))
        self.folds = [
            (first, min(self.fold_rows, self.deep - first)) for first in range(0, self.deep, self.fold_rows)
        ]
        self.height = self.tiles * self.deep + (self.fold_rows if self.rest else 0)

    def write(self, ref, block):
        for tile in range(self.tiles):
            ref[tile * self.deep : (tile + 1) * self.deep, :] = block[
                :, tile * LANES : (tile + 1) * LANES
            ].astype(ref.dtype)
        if self.rest:
            left = block[:, self.tiles * LANES :]
            parts = []
            for first, count in self.folds:
                part = left[first : first + count]
                if count < self.fold_rows:
                    part = jnp.concatenate(
                        [part, jnp.zeros((self.fold_rows - count, self.rest), part.dtype)], axis=0
                    )
                parts.append(part)
            spare = LANES - self.rest * len(parts)
            if spare:
                parts.append(jnp.zeros((self.fold_rows, spare), left.dtype))
            ref[self.tiles * self.deep :, :] = jnp.concatenate(parts, axis=1).astype(ref.dtype)

    def read(self, ref):
        pieces = [
            ref[tile * self.deep : (tile + 1) * self.deep, :].astype(jnp.float32) for tile in range(self.tiles)
        ]
        if self.rest:
            left = ref[self.tiles * self.deep :, :].astype(jnp.float32)
            parts = [
                left[:count, i * self.rest : (i + 1) * self.rest] for i, (_, count) in enumerate(self.folds)
            ]
            pieces.append(jnp.concatenate(parts, axis=0) if len(parts) > 1 else parts[0])
        return jnp.concatenate(pieces, axis=1) if len(pieces) > 1 else pieces[0]

    def unpack(self, ref, out_ref, first_row):
        for tile in range(self.tiles):
            out_ref[first_row : first_row + self.deep, tile * LANES : (tile + 1) * LANES] = ref[
                tile * self.deep : (tile + 1) * self.deep, :
            ]
        if self.rest:
            left = ref[self.tiles * self.deep :, :]
            for i, (first, count) in enumerate(self.folds):
                out_ref[first_row + first : first_row + first + count, self.tiles * LANES :] = left[
                    :count, i * self.rest : (i + 1) * self.rest
                ]

    def payload(self):
        return jax.ShapeDtypeStruct((self.height, LANES), jnp.bfloat16)

    def block(self):
        return jax.ShapeDtypeStruct((self.deep, self.columns), jnp.float32)


def group_sums(rows, same_group):
    high = rows.astype(jnp.bfloat16).astype(jnp.float32)
    rest = rows - high
    middle = rest.astype(jnp.bfloat16).astype(jnp.float32)
    count = rows.shape[0]
    stacked = jnp.concatenate([high, middle, rest - middle], axis=0).astype(jnp.bfloat16)
    sums = jnp.dot(stacked, same_group, preferred_element_type=jnp.float32)
    return sums[:count] + (sums[count : 2 * count] + sums[2 * count :])


def table_sums(packs, rows, same_group):
    return jnp.concatenate(
        [
            group_sums(rows[:, pack.start : pack.stop], same_group[: pack.columns, : pack.columns])
            for pack in packs
        ],
        axis=1,
    )


def position_sums(parts):
    return jnp.concatenate([jnp.sum(part, axis=0, keepdims=True) for part in parts], axis=0)


def doubled_silu_grad(half, turned):
    return (1.0 + turned) + half * (1.0 - turned * turned)


def row(vector, i):
    return vector[i : i + 1]


def eight_sums(block):
    return sum(block[first : first + 8] for first in range(0, block.shape[0], 8))


def squares_sums(samples, positions, step, load, offset):
    sums = []
    for i in range(samples):

        def body(k, total):
            value = load(i, pl.multiple_of(k * step, step), step) + row(offset, i)
            return total + eight_sums(value * value)

        total = lax.fori_loop(0, positions // step, body, jnp.zeros((8, offset.shape[1]), jnp.float32), unroll=UNROLL)
        sums.append(jnp.sum(total, axis=0, keepdims=True))
    return jnp.concatenate(sums, axis=0)


def norm_back(table_mean, samples, positions, step, load, scales, offsets, inverse, incoming, kept_ref, store):
    firsts, seconds = [], []
    zeros = jnp.zeros((8, scales.shape[1]), jnp.float32)
    for i in range(samples):

        def body(k, totals):
            first_row = pl.multiple_of(k * step, step)
            half = load(i, first_row, step) * row(scales, i) + row(offsets, i)
            doubled = incoming(i, first_row, step) * doubled_silu_grad(half, jnp.tanh(half))
            kept_ref[pl.ds(pl.multiple_of(i * positions + first_row, step), step), :] = doubled
            return totals[0] + eight_sums(doubled), totals[1] + eight_sums(doubled * half)

        first, second = lax.fori_loop(0, positions // step, body, (zeros, zeros), unroll=UNROLL)
        firsts.append(jnp.sum(first, axis=0, keepdims=True))
        seconds.append(jnp.sum(second, axis=0, keepdims=True))
    means = table_mean(jnp.concatenate(firsts + seconds, axis=0))
    first, second = 0.5 * means[:samples], means[samples:]
    gain = 0.5 * inverse
    slope = (2.0 * inverse) * second * scales
    level = inverse * (first + 2.0 * offsets * second)
    for i in range(samples):

        def body(k, carry):
            first_row = pl.multiple_of(k * step, step)
            doubled = kept_ref[pl.ds(pl.multiple_of(i * positions + first_row, step), step), :]
            value = load(i, first_row, step)
            store(i, first_row, step, doubled * row(gain, i) - (value * row(slope, i) + row(level, i)))
            return carry

        lax.fori_loop(0, positions // step, body, 0, unroll=UNROLL)


def sigmoid(values):
    return 0.5 * jnp.tanh(0.5 * values) + 0.5


def silu_grad(values):
    gate = sigmoid(values)
    return gate * (1.0 + values * (1.0 - gate))


def cast_kernel(pack, push_ref, params_ref, token_ref, other_token_ref, out_ref, rows_ref):
    rows = pack.rows
    rows_ref[rows // 8 * 8 :, :] = jnp.zeros((pack.deep - rows // 8 * 8, pack.columns), jnp.float32)
    rows_ref[:rows, :] = params_ref[:, 0, pack.start : pack.stop] / push_ref[...]
    pack.write(out_ref, rows_ref[...])


def norm_in_kernel(shards, packs, me_ref, scales_ref, shift_ref, x_hbm, out_grad_hbm, *refs):
    act_ref, mean_ref, inverse_ref, same_group_ref = refs[:4]
    shift_refs, out_grad_refs = refs[4 : 4 + len(packs)], refs[4 + len(packs) : 4 + 2 * len(packs)]
    x_ref, out_grad_ref, sems = refs[4 + 2 * len(packs) :]
    copies = [
        pltpu.make_async_copy(x_hbm, x_ref, sems.at[0]),
        pltpu.make_async_copy(out_grad_hbm, out_grad_ref, sems.at[1]),
    ]
    for copy in copies:
        copy.start()
    samples, positions, channels = x_ref.shape
    rows = channels // shards
    deep = act_ref.shape[0] // shards
    entries = positions * GSIZE
    group_of_row = lax.broadcasted_iota(jnp.int32, same_group_ref.shape, 0) // GSIZE
    group_of_column = lax.broadcasted_iota(jnp.int32, same_group_ref.shape, 1) // GSIZE
    same_group_ref[...] = (group_of_row == group_of_column).astype(jnp.float32).astype(jnp.bfloat16)
    same_group = same_group_ref[...]
    for pack, shift_out in zip(packs, shift_refs):
        shift_out[...] = shift_ref[...].astype(jnp.float32)[:, pack.start : pack.stop]
    copies[0].wait()
    parts = [x_ref[i].astype(jnp.float32) for i in range(samples)]
    mean = table_sums(packs, position_sums(parts), same_group) / entries
    centered = [parts[i] - mean[i : i + 1] for i in range(samples)]
    variance = table_sums(packs, position_sums([part * part for part in centered]), same_group) / entries
    inverse = lax.rsqrt(variance + NORM_EPS)
    mean_ref[...] = mean
    inverse_ref[...] = inverse
    normed = [centered[i] * inverse[i : i + 1] for i in range(samples)]
    act = jnp.concatenate([part * sigmoid(part) for part in normed], axis=0).T
    for block in range(shards):
        slot = jnp.bitwise_xor(me_ref[0], block)
        act_ref[pl.ds(pl.multiple_of(slot * deep, TILE_ROWS), deep), :] = jnp.concatenate(
            [act[block * rows : (block + 1) * rows], jnp.zeros((deep - rows, act.shape[1]), jnp.float32)], axis=0
        ).astype(jnp.bfloat16)
    copies[1].wait()
    for pack, out_grad_out in zip(packs, out_grad_refs):
        for i in range(samples):
            out_grad_out[i] = out_grad_ref[i][:, pack.start : pack.stop]


def mix_kernel(shards, pack, act_ref, shift_ref, out_grad_ref, same_group_ref, *refs):
    weight_refs, token_ref, refs = refs[:shards], refs[shards], refs[shards + 1 :]
    grad_hidden_ref, weight_out_ref, own_ref = refs[:3]
    send_refs, (weight_ref, kept_ref, hidden_ref, doubled_ref, sems) = refs[3 : 2 + shards], refs[2 + shards :]
    samples, positions, columns = out_grad_ref.shape
    entries = positions * GSIZE
    deep = pack.deep
    for slot, shard_ref in enumerate(weight_refs):
        pack.unpack(shard_ref, weight_ref, slot * deep)
    weight_copy = pltpu.make_async_copy(weight_ref, weight_out_ref, sems.at[0])
    weight_copy.start()
    same_group = same_group_ref[:columns, :columns]
    hidden_ref[...] = lax.dot_general(
        act_ref[...], weight_ref[...], (((0,), (0,)), ((), ())), preferred_element_type=jnp.float32
    )

    def table_mean(rows):
        return group_sums(rows, same_group) / entries

    def load(i, first_row, count):
        return hidden_ref[pl.ds(pl.multiple_of(i * positions + first_row, count), count), :]

    def incoming(i, first_row, count):
        return out_grad_ref[i, pl.ds(first_row, count), :].astype(jnp.float32)

    def store(i, first_row, count, grad):
        kept_ref[pl.ds(pl.multiple_of(i * positions + first_row, count), count), :] = grad.astype(jnp.bfloat16)

    shift = shift_ref[...]
    sums = position_sums([hidden_ref[i * positions : (i + 1) * positions, :] for i in range(samples)])
    offset = shift - table_mean(sums + positions * shift)
    squares = squares_sums(samples, positions, ROW_STEP, load, offset)
    inverse = lax.rsqrt(table_mean(squares) + NORM_EPS)
    scales = 0.5 * inverse
    norm_back(
        table_mean, samples, positions, ROW_STEP, load, scales, offset * scales, inverse, incoming, doubled_ref, store
    )
    copy = pltpu.make_async_copy(kept_ref, grad_hidden_ref, sems.at[1])
    copy.start()
    grad = jnp.dot(act_ref[...], kept_ref[...], preferred_element_type=jnp.float32)
    for slot, send_ref in enumerate(send_refs, 1):
        pack.write(send_ref, grad[slot * deep : (slot + 1) * deep])
    own_ref[...] = grad[:deep]
    weight_copy.wait()
    copy.wait()


def input_grad_kernel(shards, packs, me_ref, mean_ref, inverse_ref, same_group_ref, x_hbm, *refs):
    count = len(packs)
    grad_refs, weight_refs, out_ref = refs[:count], refs[count : 2 * count], refs[2 * count]
    rows_ref, x_ref, made_ref, act_ref, sems = refs[2 * count + 1 :]
    copies = [pltpu.make_async_copy(x_hbm, x_ref, sems.at[0])]
    copies[0].start()
    samples, positions, channels = x_ref.shape
    entries = positions * GSIZE
    rows = channels // shards
    weights = []
    for index, (pack, weight_ref) in enumerate(zip(packs, weight_refs)):
        for block in range(shards):
            slot = jnp.bitwise_xor(me_ref[0], block)
            rows_ref[block * rows : (block + 1) * rows, : pack.columns] = weight_ref[
                pl.ds(pl.multiple_of(slot * pack.deep, TILE_ROWS), pack.deep), :
            ].astype(jnp.float32)[:rows]
        weights.append(rows_ref[:, : pack.columns].astype(jnp.bfloat16))
    grad_act = 0.0
    for index, (grad_ref, weight) in enumerate(zip(grad_refs, weights)):
        grad_act += lax.dot_general(
            grad_ref[...], weight, (((1,), (1,)), ((), ())), preferred_element_type=jnp.float32
        )
    act_ref[...] = grad_act
    copies[0].wait()
    same_group = same_group_ref[...]
    inverse = inverse_ref[...]

    def table_mean(rows):
        return table_sums(packs, rows, same_group) / entries

    def load(i, first_row, count):
        return x_ref[i, pl.ds(first_row, count), :].astype(jnp.float32)

    def incoming(i, first_row, count):
        return act_ref[pl.ds(pl.multiple_of(i * positions + first_row, count), count), :]

    def store(i, first_row, count, grad):
        made_ref[i, pl.ds(first_row, count), :] = grad.astype(jnp.bfloat16)

    scales = 0.5 * inverse
    norm_back(
        table_mean, samples, positions, ROW_STEP, load, scales, -mean_ref[...] * scales, inverse, incoming, act_ref, store
    )
    for i in range(samples):
        copies.append(pltpu.make_async_copy(made_ref.at[i], out_ref.at[i], sems.at[len(copies)]))
        copies[-1].start()
    for copy in copies[-samples:]:
        copy.wait()


def merge_kernel(one_ref, other_ref, *refs):
    count = len(refs) // 2
    through_refs, out_ref, through_out_refs = refs[:count], refs[count], refs[count + 1 :]
    out_ref[...] = (one_ref[...].astype(jnp.float32) + other_ref[...].astype(jnp.float32)).astype(out_ref.dtype)
    for through_ref, through_out_ref in zip(through_refs, through_out_refs):
        through_out_ref[...] = through_ref[...]


def cut_kernel(packs, *refs):
    count = 3 * len(packs)
    hbm_refs, out_refs = refs[:3], refs[4 : 4 + count]
    row_refs, block_refs, sems = refs[4 + count : 7 + count], refs[7 + count : -1], refs[-1]
    copies = [
        pltpu.make_async_copy(source, target, sems.at[i])
        for i, (source, target) in enumerate(zip(hbm_refs, row_refs))
    ]
    for copy in copies:
        copy.start()
    out_copies = []
    for i, row_ref in enumerate(row_refs):
        copies[i].wait()
        for index, pack in enumerate(packs):
            place = 3 * index + i
            block_refs[place][...] = row_ref[:, 0, pack.start : pack.stop]
            out_copies.append(pltpu.make_async_copy(block_refs[place], out_refs[place], sems.at[3 + place]))
            out_copies[-1].start()
    for copy in out_copies:
        copy.wait()


def adam_kernel(count, pack, spare_value, scales_ref, own_ref, *refs):
    other_refs, refs = refs[:count], refs[count:]
    (params_ref, first_ref, second_ref), (grad_ref, moved_ref, sent_ref) = refs[:3], refs[-3:]
    rows = pack.rows
    total = own_ref[...]
    for other_ref in other_refs:
        total = total + pack.read(other_ref)
    grad_ref[...] = total * scales_ref[2]
    grad = grad_ref[:rows, :]
    first_new = BETA_ONE * first_ref[...] + (1.0 - BETA_ONE) * grad
    second_new = BETA_TWO * second_ref[...] + (1.0 - BETA_TWO) * grad * grad
    update = (scales_ref[0] * first_new) / (jnp.sqrt(second_new * scales_ref[1]) + ADAM_EPS)
    value = scales_ref[3] if spare_value else 0.0
    moved_ref[rows // 8 * 8 :, :] = jnp.full((pack.deep - rows // 8 * 8, pack.columns), value, jnp.float32)
    moved_ref[:rows, :] = params_ref[...] - update
    pack.write(sent_ref, moved_ref[...])


def half_average_kernel(pack, scales_ref, moved_ref, other_ref, mean_ref, push_out_ref):
    other = pack.read(other_ref)
    mean_ref[...] = 0.5 * (moved_ref[...] + other)
    push_out_ref[...] = 0.5 * (scales_ref[3] + other[pack.rows, :1])


def moments_kernel(packs, first_hbm, second_hbm, *refs):
    grad_refs, (first_out, second_out, first_ref, second_ref, sems) = refs[: len(packs)], refs[len(packs) :]
    copies = [
        pltpu.make_async_copy(first_hbm, first_ref, sems.at[0]),
        pltpu.make_async_copy(second_hbm, second_ref, sems.at[1]),
    ]
    for copy in copies:
        copy.start()
    rows = first_ref.shape[0]
    grad = jnp.concatenate([grad_ref[:rows, :] for grad_ref in grad_refs], axis=1)
    copies[0].wait()
    first_out[:, 0, :] = BETA_ONE * first_ref[:, 0, :] + (1.0 - BETA_ONE) * grad
    copies[1].wait()
    second_out[:, 0, :] = BETA_TWO * second_ref[:, 0, :] + (1.0 - BETA_TWO) * grad * grad


def average_kernel(pack, mean_ref, moved_ref, other_ref, out_ref, rows_ref, sem):
    rows = out_ref.shape[0]
    later = 0.5 * (moved_ref[...] + pack.read(other_ref))
    rows_ref[:, 0, :] = jnp.concatenate([mean_ref[...], later], axis=1)[:rows]
    copy = pltpu.make_async_copy(rows_ref, out_ref, sem)
    copy.start()
    copy.wait()


SCALARS = pl.BlockSpec(memory_space=pltpu.SMEM)
BLOCKS = pl.BlockSpec(memory_space=pltpu.VMEM)
TOKEN = pl.BlockSpec(memory_space=pl.ANY)
IN_HBM = pl.BlockSpec(memory_space=pltpu.HBM)


def call(kernel, name, outs, specs, operands, scratch=(), out_specs=None, flops=0, elements=0):
    return pl.pallas_call(
        kernel,
        out_shape=outs,
        in_specs=specs,
        out_specs=out_specs or jax.tree.map(lambda _: BLOCKS, outs),
        scratch_shapes=list(scratch),
        compiler_params=pltpu.CompilerParams(vmem_limit_bytes=VMEM_BYTES),
        cost_estimate=pl.CostEstimate(flops=flops, bytes_accessed=8 * elements, transcendentals=elements),
        name=name,
    )(*operands)


def stay(array):
    return pltpu.with_memory_space_constraint(array, pltpu.HBM)


def moved_on(block, axis, distance):
    size = lax.axis_size(axis)
    return lax.ppermute(block, axis, [(i, (i + distance) % size) for i in range(size)])


def exchanged(block, axis, bit):
    return lax.ppermute(block, axis, [(i, i ^ bit) for i in range(lax.axis_size(axis))])


def lowest_bit(slot):
    return slot & -slot


def hold_kernel(block_ref, token_ref, out_ref):
    out_ref[...] = block_ref[...]


def gathered(piece, shards, token=None):
    held = [piece]
    for slot in range(1, shards):
        bit = lowest_bit(slot)
        held.append(exchanged(held[slot ^ bit], "dp", bit))
        if token is not None and slot == 2:
            shape = jax.ShapeDtypeStruct(piece.shape, piece.dtype)
            held[slot] = call(hold_kernel, "hold", shape, [BLOCKS, IN_HBM], (held[slot], stay(token)))
    return held


def scattered(parts, shards):
    arrived = []
    for part, sends in enumerate(parts):
        held = dict(enumerate(sends, 1))
        slots = sorted(range(2, shards), key=lambda slot: (-slot.bit_count(), -slot))
        last = part == len(parts) - 1
        got = [] if last else [exchanged(held[1], "dp", 1)]
        for slot in slots:
            bit = lowest_bit(slot)
            other = exchanged(held[slot], "dp", bit)
            if slot == bit:
                got.append(other)
                continue
            shape = jax.ShapeDtypeStruct(other.shape, other.dtype)
            held[slot ^ bit], held[1] = call(
                merge_kernel, "merge", (shape,) * 2, [BLOCKS] * 3, (held[slot ^ bit], other, held[1] if last else got[0])
            )
        if last:
            got.append(exchanged(held[1], "dp", 1))
        else:
            got[0] = held[1]
        arrived.append(got)
    return arrived


def column_cuts(channels):
    half = (channels // GSIZE + 1) // 2 * GSIZE
    return [(0, half), (half, channels)]


def local(
    block_input, time_shift, out_grad, params, first_moment, second_moment, push_weight, step
):
    samples, positions, channels = block_input.shape
    tokens = samples * positions
    shards = lax.axis_size("dp")
    rows = params.shape[1]
    deep = packed_rows(rows)
    me = lax.axis_index("dp").astype(jnp.int32).reshape(1)
    packs = [Packing(rows, start, stop) for start, stop in column_cuts(channels)]
    params, first_moment, second_moment = (
        jnp.transpose(array, (1, 0, 2)) for array in (params, first_moment, second_moment)
    )
    def shards_of(pack, *tokens, late=None):
        piece = call(
            functools.partial(cast_kernel, pack),
            "cast",
            pack.payload(),
            [BLOCKS, BLOCKS, TOKEN, TOKEN],
            (push_weight.reshape(1, 1), params, *tokens),
            scratch=[pltpu.VMEM((deep, pack.columns), jnp.float32)],
            elements=rows * pack.columns,
        )
        return gathered(piece, shards, late)

    level_count = lax.axis_size("replica").bit_length() - 1
    distance_bits = step[0] % level_count
    step_count = (step[0] + 1).astype(jnp.float32)
    scales = jnp.stack(
        [
            LEARN_RATE / (1.0 - jnp.power(BETA_ONE, step_count)),
            1.0 / (1.0 - jnp.power(BETA_TWO, step_count)),
            jnp.float32(1.0 / shards),
            push_weight[0],
        ]
    )

    activation, mean_in, inverse_in, same_group, *pieces = call(
        functools.partial(norm_in_kernel, shards, packs),
        "norm_in",
        (
            jax.ShapeDtypeStruct((shards * deep, tokens), jnp.bfloat16),
            jax.ShapeDtypeStruct((samples, channels), jnp.float32),
            jax.ShapeDtypeStruct((samples, channels), jnp.float32),
            jax.ShapeDtypeStruct((max(pack.columns for pack in packs),) * 2, jnp.bfloat16),
            *(jax.ShapeDtypeStruct((samples, pack.columns), jnp.float32) for pack in packs),
            *(jax.ShapeDtypeStruct((samples, positions, pack.columns), jnp.bfloat16) for pack in packs),
        ),
        [SCALARS, SCALARS, BLOCKS, IN_HBM, IN_HBM],
        (me, scales, time_shift, stay(block_input), stay(out_grad)),
        scratch=[
            pltpu.VMEM(block_input.shape, jnp.bfloat16),
            pltpu.VMEM(out_grad.shape, jnp.bfloat16),
            pltpu.SemaphoreType.DMA((2,)),
        ],
        elements=tokens * channels,
    )

    columns = [pack.columns for pack in packs for _ in range(3)]
    blocks = call(
        functools.partial(cut_kernel, packs),
        "cut",
        tuple(pltpu.HBM((rows, width), jnp.float32) for width in columns),
        [IN_HBM] * 3 + [TOKEN],
        (stay(params), stay(first_moment), stay(second_moment), mean_in),
        scratch=[pltpu.VMEM(params.shape, jnp.float32)] * 3
        + [pltpu.VMEM((rows, width), jnp.float32) for width in columns]
        + [pltpu.SemaphoreType.DMA((3 + len(columns),))],
        out_specs=(IN_HBM,) * len(columns),
        elements=rows * channels,
    )
    weights = [shards_of(packs[0], params, params)]
    weights.append(shards_of(packs[1], weights[0][1], mean_in, late=blocks[-1]))
    hidden_grads, full_weights, owns, parts = [], [], [], []
    token = mean_in
    shifts, out_grads = pieces[: len(packs)], pieces[len(packs) :]
    for pack, shard_list, shift, out_grad_piece in zip(packs, weights, shifts, out_grads):
        kept = jax.ShapeDtypeStruct if pack is packs[-1] else pltpu.HBM
        kept_spec = BLOCKS if pack is packs[-1] else IN_HBM
        grad_hidden, full_weight, own, *sends = call(
            functools.partial(mix_kernel, shards, pack),
            "mix",
            (
                kept((tokens, pack.columns), jnp.bfloat16),
                kept((shards * deep, pack.columns), jnp.bfloat16),
                pack.block(),
            )
            + (pack.payload(),) * (shards - 1),
            [BLOCKS] * (4 + shards) + [TOKEN],
            (activation, shift, out_grad_piece, same_group, *shard_list, token),
            scratch=[
                pltpu.VMEM((shards * deep, pack.columns), jnp.bfloat16),
                pltpu.VMEM((tokens, pack.columns), jnp.bfloat16),
                pltpu.VMEM((tokens, pack.columns), jnp.float32),
                pltpu.VMEM((tokens, pack.columns), jnp.float32),
                pltpu.SemaphoreType.DMA((2,)),
            ],
            out_specs=(kept_spec,) * 2 + (BLOCKS,) * shards,
            flops=4 * tokens * channels * pack.columns,
            elements=tokens * pack.columns,
        )
        token = own
        hidden_grads.append(grad_hidden)
        full_weights.append(full_weight)
        owns.append(own)
        parts.append(sends)

    def input_grad(*operands):
        return call(
            functools.partial(input_grad_kernel, shards, packs),
            "input_grad",
            pltpu.HBM(block_input.shape, jnp.bfloat16),
            [SCALARS] + [BLOCKS] * 3 + [IN_HBM] + [BLOCKS] * (2 * len(packs)),
            operands[:4] + (stay(operands[4]),) + operands[5:],
            scratch=[
                pltpu.VMEM((channels, max(pack.columns for pack in packs)), jnp.float32),
                pltpu.VMEM(block_input.shape, jnp.bfloat16),
                pltpu.VMEM(block_input.shape, jnp.bfloat16),
                pltpu.VMEM((tokens, channels), jnp.float32),
                pltpu.SemaphoreType.DMA((1 + samples,)),
            ],
            out_specs=IN_HBM,
            flops=2 * tokens * channels * channels,
            elements=tokens * channels,
        )

    def moments(*grads):
        return call(
            functools.partial(moments_kernel, packs),
            "moments",
            (jax.ShapeDtypeStruct(params.shape, jnp.float32),) * 2,
            [IN_HBM] * 2 + [BLOCKS] * len(packs),
            (stay(first_moment), stay(second_moment), *grads),
            scratch=[pltpu.VMEM(params.shape, jnp.float32)] * 2 + [pltpu.SemaphoreType.DMA((2,))],
            elements=rows * channels,
        )

    def from_behind(finish, *operands):
        def branch(distance):
            return lambda *values: finish(lambda block: moved_on(block, "replica", distance), *values)

        return lax.switch(distance_bits, [branch(1 << power) for power in range(level_count)], *operands)

    grad_input = input_grad(
        me, mean_in, inverse_in, same_group, block_input, *hidden_grads, *full_weights
    )
    arrived = scattered(parts, shards)
    early, late = packs

    def adam(pack, own, others, blocks):
        return call(
            functools.partial(adam_kernel, len(others), pack, pack is early),
            "adam",
            (pack.block(), pack.block(), pack.payload()),
            [SCALARS] + [BLOCKS] * (4 + len(others)),
            (scales, own, *others, *blocks),
            elements=rows * pack.columns,
        )

    grad_a, moved_a, sent_a = adam(early, owns[0], arrived[0], blocks[:3])

    def finish(move, sent, grad_a, moved_a, own, *operands):
        other_a = move(sent)
        grad_b, moved_b, sent_b = adam(late, own, operands[:-3], operands[-3:])
        other_b = move(sent_b)
        mean, weight = call(
            functools.partial(half_average_kernel, early),
            "half_average",
            (early.block(), jax.ShapeDtypeStruct((1,), jnp.float32)),
            [SCALARS] + [BLOCKS] * 2,
            (scales, moved_a, other_a),
            elements=rows * early.columns,
        )
        averaged = call(
            functools.partial(average_kernel, late),
            "average",
            pltpu.HBM(params.shape, jnp.float32),
            [BLOCKS] * 3,
            (mean, moved_b, other_b),
            scratch=[pltpu.VMEM(params.shape, jnp.float32), pltpu.SemaphoreType.DMA],
            out_specs=IN_HBM,
            elements=rows * channels,
        )
        return (*moments(grad_a, grad_b), averaged, weight)

    first_new, second_new, averaged, new_weight = from_behind(
        finish, sent_a, grad_a, moved_a, owns[1], *arrived[1], *blocks[3:]
    )
    return (
        grad_input,
        *(jnp.transpose(array, (1, 0, 2)) for array in (averaged, first_new, second_new)),
        new_weight,
    )


def solution(mesh):
    placed = (
        P(("replica", "dp"), None, None),
        P(("replica", "dp"), None),
        P(("replica", "dp"), None, None),
        P("replica", "dp", None),
        P("replica", "dp", None),
        P("replica", "dp", None),
        P("replica"),
        P(),
    )
    return jax.shard_map(
        local,
        mesh=mesh,
        in_specs=placed,
        out_specs=(
            P(("replica", "dp"), None, None),
            P("replica", "dp", None),
            P("replica", "dp", None),
            P("replica", "dp", None),
            P("replica"),
        ),
        check_vma=False,
    )
```

```python
import functools

import jax
import jax.numpy as jnp
from jax import lax
from jax.experimental import pallas as pl
from jax.experimental.pallas import tpu as pltpu
from jax.sharding import PartitionSpec as P

GSIZE = 40

NORM_EPS = 1e-05
BETA_ONE = 0.9
BETA_TWO = 0.999
LEARN_RATE = 0.002
ADAM_EPS = 1e-08

LANES = 128
ROW_STEP = 32
UNROLL = 3
TILE_ROWS = 16
VMEM_BYTES = 16 * 1024 * 1024


def padded(rows):
    return -(-rows // TILE_ROWS) * TILE_ROWS


def packed_rows(rows):
    return padded(rows + 1)


class Packing:
    def __init__(self, rows, start, stop):
        self.rows, self.start, self.stop = rows, start, stop
        self.columns = stop - start
        self.deep = packed_rows(rows)
        self.tiles, self.rest = divmod(self.columns, LANES)
        fold = LANES // self.rest if self.rest else 1
        self.fold_rows = padded(-(-self.deep // fold))
        self.folds = [
            (first, min(self.fold_rows, self.deep - first)) for first in range(0, self.deep, self.fold_rows)
        ]
        self.height = self.tiles * self.deep + (self.fold_rows if self.rest else 0)

    def write(self, ref, block):
        for tile in range(self.tiles):
            ref[tile * self.deep : (tile + 1) * self.deep, :] = block[
                :, tile * LANES : (tile + 1) * LANES
            ].astype(ref.dtype)
        if self.rest:
            left = block[:, self.tiles * LANES :]
            parts = []
            for first, count in self.folds:
                part = left[first : first + count]
                if count < self.fold_rows:
                    part = jnp.concatenate(
                        [part, jnp.zeros((self.fold_rows - count, self.rest), part.dtype)], axis=0
                    )
                parts.append(part)
            spare = LANES - self.rest * len(parts)
            if spare:
                parts.append(jnp.zeros((self.fold_rows, spare), left.dtype))
            ref[self.tiles * self.deep :, :] = jnp.concatenate(parts, axis=1).astype(ref.dtype)

    def read(self, ref):
        pieces = [
            ref[tile * self.deep : (tile + 1) * self.deep, :].astype(jnp.float32) for tile in range(self.tiles)
        ]
        if self.rest:
            left = ref[self.tiles * self.deep :, :].astype(jnp.float32)
            parts = [
                left[:count, i * self.rest : (i + 1) * self.rest] for i, (_, count) in enumerate(self.folds)
            ]
            pieces.append(jnp.concatenate(parts, axis=0) if len(parts) > 1 else parts[0])
        return jnp.concatenate(pieces, axis=1) if len(pieces) > 1 else pieces[0]

    def unpack(self, ref, out_ref, first_row):
        for tile in range(self.tiles):
            out_ref[first_row : first_row + self.deep, tile * LANES : (tile + 1) * LANES] = ref[
                tile * self.deep : (tile + 1) * self.deep, :
            ]
        if self.rest:
            left = ref[self.tiles * self.deep :, :]
            for i, (first, count) in enumerate(self.folds):
                out_ref[first_row + first : first_row + first + count, self.tiles * LANES :] = left[
                    :count, i * self.rest : (i + 1) * self.rest
                ]

    def payload(self):
        return jax.ShapeDtypeStruct((self.height, LANES), jnp.bfloat16)

    def block(self):
        return jax.ShapeDtypeStruct((self.deep, self.columns), jnp.float32)


def group_sums(rows, same_group):
    high = rows.astype(jnp.bfloat16).astype(jnp.float32)
    rest = rows - high
    middle = rest.astype(jnp.bfloat16).astype(jnp.float32)
    count = rows.shape[0]
    stacked = jnp.concatenate([high, middle, rest - middle], axis=0).astype(jnp.bfloat16)
    sums = jnp.dot(stacked, same_group, preferred_element_type=jnp.float32)
    return sums[:count] + (sums[count : 2 * count] + sums[2 * count :])


def table_sums(packs, rows, same_group):
    return jnp.concatenate(
        [
            group_sums(rows[:, pack.start : pack.stop], same_group[: pack.columns, : pack.columns])
            for pack in packs
        ],
        axis=1,
    )


def position_sums(parts):
    return jnp.concatenate([jnp.sum(part, axis=0, keepdims=True) for part in parts], axis=0)


def doubled_silu_grad(half, turned):
    return (1.0 + turned) + half * (1.0 - turned * turned)


def row(vector, i):
    return vector[i : i + 1]


def eight_sums(block):
    return sum(block[first : first + 8] for first in range(0, block.shape[0], 8))


def squares_sums(samples, positions, step, load, offset):
    sums = []
    for i in range(samples):

        def body(k, total):
            value = load(i, pl.multiple_of(k * step, step), step) + row(offset, i)
            return total + eight_sums(value * value)

        total = lax.fori_loop(0, positions // step, body, jnp.zeros((8, offset.shape[1]), jnp.float32), unroll=UNROLL)
        sums.append(jnp.sum(total, axis=0, keepdims=True))
    return jnp.concatenate(sums, axis=0)


def norm_back(table_mean, samples, positions, step, load, scales, offsets, inverse, incoming, kept_ref, store, stored):
    firsts, seconds = [], []
    zeros = jnp.zeros((8, scales.shape[1]), jnp.float32)
    for i in range(samples):

        def body(k, totals):
            first_row = pl.multiple_of(k * step, step)
            half = load(i, first_row, step) * row(scales, i) + row(offsets, i)
            doubled = incoming(i, first_row, step) * doubled_silu_grad(half, jnp.tanh(half))
            kept_ref[pl.ds(pl.multiple_of(i * positions + first_row, step), step), :] = doubled
            return totals[0] + eight_sums(doubled), totals[1] + eight_sums(doubled * half)

        first, second = lax.fori_loop(0, positions // step, body, (zeros, zeros), unroll=UNROLL)
        firsts.append(jnp.sum(first, axis=0, keepdims=True))
        seconds.append(jnp.sum(second, axis=0, keepdims=True))
    means = table_mean(jnp.concatenate(firsts + seconds, axis=0))
    first, second = 0.5 * means[:samples], means[samples:]
    gain = 0.5 * inverse
    slope = (2.0 * inverse) * second * scales
    level = inverse * (first + 2.0 * offsets * second)
    for i in range(samples):

        def body(k, carry):
            first_row = pl.multiple_of(k * step, step)
            doubled = kept_ref[pl.ds(pl.multiple_of(i * positions + first_row, step), step), :]
            value = load(i, first_row, step)
            store(i, first_row, step, doubled * row(gain, i) - (value * row(slope, i) + row(level, i)))
            return carry

        lax.fori_loop(0, positions // step, body, 0, unroll=UNROLL)
        stored(i)


def sigmoid(values):
    return 0.5 * jnp.tanh(0.5 * values) + 0.5


def silu_grad(values):
    gate = sigmoid(values)
    return gate * (1.0 + values * (1.0 - gate))


def cast_kernel(pack, push_ref, params_ref, token_ref, other_token_ref, out_ref, rows_ref):
    rows = pack.rows
    rows_ref[rows // 8 * 8 :, :] = jnp.zeros((pack.deep - rows // 8 * 8, pack.columns), jnp.float32)
    rows_ref[:rows, :] = params_ref[:, 0, pack.start : pack.stop] / push_ref[...]
    pack.write(out_ref, rows_ref[...])


def norm_in_kernel(shards, packs, me_ref, scales_ref, shift_ref, x_hbm, out_grad_hbm, *refs):
    act_ref, mean_ref, inverse_ref, same_group_ref = refs[:4]
    shift_refs, out_grad_refs = refs[4 : 4 + len(packs)], refs[4 + len(packs) : 4 + 2 * len(packs)]
    x_ref, out_grad_ref, sems = refs[4 + 2 * len(packs) :]
    copies = [
        pltpu.make_async_copy(x_hbm, x_ref, sems.at[0]),
        pltpu.make_async_copy(out_grad_hbm, out_grad_ref, sems.at[1]),
    ]
    for copy in copies:
        copy.start()
    samples, positions, channels = x_ref.shape
    rows = channels // shards
    deep = act_ref.shape[0] // shards
    entries = positions * GSIZE
    group_of_row = lax.broadcasted_iota(jnp.int32, same_group_ref.shape, 0) // GSIZE
    group_of_column = lax.broadcasted_iota(jnp.int32, same_group_ref.shape, 1) // GSIZE
    same_group_ref[...] = (group_of_row == group_of_column).astype(jnp.float32).astype(jnp.bfloat16)
    same_group = same_group_ref[...]
    for pack, shift_out in zip(packs, shift_refs):
        shift_out[...] = shift_ref[...].astype(jnp.float32)[:, pack.start : pack.stop]
    copies[0].wait()
    parts = [x_ref[i].astype(jnp.float32) for i in range(samples)]
    mean = table_sums(packs, position_sums(parts), same_group) / entries
    centered = [parts[i] - mean[i : i + 1] for i in range(samples)]
    variance = table_sums(packs, position_sums([part * part for part in centered]), same_group) / entries
    inverse = lax.rsqrt(variance + NORM_EPS)
    mean_ref[...] = mean
    inverse_ref[...] = inverse
    normed = [centered[i] * inverse[i : i + 1] for i in range(samples)]
    act = jnp.concatenate([part * sigmoid(part) for part in normed], axis=0).T
    for block in range(shards):
        slot = jnp.bitwise_xor(me_ref[0], block)
        act_ref[pl.ds(pl.multiple_of(slot * deep, TILE_ROWS), deep), :] = jnp.concatenate(
            [act[block * rows : (block + 1) * rows], jnp.zeros((deep - rows, act.shape[1]), jnp.float32)], axis=0
        ).astype(jnp.bfloat16)
    copies[1].wait()
    for pack, out_grad_out in zip(packs, out_grad_refs):
        for i in range(samples):
            out_grad_out[i] = out_grad_ref[i][:, pack.start : pack.stop]


def mix_kernel(shards, pack, slots, act_ref, shift_ref, out_grad_ref, same_group_ref, *refs):
    weight_refs, token_ref, refs = refs[:shards], refs[shards], refs[shards + 1 :]
    grad_hidden_ref, weight_out_ref = refs[:2]
    made_refs, refs = refs[2 : 2 + len(slots)], refs[2 + len(slots) :]
    weight_ref, kept_ref, hidden_ref, doubled_ref, sems = refs
    samples, positions, columns = out_grad_ref.shape
    entries = positions * GSIZE
    deep = pack.deep
    for slot, shard_ref in enumerate(weight_refs):
        pack.unpack(shard_ref, weight_ref, slot * deep)
    weight_copy = pltpu.make_async_copy(weight_ref, weight_out_ref, sems.at[0])
    weight_copy.start()
    same_group = same_group_ref[:columns, :columns]
    hidden_ref[...] = lax.dot_general(
        act_ref[...], weight_ref[...], (((0,), (0,)), ((), ())), preferred_element_type=jnp.float32
    )

    def table_mean(rows):
        return group_sums(rows, same_group) / entries

    def load(i, first_row, count):
        return hidden_ref[pl.ds(pl.multiple_of(i * positions + first_row, count), count), :]

    def incoming(i, first_row, count):
        return out_grad_ref[i, pl.ds(first_row, count), :].astype(jnp.float32)

    def store(i, first_row, count, grad):
        kept_ref[pl.ds(pl.multiple_of(i * positions + first_row, count), count), :] = grad.astype(jnp.bfloat16)

    shift = shift_ref[...]
    sums = position_sums([hidden_ref[i * positions : (i + 1) * positions, :] for i in range(samples)])
    offset = shift - table_mean(sums + positions * shift)
    squares = squares_sums(samples, positions, ROW_STEP, load, offset)
    inverse = lax.rsqrt(table_mean(squares) + NORM_EPS)
    scales = 0.5 * inverse
    norm_back(
        table_mean, samples, positions, ROW_STEP, load, scales, offset * scales, inverse, incoming, doubled_ref, store, lambda i: None
    )
    copy = pltpu.make_async_copy(kept_ref, grad_hidden_ref, sems.at[1])
    copy.start()
    weight_grads(pack, slots, act_ref, kept_ref, made_refs)
    weight_copy.wait()
    copy.wait()


def weight_grads(pack, slots, act_ref, grad_hidden_ref, made_refs):
    deep = pack.deep
    low, high = min(slots), max(slots) + 1
    grad = jnp.dot(act_ref[low * deep : high * deep, :], grad_hidden_ref[...], preferred_element_type=jnp.float32)
    for slot, made_ref in zip(slots, made_refs):
        block = grad[(slot - low) * deep : (slot - low + 1) * deep]
        if slot:
            pack.write(made_ref, block)
        else:
            made_ref[...] = block


def rest_kernel(pack, slots, act_ref, grad_hidden_ref, token_ref, *made_refs):
    weight_grads(pack, slots, act_ref, grad_hidden_ref, made_refs)


def input_grad_kernel(shards, packs, carried, me_ref, mean_ref, inverse_ref, same_group_ref, x_hbm, *refs):
    count = len(packs)
    grad_refs, weight_refs, refs = refs[:count], refs[count : 2 * count], refs[2 * count :]
    carried_hbms, out_ref, carried_refs = refs[:carried], refs[carried], refs[carried + 1 : 2 * carried + 1]
    rows_ref, x_ref, made_ref, act_ref, sems, carried_sems = refs[2 * carried + 1 :]
    copies = [pltpu.make_async_copy(x_hbm, x_ref, sems.at[0])]
    copies[0].start()
    carried_copies = [
        pltpu.make_async_copy(source, target, carried_sems.at[i])
        for i, (source, target) in enumerate(zip(carried_hbms, carried_refs))
    ]
    for copy in carried_copies:
        copy.start()
    samples, positions, channels = x_ref.shape
    entries = positions * GSIZE
    rows = channels // shards
    weights = []
    for index, (pack, weight_ref) in enumerate(zip(packs, weight_refs)):
        for block in range(shards):
            slot = jnp.bitwise_xor(me_ref[0], block)
            rows_ref[block * rows : (block + 1) * rows, : pack.columns] = weight_ref[
                pl.ds(pl.multiple_of(slot * pack.deep, TILE_ROWS), pack.deep), :
            ][:rows]
        weights.append(rows_ref[:, : pack.columns])
    grad_act = 0.0
    for index, (grad_ref, weight) in enumerate(zip(grad_refs, weights)):
        grad_act += lax.dot_general(
            grad_ref[...], weight, (((1,), (1,)), ((), ())), preferred_element_type=jnp.float32
        )
    act_ref[...] = grad_act
    copies[0].wait()
    same_group = same_group_ref[...]
    inverse = inverse_ref[...]

    def table_mean(rows):
        return table_sums(packs, rows, same_group) / entries

    def load(i, first_row, count):
        return x_ref[i, pl.ds(first_row, count), :].astype(jnp.float32)

    def incoming(i, first_row, count):
        return act_ref[pl.ds(pl.multiple_of(i * positions + first_row, count), count), :]

    def store(i, first_row, count, grad):
        made_ref[i, pl.ds(first_row, count), :] = grad.astype(jnp.bfloat16)

    def stored(i):
        copies.append(pltpu.make_async_copy(made_ref.at[i], out_ref.at[i], sems.at[len(copies)]))
        copies[-1].start()

    scales = 0.5 * inverse
    norm_back(
        table_mean, samples, positions, ROW_STEP // 2, load, scales, -mean_ref[...] * scales, inverse, incoming, act_ref, store, stored
    )
    for copy in carried_copies + copies[-samples:]:
        copy.wait()


def merge_kernel(one_ref, other_ref, *refs):
    count = (len(refs) - 1) // 2
    through_refs, out_ref, through_out_refs = refs[:count], refs[count], refs[count + 1 :]
    out_ref[...] = (one_ref[...].astype(jnp.float32) + other_ref[...].astype(jnp.float32)).astype(out_ref.dtype)
    for through_ref, through_out_ref in zip(through_refs, through_out_refs):
        through_out_ref[...] = through_ref[...]


def cut_kernel(packs, *refs):
    count = 3 * len(packs)
    hbm_refs, out_refs = refs[:3], refs[4 : 4 + count]
    row_refs, block_refs, sems = refs[4 + count : 7 + count], refs[7 + count : -1], refs[-1]
    copies = [
        pltpu.make_async_copy(source, target, sems.at[i])
        for i, (source, target) in enumerate(zip(hbm_refs, row_refs))
    ]
    for copy in copies:
        copy.start()
    out_copies = []
    for i, row_ref in enumerate(row_refs):
        copies[i].wait()
        for index, pack in enumerate(packs):
            place = 3 * index + i
            block_refs[place][...] = row_ref[:, 0, pack.start : pack.stop]
            out_copies.append(pltpu.make_async_copy(block_refs[place], out_refs[place], sems.at[3 + place]))
            out_copies[-1].start()
    for copy in out_copies:
        copy.wait()


def adam_kernel(count, pack, spare_value, scales_ref, own_ref, *refs):
    other_refs, refs = refs[:count], refs[count:]
    (params_ref, first_ref, second_ref), (grad_ref, moved_ref, sent_ref) = refs[:3], refs[-3:]
    rows = pack.rows
    total = own_ref[...]
    for other_ref in other_refs:
        total = total + pack.read(other_ref)
    grad_ref[...] = total * scales_ref[2]
    grad = grad_ref[:rows, :]
    first_new = BETA_ONE * first_ref[...] + (1.0 - BETA_ONE) * grad
    second_new = BETA_TWO * second_ref[...] + (1.0 - BETA_TWO) * grad * grad
    update = (scales_ref[0] * first_new) / (jnp.sqrt(second_new * scales_ref[1]) + ADAM_EPS)
    value = scales_ref[3] if spare_value else 0.0
    moved_ref[rows // 8 * 8 :, :] = jnp.full((pack.deep - rows // 8 * 8, pack.columns), value, jnp.float32)
    moved_ref[:rows, :] = params_ref[...] - update
    pack.write(sent_ref, moved_ref[...])


def half_average_kernel(pack, scales_ref, moved_ref, other_ref, mean_ref, push_out_ref):
    other = pack.read(other_ref)
    mean_ref[...] = 0.5 * (moved_ref[...] + other)
    push_out_ref[...] = 0.5 * (scales_ref[3] + other[pack.rows, :1])


def moments_kernel(packs, first_hbm, second_hbm, *refs):
    grad_refs, (first_out, second_out, first_ref, second_ref, sems) = refs[: len(packs)], refs[len(packs) :]
    copies = [
        pltpu.make_async_copy(first_hbm, first_ref, sems.at[0]),
        pltpu.make_async_copy(second_hbm, second_ref, sems.at[1]),
    ]
    for copy in copies:
        copy.start()
    rows = first_ref.shape[0]
    grad = jnp.concatenate([grad_ref[:rows, :] for grad_ref in grad_refs], axis=1)
    copies[0].wait()
    first_out[:, 0, :] = BETA_ONE * first_ref[:, 0, :] + (1.0 - BETA_ONE) * grad
    copies[1].wait()
    second_out[:, 0, :] = BETA_TWO * second_ref[:, 0, :] + (1.0 - BETA_TWO) * grad * grad


def average_kernel(pack, mean_ref, moved_ref, other_ref, out_ref, rows_ref, sem):
    rows = out_ref.shape[0]
    later = 0.5 * (moved_ref[...] + pack.read(other_ref))
    rows_ref[:, 0, :] = jnp.concatenate([mean_ref[...], later], axis=1)[:rows]
    copy = pltpu.make_async_copy(rows_ref, out_ref, sem)
    copy.start()
    copy.wait()


SCALARS = pl.BlockSpec(memory_space=pltpu.SMEM)
BLOCKS = pl.BlockSpec(memory_space=pltpu.VMEM)
TOKEN = pl.BlockSpec(memory_space=pl.ANY)
IN_HBM = pl.BlockSpec(memory_space=pltpu.HBM)


def call(kernel, name, outs, specs, operands, scratch=(), out_specs=None, flops=0, elements=0):
    return pl.pallas_call(
        kernel,
        out_shape=outs,
        in_specs=specs,
        out_specs=out_specs or jax.tree.map(lambda _: BLOCKS, outs),
        scratch_shapes=list(scratch),
        compiler_params=pltpu.CompilerParams(vmem_limit_bytes=VMEM_BYTES),
        cost_estimate=pl.CostEstimate(flops=flops, bytes_accessed=8 * elements, transcendentals=elements),
        name=name,
    )(*operands)


def stay(array):
    return pltpu.with_memory_space_constraint(array, pltpu.HBM)


def moved_on(block, axis, distance):
    size = lax.axis_size(axis)
    return lax.ppermute(block, axis, [(i, (i + distance) % size) for i in range(size)])


def exchanged(block, axis, bit):
    return lax.ppermute(block, axis, [(i, i ^ bit) for i in range(lax.axis_size(axis))])


def lowest_bit(slot):
    return slot & -slot


def hold_kernel(block_ref, token_ref, out_ref):
    out_ref[...] = block_ref[...]


def gathered(piece, shards, token=None):
    held = [piece]
    for slot in range(1, shards):
        bit = lowest_bit(slot)
        held.append(exchanged(held[slot ^ bit], "dp", bit))
        if token is not None and slot == 2:
            shape = jax.ShapeDtypeStruct(piece.shape, piece.dtype)
            held[slot] = call(hold_kernel, "hold", shape, [BLOCKS, IN_HBM], (held[slot], stay(token)))
    return held


def scattered(parts, shards):
    arrived, token = [], None
    for part, held in enumerate(parts):
        last = part == len(parts) - 1
        slots = sorted(range(2, shards), key=lambda slot: (-slot.bit_count(), -slot))
        got = [] if last else [exchanged(held[1], "dp", 1)]
        for slot in slots:
            bit = lowest_bit(slot)
            other = exchanged(held[slot], "dp", bit)
            if slot == bit:
                got.append(other)
                continue
            if None in held:
                held.update(held.pop(None)(token))
            shape = jax.ShapeDtypeStruct(other.shape, other.dtype)
            through = [held[1]] if last else []
            made = call(
                merge_kernel,
                "merge",
                (shape,) * (1 + len(through)),
                [BLOCKS] * (2 + len(through)),
                (held[slot ^ bit], other, *through),
            )
            held[slot ^ bit] = made[0]
            if last:
                held[1] = made[1]
        if last:
            got.append(exchanged(held[1], "dp", 1))
        else:
            token = got[0]
        arrived.append(got)
    return arrived


def column_cuts(channels):
    half = (channels // GSIZE + 1) // 2 * GSIZE
    return [(0, half), (half, channels)]


def local(
    block_input, time_shift, out_grad, params, first_moment, second_moment, push_weight, step
):
    samples, positions, channels = block_input.shape
    tokens = samples * positions
    shards = lax.axis_size("dp")
    rows = params.shape[1]
    deep = packed_rows(rows)
    me = lax.axis_index("dp").astype(jnp.int32).reshape(1)
    packs = [Packing(rows, start, stop) for start, stop in column_cuts(channels)]
    params, first_moment, second_moment = (
        jnp.transpose(array, (1, 0, 2)) for array in (params, first_moment, second_moment)
    )
    def shards_of(pack, *tokens, late=None):
        piece = call(
            functools.partial(cast_kernel, pack),
            "cast",
            pack.payload(),
            [BLOCKS, BLOCKS, TOKEN, TOKEN],
            (push_weight.reshape(1, 1), params, *tokens),
            scratch=[pltpu.VMEM((deep, pack.columns), jnp.float32)],
            elements=rows * pack.columns,
        )
        return gathered(piece, shards, late)

    level_count = lax.axis_size("replica").bit_length() - 1
    distance_bits = step[0] % level_count
    step_count = (step[0] + 1).astype(jnp.float32)
    scales = jnp.stack(
        [
            LEARN_RATE / (1.0 - jnp.power(BETA_ONE, step_count)),
            1.0 / (1.0 - jnp.power(BETA_TWO, step_count)),
            jnp.float32(1.0 / shards),
            push_weight[0],
        ]
    )

    activation, mean_in, inverse_in, same_group, *pieces = call(
        functools.partial(norm_in_kernel, shards, packs),
        "norm_in",
        (
            jax.ShapeDtypeStruct((shards * deep, tokens), jnp.bfloat16),
            jax.ShapeDtypeStruct((samples, channels), jnp.float32),
            jax.ShapeDtypeStruct((samples, channels), jnp.float32),
            jax.ShapeDtypeStruct((max(pack.columns for pack in packs),) * 2, jnp.bfloat16),
            *(jax.ShapeDtypeStruct((samples, pack.columns), jnp.float32) for pack in packs),
            *(jax.ShapeDtypeStruct((samples, positions, pack.columns), jnp.bfloat16) for pack in packs),
        ),
        [SCALARS, SCALARS, BLOCKS, IN_HBM, IN_HBM],
        (me, scales, time_shift, stay(block_input), stay(out_grad)),
        scratch=[
            pltpu.VMEM(block_input.shape, jnp.bfloat16),
            pltpu.VMEM(out_grad.shape, jnp.bfloat16),
            pltpu.SemaphoreType.DMA((2,)),
        ],
        elements=tokens * channels,
    )

    columns = [pack.columns for pack in packs for _ in range(3)]
    blocks = call(
        functools.partial(cut_kernel, packs),
        "cut",
        tuple(pltpu.HBM((rows, width), jnp.float32) for width in columns),
        [IN_HBM] * 3 + [TOKEN],
        (stay(params), stay(first_moment), stay(second_moment), mean_in),
        scratch=[pltpu.VMEM(params.shape, jnp.float32)] * 3
        + [pltpu.VMEM((rows, width), jnp.float32) for width in columns]
        + [pltpu.SemaphoreType.DMA((3 + len(columns),))],
        out_specs=(IN_HBM,) * len(columns),
        elements=rows * channels,
    )
    weights = [shards_of(packs[0], params, params)]
    weights.append(shards_of(packs[1], weights[0][1], mean_in, late=blocks[-1]))
    hidden_grads, full_weights, parts = [], [], []
    token = mean_in
    shifts, out_grads = pieces[: len(packs)], pieces[len(packs) :]
    for pack, shard_list, shift, out_grad_piece in zip(packs, weights, shifts, out_grads):
        kept = jax.ShapeDtypeStruct if pack is packs[-1] else pltpu.HBM
        kept_spec = BLOCKS if pack is packs[-1] else IN_HBM
        later = range(shards - 1) if pack is packs[-1] and shards > 2 else range(0)
        slots = [slot for slot in range(shards) if slot not in later]

        def made(slots, pack=pack):
            return tuple(pack.payload() if slot else pack.block() for slot in slots)

        grad_hidden, full_weight, *shares = call(
            functools.partial(mix_kernel, shards, pack, slots),
            "mix",
            (kept((tokens, pack.columns), jnp.bfloat16), kept((shards * deep, pack.columns), jnp.bfloat16))
            + made(slots),
            [BLOCKS] * (4 + shards) + [TOKEN],
            (activation, shift, out_grad_piece, same_group, *shard_list, token),
            scratch=[
                pltpu.VMEM((shards * deep, pack.columns), jnp.bfloat16),
                pltpu.VMEM((tokens, pack.columns), jnp.bfloat16),
                pltpu.VMEM((tokens, pack.columns), jnp.float32),
                pltpu.VMEM((tokens, pack.columns), jnp.float32),
                pltpu.SemaphoreType.DMA((2,)),
            ],
            out_specs=(kept_spec,) * 2 + (BLOCKS,) * len(slots),
            flops=4 * tokens * channels * pack.columns,
            elements=tokens * pack.columns,
        )
        shares = dict(zip(slots, shares))
        if later:
            def rest(token, pack=pack, later=tuple(later), outs=made(later), grad_hidden=grad_hidden):
                shares = call(
                    functools.partial(rest_kernel, pack, later),
                    "rest",
                    outs,
                    [BLOCKS] * 2 + [TOKEN],
                    (activation, grad_hidden, token),
                    flops=2 * tokens * channels * pack.columns,
                )
                return dict(zip(later, shares))

            shares[None] = rest
        token = shares[slots[-1]]
        hidden_grads.append(grad_hidden)
        full_weights.append(full_weight)
        parts.append(shares)

    def input_grad(carried, *operands):
        return call(
            functools.partial(input_grad_kernel, shards, packs, len(carried)),
            "input_grad",
            (pltpu.HBM(block_input.shape, jnp.bfloat16),)
            + tuple(jax.ShapeDtypeStruct(array.shape, array.dtype) for array in carried),
            [SCALARS] + [BLOCKS] * 3 + [IN_HBM] + [BLOCKS] * (2 * len(packs)) + [IN_HBM] * len(carried),
            operands[:4] + (stay(operands[4]),) + operands[5:] + tuple(map(stay, carried)),
            scratch=[
                pltpu.VMEM((channels, max(pack.columns for pack in packs)), jnp.bfloat16),
                pltpu.VMEM(block_input.shape, jnp.bfloat16),
                pltpu.VMEM(block_input.shape, jnp.bfloat16),
                pltpu.VMEM((tokens, channels), jnp.float32),
                pltpu.SemaphoreType.DMA((1 + samples,)),
                pltpu.SemaphoreType.DMA((len(carried),)),
            ],
            out_specs=(IN_HBM,) + (BLOCKS,) * len(carried),
            flops=2 * tokens * channels * channels,
            elements=tokens * channels,
        )

    def moments(*grads):
        return call(
            functools.partial(moments_kernel, packs),
            "moments",
            (jax.ShapeDtypeStruct(params.shape, jnp.float32),) * 2,
            [IN_HBM] * 2 + [BLOCKS] * len(packs),
            (stay(first_moment), stay(second_moment), *grads),
            scratch=[pltpu.VMEM(params.shape, jnp.float32)] * 2 + [pltpu.SemaphoreType.DMA((2,))],
            elements=rows * channels,
        )

    def from_behind(finish, *operands):
        def branch(distance):
            return lambda *values: finish(lambda block: moved_on(block, "replica", distance), *values)

        return lax.switch(distance_bits, [branch(1 << power) for power in range(level_count)], *operands)

    grad_input, *early_blocks = input_grad(
        blocks[:3], me, mean_in, inverse_in, same_group, block_input, *hidden_grads, *full_weights
    )
    arrived = scattered(parts, shards)
    owns = [shares[0] for shares in parts]
    early, late = packs

    def adam(pack, own, others, blocks):
        return call(
            functools.partial(adam_kernel, len(others), pack, pack is early),
            "adam",
            (pack.block(), pack.block(), pack.payload()),
            [SCALARS] + [BLOCKS] * (4 + len(others)),
            (scales, own, *others, *blocks),
            elements=rows * pack.columns,
        )

    grad_a, moved_a, sent_a = adam(early, owns[0], arrived[0], early_blocks)

    def finish(move, sent, grad_a, moved_a, own, *operands):
        other_a = move(sent)
        grad_b, moved_b, sent_b = adam(late, own, operands[:-3], operands[-3:])
        other_b = move(sent_b)
        mean, weight = call(
            functools.partial(half_average_kernel, early),
            "half_average",
            (early.block(), jax.ShapeDtypeStruct((1,), jnp.float32)),
            [SCALARS] + [BLOCKS] * 2,
            (scales, moved_a, other_a),
            elements=rows * early.columns,
        )
        averaged = call(
            functools.partial(average_kernel, late),
            "average",
            pltpu.HBM(params.shape, jnp.float32),
            [BLOCKS] * 3,
            (mean, moved_b, other_b),
            scratch=[pltpu.VMEM(params.shape, jnp.float32), pltpu.SemaphoreType.DMA],
            out_specs=IN_HBM,
            elements=rows * channels,
        )
        return (*moments(grad_a, grad_b), averaged, weight)

    first_new, second_new, averaged, new_weight = from_behind(
        finish, sent_a, grad_a, moved_a, owns[1], *arrived[1], *blocks[3:]
    )
    return (
        grad_input,
        *(jnp.transpose(array, (1, 0, 2)) for array in (averaged, first_new, second_new)),
        new_weight,
    )


def solution(mesh):
    placed = (
        P(("replica", "dp"), None, None),
        P(("replica", "dp"), None),
        P(("replica", "dp"), None, None),
        P("replica", "dp", None),
        P("replica", "dp", None),
        P("replica", "dp", None),
        P("replica"),
        P(),
    )
    return jax.shard_map(
        local,
        mesh=mesh,
        in_specs=placed,
        out_specs=(
            P(("replica", "dp"), None, None),
            P("replica", "dp", None),
            P("replica", "dp", None),
            P("replica", "dp", None),
            P("replica"),
        ),
        check_vma=False,
    )
```

```python
import functools
import math

import jax
import jax.numpy as jnp
from jax import lax
from jax.experimental import pallas as pl
from jax.experimental.pallas import tpu as pltpu
from jax.sharding import PartitionSpec as P

GSIZE = 40

NORM_EPS = 1e-05
BETA_ONE = 0.9
BETA_TWO = 0.999
LEARN_RATE = 0.002
ADAM_EPS = 1e-08

LANES = 128
ROW_STEP = 32
UNROLL = 3
TILE_ROWS = 16
VMEM_BYTES = 16 * 1024 * 1024


def padded(rows):
    return -(-rows // TILE_ROWS) * TILE_ROWS


def packed_rows(rows):
    return padded(rows + 1)


class Packing:
    def __init__(self, rows, start, stop):
        self.rows, self.start, self.stop = rows, start, stop
        self.columns = stop - start
        self.deep = packed_rows(rows)
        self.tiles, self.rest = divmod(self.columns, LANES)
        fold = LANES // self.rest if self.rest else 1
        self.fold_rows = padded(-(-self.deep // fold))
        self.folds = [
            (first, min(self.fold_rows, self.deep - first)) for first in range(0, self.deep, self.fold_rows)
        ]
        self.height = self.tiles * self.deep + (self.fold_rows if self.rest else 0)

    def write(self, ref, block):
        for tile in range(self.tiles):
            ref[tile * self.deep : (tile + 1) * self.deep, :] = block[
                :, tile * LANES : (tile + 1) * LANES
            ].astype(ref.dtype)
        if self.rest:
            left = block[:, self.tiles * LANES :]
            parts = []
            for first, count in self.folds:
                part = left[first : first + count]
                if count < self.fold_rows:
                    part = jnp.concatenate(
                        [part, jnp.zeros((self.fold_rows - count, self.rest), part.dtype)], axis=0
                    )
                parts.append(part)
            spare = LANES - self.rest * len(parts)
            if spare:
                parts.append(jnp.zeros((self.fold_rows, spare), left.dtype))
            ref[self.tiles * self.deep :, :] = jnp.concatenate(parts, axis=1).astype(ref.dtype)

    def read(self, ref):
        pieces = [
            ref[tile * self.deep : (tile + 1) * self.deep, :].astype(jnp.float32) for tile in range(self.tiles)
        ]
        if self.rest:
            left = ref[self.tiles * self.deep :, :].astype(jnp.float32)
            parts = [
                left[:count, i * self.rest : (i + 1) * self.rest] for i, (_, count) in enumerate(self.folds)
            ]
            pieces.append(jnp.concatenate(parts, axis=0) if len(parts) > 1 else parts[0])
        return jnp.concatenate(pieces, axis=1) if len(pieces) > 1 else pieces[0]

    def unpack(self, ref, out_ref, first_row):
        for tile in range(self.tiles):
            out_ref[first_row : first_row + self.deep, tile * LANES : (tile + 1) * LANES] = ref[
                tile * self.deep : (tile + 1) * self.deep, :
            ]
        if self.rest:
            left = ref[self.tiles * self.deep :, :]
            for i, (first, count) in enumerate(self.folds):
                out_ref[first_row + first : first_row + first + count, self.tiles * LANES :] = left[
                    :count, i * self.rest : (i + 1) * self.rest
                ]

    def payload(self):
        return jax.ShapeDtypeStruct((self.height, LANES), jnp.bfloat16)

    def block(self):
        return jax.ShapeDtypeStruct((self.deep, self.columns), jnp.float32)


def group_sums(rows, same_group):
    high = rows.astype(jnp.bfloat16).astype(jnp.float32)
    rest = rows - high
    middle = rest.astype(jnp.bfloat16).astype(jnp.float32)
    count = rows.shape[0]
    stacked = jnp.concatenate([high, middle, rest - middle], axis=0).astype(jnp.bfloat16)
    sums = jnp.dot(stacked, same_group, preferred_element_type=jnp.float32)
    return sums[:count] + (sums[count : 2 * count] + sums[2 * count :])


def table_sums(packs, rows, same_group):
    return jnp.concatenate(
        [
            group_sums(rows[:, pack.start : pack.stop], same_group[: pack.columns, : pack.columns])
            for pack in packs
        ],
        axis=1,
    )


def position_sums(parts):
    return jnp.concatenate([jnp.sum(part, axis=0, keepdims=True) for part in parts], axis=0)


def doubled_silu_grad(half, turned):
    return (1.0 + turned) + half * (1.0 - turned * turned)


def row(vector, i):
    return vector[i : i + 1]


def eight_sums(block):
    return sum(block[first : first + 8] for first in range(0, block.shape[0], 8))


def squares_sums(samples, positions, step, load, offset):
    sums = []
    for i in range(samples):

        def body(k, total):
            value = load(i, pl.multiple_of(k * step, step), step) + row(offset, i)
            return total + eight_sums(value * value)

        total = lax.fori_loop(0, positions // step, body, jnp.zeros((8, offset.shape[1]), jnp.float32), unroll=UNROLL)
        sums.append(jnp.sum(total, axis=0, keepdims=True))
    return jnp.concatenate(sums, axis=0)


def norm_back(table_mean, samples, positions, step, load, scales, offsets, inverse, incoming, kept_ref, store, stored):
    firsts, seconds = [], []
    zeros = jnp.zeros((8, scales.shape[1]), jnp.float32)
    for i in range(samples):

        def body(k, totals):
            first_row = pl.multiple_of(k * step, step)
            half = load(i, first_row, step) * row(scales, i) + row(offsets, i)
            doubled = incoming(i, first_row, step) * doubled_silu_grad(half, jnp.tanh(half))
            kept_ref[pl.ds(pl.multiple_of(i * positions + first_row, step), step), :] = doubled
            return totals[0] + eight_sums(doubled), totals[1] + eight_sums(doubled * half)

        first, second = lax.fori_loop(0, positions // step, body, (zeros, zeros), unroll=UNROLL)
        firsts.append(jnp.sum(first, axis=0, keepdims=True))
        seconds.append(jnp.sum(second, axis=0, keepdims=True))
    means = table_mean(jnp.concatenate(firsts + seconds, axis=0))
    first, second = 0.5 * means[:samples], means[samples:]
    gain = 0.5 * inverse
    slope = (2.0 * inverse) * second * scales
    level = inverse * (first + 2.0 * offsets * second)
    for i in range(samples):

        def body(k, carry):
            first_row = pl.multiple_of(k * step, step)
            doubled = kept_ref[pl.ds(pl.multiple_of(i * positions + first_row, step), step), :]
            value = load(i, first_row, step)
            store(i, first_row, step, doubled * row(gain, i) - (value * row(slope, i) + row(level, i)))
            return carry

        lax.fori_loop(0, positions // step, body, 0, unroll=UNROLL)
        stored(i)


def sigmoid(values):
    return 0.5 * jnp.tanh(0.5 * values) + 0.5


def cast_kernel(pack, push_ref, params_ref, token_ref, other_token_ref, out_ref, rows_ref):
    rows = pack.rows
    rows_ref[rows // 8 * 8 :, :] = jnp.zeros((pack.deep - rows // 8 * 8, pack.columns), jnp.float32)
    rows_ref[:rows, :] = params_ref[:, 0, pack.start : pack.stop] / push_ref[...]
    pack.write(out_ref, rows_ref[...])


def norm_in_kernel(shards, packs, me_ref, scales_ref, shift_ref, x_hbm, out_grad_hbm, *refs):
    act_ref, mean_ref, inverse_ref, same_group_ref = refs[:4]
    shift_refs, out_grad_refs = refs[4 : 4 + len(packs)], refs[4 + len(packs) : 4 + 2 * len(packs)]
    x_ref, out_grad_ref, sems = refs[4 + 2 * len(packs) :]
    copies = [
        pltpu.make_async_copy(x_hbm, x_ref, sems.at[0]),
        pltpu.make_async_copy(out_grad_hbm, out_grad_ref, sems.at[1]),
    ]
    for copy in copies:
        copy.start()
    samples, positions, channels = x_ref.shape
    rows = channels // shards
    deep = act_ref.shape[0] // shards
    entries = positions * GSIZE
    group_of_row = lax.broadcasted_iota(jnp.int32, same_group_ref.shape, 0) // GSIZE
    group_of_column = lax.broadcasted_iota(jnp.int32, same_group_ref.shape, 1) // GSIZE
    same_group_ref[...] = (group_of_row == group_of_column).astype(jnp.float32).astype(jnp.bfloat16)
    same_group = same_group_ref[...]
    for pack, shift_out in zip(packs, shift_refs):
        shift_out[...] = shift_ref[...].astype(jnp.float32)[:, pack.start : pack.stop]
    copies[0].wait()
    parts = [x_ref[i].astype(jnp.float32) for i in range(samples)]
    mean = table_sums(packs, position_sums(parts), same_group) / entries
    centered = [parts[i] - mean[i : i + 1] for i in range(samples)]
    variance = table_sums(packs, position_sums([part * part for part in centered]), same_group) / entries
    inverse = lax.rsqrt(variance + NORM_EPS)
    mean_ref[...] = mean
    inverse_ref[...] = inverse
    normed = [centered[i] * inverse[i : i + 1] for i in range(samples)]
    act = jnp.concatenate([part * sigmoid(part) for part in normed], axis=0).T
    for block in range(shards):
        slot = jnp.bitwise_xor(me_ref[0], block)
        act_ref[pl.ds(pl.multiple_of(slot * deep, TILE_ROWS), deep), :] = jnp.concatenate(
            [act[block * rows : (block + 1) * rows], jnp.zeros((deep - rows, act.shape[1]), jnp.float32)], axis=0
        ).astype(jnp.bfloat16)
    copies[1].wait()
    for pack, out_grad_out in zip(packs, out_grad_refs):
        for i in range(samples):
            out_grad_out[i] = out_grad_ref[i][:, pack.start : pack.stop]


def mix_kernel(shards, pack, slots, act_ref, shift_ref, out_grad_ref, same_group_ref, *refs):
    weight_refs, token_ref, refs = refs[:shards], refs[shards], refs[shards + 1 :]
    grad_hidden_ref, weight_out_ref = refs[:2]
    made_refs, refs = refs[2 : 2 + len(slots)], refs[2 + len(slots) :]
    weight_ref, kept_ref, hidden_ref, doubled_ref, sems = refs
    samples, positions, columns = out_grad_ref.shape
    entries = positions * GSIZE
    deep = pack.deep
    for slot, shard_ref in enumerate(weight_refs):
        pack.unpack(shard_ref, weight_ref, slot * deep)
    weight_copy = pltpu.make_async_copy(weight_ref, weight_out_ref, sems.at[0])
    weight_copy.start()
    same_group = same_group_ref[:columns, :columns]
    hidden_ref[...] = lax.dot_general(
        act_ref[...], weight_ref[...], (((0,), (0,)), ((), ())), preferred_element_type=jnp.float32
    )

    def table_mean(rows):
        return group_sums(rows, same_group) / entries

    def load(i, first_row, count):
        return hidden_ref[pl.ds(pl.multiple_of(i * positions + first_row, count), count), :]

    def incoming(i, first_row, count):
        return out_grad_ref[i, pl.ds(first_row, count), :].astype(jnp.float32)

    def store(i, first_row, count, grad):
        kept_ref[pl.ds(pl.multiple_of(i * positions + first_row, count), count), :] = grad.astype(jnp.bfloat16)

    shift = shift_ref[...]
    sums = position_sums([hidden_ref[i * positions : (i + 1) * positions, :] for i in range(samples)])
    offset = shift - table_mean(sums + positions * shift)
    squares = squares_sums(samples, positions, math.gcd(positions, ROW_STEP), load, offset)
    inverse = lax.rsqrt(table_mean(squares) + NORM_EPS)
    scales = 0.5 * inverse
    norm_back(
        table_mean,
        samples,
        positions,
        math.gcd(positions, ROW_STEP),
        load,
        scales,
        offset * scales,
        inverse,
        incoming,
        doubled_ref,
        store,
        lambda i: None,
    )
    copy = pltpu.make_async_copy(kept_ref, grad_hidden_ref, sems.at[1])
    copy.start()
    weight_grads(pack, slots, act_ref, kept_ref, made_refs)
    weight_copy.wait()
    copy.wait()


def weight_grads(pack, slots, act_ref, grad_hidden_ref, made_refs):
    deep = pack.deep
    low, high = min(slots), max(slots) + 1
    grad = jnp.dot(act_ref[low * deep : high * deep, :], grad_hidden_ref[...], preferred_element_type=jnp.float32)
    for slot, made_ref in zip(slots, made_refs):
        block = grad[(slot - low) * deep : (slot - low + 1) * deep]
        if slot:
            pack.write(made_ref, block)
        else:
            made_ref[...] = block


def rest_kernel(pack, slots, act_ref, grad_hidden_ref, token_ref, *made_refs):
    weight_grads(pack, slots, act_ref, grad_hidden_ref, made_refs)


def input_grad_kernel(shards, packs, carried, me_ref, mean_ref, inverse_ref, same_group_ref, x_hbm, *refs):
    count = len(packs)
    grad_refs, weight_refs, refs = refs[:count], refs[count : 2 * count], refs[2 * count :]
    carried_hbms, out_ref, carried_refs = refs[:carried], refs[carried], refs[carried + 1 : 2 * carried + 1]
    rows_ref, x_ref, made_ref, act_ref, sems, carried_sems = refs[2 * carried + 1 :]
    copies = [pltpu.make_async_copy(x_hbm, x_ref, sems.at[0])]
    copies[0].start()
    carried_copies = [
        pltpu.make_async_copy(source, target, carried_sems.at[i])
        for i, (source, target) in enumerate(zip(carried_hbms, carried_refs))
    ]
    for copy in carried_copies:
        copy.start()
    samples, positions, channels = x_ref.shape
    entries = positions * GSIZE
    rows = channels // shards
    weights = []
    for index, (pack, weight_ref) in enumerate(zip(packs, weight_refs)):
        for block in range(shards):
            slot = jnp.bitwise_xor(me_ref[0], block)
            rows_ref[block * rows : (block + 1) * rows, : pack.columns] = weight_ref[
                pl.ds(pl.multiple_of(slot * pack.deep, TILE_ROWS), pack.deep), :
            ].astype(jnp.float32)[:rows]
        weights.append(rows_ref[:, : pack.columns].astype(jnp.bfloat16))
    grad_act = 0.0
    for index, (grad_ref, weight) in enumerate(zip(grad_refs, weights)):
        grad_act += lax.dot_general(
            grad_ref[...], weight, (((1,), (1,)), ((), ())), preferred_element_type=jnp.float32
        )
    act_ref[...] = grad_act
    copies[0].wait()
    same_group = same_group_ref[...]
    inverse = inverse_ref[...]

    def table_mean(rows):
        return table_sums(packs, rows, same_group) / entries

    def load(i, first_row, count):
        return x_ref[i, pl.ds(first_row, count), :].astype(jnp.float32)

    def incoming(i, first_row, count):
        return act_ref[pl.ds(pl.multiple_of(i * positions + first_row, count), count), :]

    def store(i, first_row, count, grad):
        made_ref[i, pl.ds(first_row, count), :] = grad.astype(jnp.bfloat16)

    def stored(i):
        copies.append(pltpu.make_async_copy(made_ref.at[i], out_ref.at[i], sems.at[len(copies)]))
        copies[-1].start()

    scales = 0.5 * inverse
    norm_back(
        table_mean, samples, positions, math.gcd(positions, ROW_STEP // 2), load, scales, -mean_ref[...] * scales, inverse, incoming, act_ref, store, stored
    )
    for copy in carried_copies + copies[-samples:]:
        copy.wait()


def merge_kernel(one_ref, other_ref, *refs):
    count = (len(refs) - 1) // 2
    through_refs, out_ref, through_out_refs = refs[:count], refs[count], refs[count + 1 :]
    out_ref[...] = (one_ref[...].astype(jnp.float32) + other_ref[...].astype(jnp.float32)).astype(out_ref.dtype)
    for through_ref, through_out_ref in zip(through_refs, through_out_refs):
        through_out_ref[...] = through_ref[...]


def cut_kernel(packs, *refs):
    count = 3 * len(packs)
    hbm_refs, out_refs = refs[:3], refs[4 : 4 + count]
    row_refs, block_refs, sems = refs[4 + count : 7 + count], refs[7 + count : -1], refs[-1]
    copies = [
        pltpu.make_async_copy(source, target, sems.at[i])
        for i, (source, target) in enumerate(zip(hbm_refs, row_refs))
    ]
    for copy in copies:
        copy.start()
    out_copies = []
    for i, row_ref in enumerate(row_refs):
        copies[i].wait()
        for index, pack in enumerate(packs):
            place = 3 * index + i
            block_refs[place][...] = row_ref[:, 0, pack.start : pack.stop]
            out_copies.append(pltpu.make_async_copy(block_refs[place], out_refs[place], sems.at[3 + place]))
            out_copies[-1].start()
    for copy in out_copies:
        copy.wait()


def adam_kernel(count, pack, spare_value, scales_ref, own_ref, *refs):
    other_refs, refs = refs[:count], refs[count:]
    (params_ref, first_ref, second_ref), (grad_ref, moved_ref, sent_ref) = refs[:3], refs[-3:]
    rows = pack.rows
    total = own_ref[...]
    for other_ref in other_refs:
        total = total + pack.read(other_ref)
    grad_ref[...] = total * scales_ref[2]
    grad = grad_ref[:rows, :]
    first_new = BETA_ONE * first_ref[...] + (1.0 - BETA_ONE) * grad
    second_new = BETA_TWO * second_ref[...] + (1.0 - BETA_TWO) * grad * grad
    update = (scales_ref[0] * first_new) / (jnp.sqrt(second_new * scales_ref[1]) + ADAM_EPS)
    value = scales_ref[3] if spare_value else 0.0
    moved_ref[rows // 8 * 8 :, :] = jnp.full((pack.deep - rows // 8 * 8, pack.columns), value, jnp.float32)
    moved_ref[:rows, :] = params_ref[...] - update
    pack.write(sent_ref, moved_ref[...])


def half_average_kernel(pack, scales_ref, moved_ref, other_ref, mean_ref, push_out_ref):
    other = pack.read(other_ref)
    mean_ref[...] = 0.5 * (moved_ref[...] + other)
    push_out_ref[...] = 0.5 * (scales_ref[3] + other[pack.rows, :1])


def moments_kernel(packs, first_hbm, second_hbm, *refs):
    grad_refs, (first_out, second_out, first_ref, second_ref, sems) = refs[: len(packs)], refs[len(packs) :]
    copies = [
        pltpu.make_async_copy(first_hbm, first_ref, sems.at[0]),
        pltpu.make_async_copy(second_hbm, second_ref, sems.at[1]),
    ]
    for copy in copies:
        copy.start()
    rows = first_ref.shape[0]
    grad = jnp.concatenate([grad_ref[:rows, :] for grad_ref in grad_refs], axis=1)
    copies[0].wait()
    first_out[:, 0, :] = BETA_ONE * first_ref[:, 0, :] + (1.0 - BETA_ONE) * grad
    copies[1].wait()
    second_out[:, 0, :] = BETA_TWO * second_ref[:, 0, :] + (1.0 - BETA_TWO) * grad * grad


def average_kernel(pack, mean_ref, moved_ref, other_ref, out_ref, rows_ref, sem):
    rows = out_ref.shape[0]
    later = 0.5 * (moved_ref[...] + pack.read(other_ref))
    rows_ref[:, 0, :] = jnp.concatenate([mean_ref[...], later], axis=1)[:rows]
    copy = pltpu.make_async_copy(rows_ref, out_ref, sem)
    copy.start()
    copy.wait()


SCALARS = pl.BlockSpec(memory_space=pltpu.SMEM)
BLOCKS = pl.BlockSpec(memory_space=pltpu.VMEM)
TOKEN = pl.BlockSpec(memory_space=pl.ANY)
IN_HBM = pl.BlockSpec(memory_space=pltpu.HBM)


def call(kernel, name, outs, specs, operands, scratch=(), out_specs=None, flops=0, elements=0):
    return pl.pallas_call(
        kernel,
        out_shape=outs,
        in_specs=specs,
        out_specs=out_specs or jax.tree.map(lambda _: BLOCKS, outs),
        scratch_shapes=list(scratch),
        compiler_params=pltpu.CompilerParams(vmem_limit_bytes=VMEM_BYTES),
        cost_estimate=pl.CostEstimate(flops=flops, bytes_accessed=8 * elements, transcendentals=elements),
        name=name,
    )(*operands)


def stay(array):
    return pltpu.with_memory_space_constraint(array, pltpu.HBM)


def moved_on(block, axis, distance):
    size = lax.axis_size(axis)
    return lax.ppermute(block, axis, [(i, (i + distance) % size) for i in range(size)])


def exchanged(block, axis, bit):
    return lax.ppermute(block, axis, [(i, i ^ bit) for i in range(lax.axis_size(axis))])


def lowest_bit(slot):
    return slot & -slot


def hold_kernel(block_ref, token_ref, out_ref):
    out_ref[...] = block_ref[...]


def gathered(piece, shards, token=None):
    held = [piece]
    for slot in range(1, shards):
        bit = lowest_bit(slot)
        held.append(exchanged(held[slot ^ bit], "dp", bit))
        if token is not None and slot == 2:
            shape = jax.ShapeDtypeStruct(piece.shape, piece.dtype)
            held[slot] = call(hold_kernel, "hold", shape, [BLOCKS, IN_HBM], (held[slot], stay(token)))
    return held


def scattered(parts, shards):
    arrived, token = [], None
    for part, held in enumerate(parts):
        last = part == len(parts) - 1
        slots = sorted(range(2, shards), key=lambda slot: (-slot.bit_count(), -slot))
        got = [] if last else [exchanged(held[1], "dp", 1)]
        for slot in slots:
            bit = lowest_bit(slot)
            other = exchanged(held[slot], "dp", bit)
            if slot == bit:
                got.append(other)
                continue
            if None in held:
                held.update(held.pop(None)(token))
            shape = jax.ShapeDtypeStruct(other.shape, other.dtype)
            through = [held[1]] if last else []
            made = call(
                merge_kernel,
                "merge",
                (shape,) * (1 + len(through)),
                [BLOCKS] * (2 + len(through)),
                (held[slot ^ bit], other, *through),
            )
            held[slot ^ bit] = made[0]
            if last:
                held[1] = made[1]
        if last:
            got.append(exchanged(held[1], "dp", 1))
        else:
            token = got[0]
        arrived.append(got)
    return arrived


def column_cuts(channels):
    half = (channels // GSIZE + 1) // 2 * GSIZE
    return [(0, half), (half, channels)]


def local(
    block_input, time_shift, out_grad, params, first_moment, second_moment, push_weight, step
):
    samples, positions, channels = block_input.shape
    tokens = samples * positions
    shards = lax.axis_size("dp")
    rows = params.shape[1]
    deep = packed_rows(rows)
    me = lax.axis_index("dp").astype(jnp.int32).reshape(1)
    packs = [Packing(rows, start, stop) for start, stop in column_cuts(channels)]
    params, first_moment, second_moment = (
        jnp.transpose(array, (1, 0, 2)) for array in (params, first_moment, second_moment)
    )
    def shards_of(pack, *tokens, late=None):
        piece = call(
            functools.partial(cast_kernel, pack),
            "cast",
            pack.payload(),
            [BLOCKS, BLOCKS, TOKEN, TOKEN],
            (push_weight.reshape(1, 1), params, *tokens),
            scratch=[pltpu.VMEM((deep, pack.columns), jnp.float32)],
            elements=rows * pack.columns,
        )
        return gathered(piece, shards, late)

    level_count = lax.axis_size("replica").bit_length() - 1
    distance_bits = step[0] % level_count
    step_count = (step[0] + 1).astype(jnp.float32)
    scales = jnp.stack(
        [
            LEARN_RATE / (1.0 - jnp.power(BETA_ONE, step_count)),
            1.0 / (1.0 - jnp.power(BETA_TWO, step_count)),
            jnp.float32(1.0 / shards),
            push_weight[0],
        ]
    )

    activation, mean_in, inverse_in, same_group, *pieces = call(
        functools.partial(norm_in_kernel, shards, packs),
        "norm_in",
        (
            jax.ShapeDtypeStruct((shards * deep, tokens), jnp.bfloat16),
            jax.ShapeDtypeStruct((samples, channels), jnp.float32),
            jax.ShapeDtypeStruct((samples, channels), jnp.float32),
            jax.ShapeDtypeStruct((max(pack.columns for pack in packs),) * 2, jnp.bfloat16),
            *(jax.ShapeDtypeStruct((samples, pack.columns), jnp.float32) for pack in packs),
            *(jax.ShapeDtypeStruct((samples, positions, pack.columns), jnp.bfloat16) for pack in packs),
        ),
        [SCALARS, SCALARS, BLOCKS, IN_HBM, IN_HBM],
        (me, scales, time_shift, stay(block_input), stay(out_grad)),
        scratch=[
            pltpu.VMEM(block_input.shape, jnp.bfloat16),
            pltpu.VMEM(out_grad.shape, jnp.bfloat16),
            pltpu.SemaphoreType.DMA((2,)),
        ],
        elements=tokens * channels,
    )

    columns = [pack.columns for pack in packs for _ in range(3)]
    blocks = call(
        functools.partial(cut_kernel, packs),
        "cut",
        tuple(pltpu.HBM((rows, width), jnp.float32) for width in columns),
        [IN_HBM] * 3 + [TOKEN],
        (stay(params), stay(first_moment), stay(second_moment), mean_in),
        scratch=[pltpu.VMEM(params.shape, jnp.float32)] * 3
        + [pltpu.VMEM((rows, width), jnp.float32) for width in columns]
        + [pltpu.SemaphoreType.DMA((3 + len(columns),))],
        out_specs=(IN_HBM,) * len(columns),
        elements=rows * channels,
    )
    weights = [shards_of(packs[0], params, params)]
    weights.append(shards_of(packs[1], weights[0][1], mean_in, late=blocks[-1]))
    hidden_grads, full_weights, parts = [], [], []
    token = mean_in
    shifts, out_grads = pieces[: len(packs)], pieces[len(packs) :]
    for pack, shard_list, shift, out_grad_piece in zip(packs, weights, shifts, out_grads):
        kept = jax.ShapeDtypeStruct if pack is packs[-1] else pltpu.HBM
        kept_spec = BLOCKS if pack is packs[-1] else IN_HBM
        later = range(shards - 1) if pack is packs[-1] and shards > 2 else range(0)
        slots = [slot for slot in range(shards) if slot not in later]

        def made(slots, pack=pack):
            return tuple(pack.payload() if slot else pack.block() for slot in slots)

        grad_hidden, full_weight, *shares = call(
            functools.partial(mix_kernel, shards, pack, slots),
            "mix",
            (kept((tokens, pack.columns), jnp.bfloat16), kept((shards * deep, pack.columns), jnp.bfloat16))
            + made(slots),
            [BLOCKS] * (4 + shards) + [TOKEN],
            (activation, shift, out_grad_piece, same_group, *shard_list, token),
            scratch=[
                pltpu.VMEM((shards * deep, pack.columns), jnp.bfloat16),
                pltpu.VMEM((tokens, pack.columns), jnp.bfloat16),
                pltpu.VMEM((tokens, pack.columns), jnp.float32),
                pltpu.VMEM((tokens, pack.columns), jnp.float32),
                pltpu.SemaphoreType.DMA((2,)),
            ],
            out_specs=(kept_spec,) * 2 + (BLOCKS,) * len(slots),
            flops=4 * tokens * channels * pack.columns,
            elements=tokens * pack.columns,
        )
        shares = dict(zip(slots, shares))
        if later:
            def rest(token, pack=pack, later=tuple(later), outs=made(later), grad_hidden=grad_hidden):
                shares = call(
                    functools.partial(rest_kernel, pack, later),
                    "rest",
                    outs,
                    [BLOCKS] * 2 + [TOKEN],
                    (activation, grad_hidden, token),
                    flops=2 * tokens * channels * pack.columns,
                )
                return dict(zip(later, shares))

            shares[None] = rest
        token = shares[slots[-1]]
        hidden_grads.append(grad_hidden)
        full_weights.append(full_weight)
        parts.append(shares)

    def input_grad(carried, *operands):
        return call(
            functools.partial(input_grad_kernel, shards, packs, len(carried)),
            "input_grad",
            (pltpu.HBM(block_input.shape, jnp.bfloat16),)
            + tuple(jax.ShapeDtypeStruct(array.shape, array.dtype) for array in carried),
            [SCALARS] + [BLOCKS] * 3 + [IN_HBM] + [BLOCKS] * (2 * len(packs)) + [IN_HBM] * len(carried),
            operands[:4] + (stay(operands[4]),) + operands[5:] + tuple(map(stay, carried)),
            scratch=[
                pltpu.VMEM((channels, max(pack.columns for pack in packs)), jnp.float32),
                pltpu.VMEM(block_input.shape, jnp.bfloat16),
                pltpu.VMEM(block_input.shape, jnp.bfloat16),
                pltpu.VMEM((tokens, channels), jnp.float32),
                pltpu.SemaphoreType.DMA((1 + samples,)),
                pltpu.SemaphoreType.DMA((len(carried),)),
            ],
            out_specs=(IN_HBM,) + (BLOCKS,) * len(carried),
            flops=2 * tokens * channels * channels,
            elements=tokens * channels,
        )

    def moments(*grads):
        return call(
            functools.partial(moments_kernel, packs),
            "moments",
            (jax.ShapeDtypeStruct(params.shape, jnp.float32),) * 2,
            [IN_HBM] * 2 + [BLOCKS] * len(packs),
            (stay(first_moment), stay(second_moment), *grads),
            scratch=[pltpu.VMEM(params.shape, jnp.float32)] * 2 + [pltpu.SemaphoreType.DMA((2,))],
            elements=rows * channels,
        )

    def from_behind(finish, *operands):
        def branch(distance):
            return lambda *values: finish(lambda block: moved_on(block, "replica", distance), *values)

        return lax.switch(distance_bits, [branch(1 << power) for power in range(level_count)], *operands)

    grad_input, *early_blocks = input_grad(
        blocks[:3], me, mean_in, inverse_in, same_group, block_input, *hidden_grads, *full_weights
    )
    arrived = scattered(parts, shards)
    owns = [shares[0] for shares in parts]
    early, late = packs

    def adam(pack, own, others, blocks):
        return call(
            functools.partial(adam_kernel, len(others), pack, pack is early),
            "adam",
            (pack.block(), pack.block(), pack.payload()),
            [SCALARS] + [BLOCKS] * (4 + len(others)),
            (scales, own, *others, *blocks),
            elements=rows * pack.columns,
        )

    grad_a, moved_a, sent_a = adam(early, owns[0], arrived[0], early_blocks)

    def finish(move, sent, grad_a, moved_a, own, *operands):
        other_a = move(sent)
        grad_b, moved_b, sent_b = adam(late, own, operands[:-3], operands[-3:])
        other_b = move(sent_b)
        mean, weight = call(
            functools.partial(half_average_kernel, early),
            "half_average",
            (early.block(), jax.ShapeDtypeStruct((1,), jnp.float32)),
            [SCALARS] + [BLOCKS] * 2,
            (scales, moved_a, other_a),
            elements=rows * early.columns,
        )
        averaged = call(
            functools.partial(average_kernel, late),
            "average",
            pltpu.HBM(params.shape, jnp.float32),
            [BLOCKS] * 3,
            (mean, moved_b, other_b),
            scratch=[pltpu.VMEM(params.shape, jnp.float32), pltpu.SemaphoreType.DMA],
            out_specs=IN_HBM,
            elements=rows * channels,
        )
        return (*moments(grad_a, grad_b), averaged, weight)

    first_new, second_new, averaged, new_weight = from_behind(
        finish, sent_a, grad_a, moved_a, owns[1], *arrived[1], *blocks[3:]
    )
    return (
        grad_input,
        *(jnp.transpose(array, (1, 0, 2)) for array in (averaged, first_new, second_new)),
        new_weight,
    )


def solution(mesh):
    placed = (
        P(("replica", "dp"), None, None),
        P(("replica", "dp"), None),
        P(("replica", "dp"), None, None),
        P("replica", "dp", None),
        P("replica", "dp", None),
        P("replica", "dp", None),
        P("replica"),
        P(),
    )
    return jax.shard_map(
        local,
        mesh=mesh,
        in_specs=placed,
        out_specs=(
            P(("replica", "dp"), None, None),
            P("replica", "dp", None),
            P("replica", "dp", None),
            P("replica", "dp", None),
            P("replica"),
        ),
        check_vma=False,
    )
```

```python
import functools
import math

import jax
import jax.numpy as jnp
from jax import lax
from jax.experimental import pallas as pl
from jax.experimental.pallas import tpu as pltpu
from jax.sharding import PartitionSpec as P

GSIZE = 40

NORM_EPS = 1e-05
BETA_ONE = 0.9
BETA_TWO = 0.999
LEARN_RATE = 0.002
ADAM_EPS = 1e-08

LANES = 128
ROW_STEP = 32
UNROLL = 3
TILE_ROWS = 16
VMEM_BYTES = 16 * 1024 * 1024


def padded(rows):
    return -(-rows // TILE_ROWS) * TILE_ROWS


def packed_rows(rows):
    return padded(rows + 1)


class Packing:
    def __init__(self, rows, start, stop):
        self.rows, self.start, self.stop = rows, start, stop
        self.columns = stop - start
        self.deep = packed_rows(rows)
        self.tiles, self.rest = divmod(self.columns, LANES)
        fold = LANES // self.rest if self.rest else 1
        self.fold_rows = padded(-(-self.deep // fold))
        self.folds = [
            (first, min(self.fold_rows, self.deep - first)) for first in range(0, self.deep, self.fold_rows)
        ]
        self.height = self.tiles * self.deep + (self.fold_rows if self.rest else 0)

    def write(self, ref, block):
        for tile in range(self.tiles):
            ref[tile * self.deep : (tile + 1) * self.deep, :] = block[
                :, tile * LANES : (tile + 1) * LANES
            ].astype(ref.dtype)
        if self.rest:
            left = block[:, self.tiles * LANES :]
            parts = []
            for first, count in self.folds:
                part = left[first : first + count]
                if count < self.fold_rows:
                    part = jnp.concatenate(
                        [part, jnp.zeros((self.fold_rows - count, self.rest), part.dtype)], axis=0
                    )
                parts.append(part)
            spare = LANES - self.rest * len(parts)
            if spare:
                parts.append(jnp.zeros((self.fold_rows, spare), left.dtype))
            ref[self.tiles * self.deep :, :] = jnp.concatenate(parts, axis=1).astype(ref.dtype)

    def read(self, ref):
        pieces = [
            ref[tile * self.deep : (tile + 1) * self.deep, :].astype(jnp.float32) for tile in range(self.tiles)
        ]
        if self.rest:
            left = ref[self.tiles * self.deep :, :].astype(jnp.float32)
            parts = [
                left[:count, i * self.rest : (i + 1) * self.rest] for i, (_, count) in enumerate(self.folds)
            ]
            pieces.append(jnp.concatenate(parts, axis=0) if len(parts) > 1 else parts[0])
        return jnp.concatenate(pieces, axis=1) if len(pieces) > 1 else pieces[0]

    def unpack(self, ref, out_ref, first_row):
        for tile in range(self.tiles):
            out_ref[first_row : first_row + self.deep, tile * LANES : (tile + 1) * LANES] = ref[
                tile * self.deep : (tile + 1) * self.deep, :
            ]
        if self.rest:
            left = ref[self.tiles * self.deep :, :]
            for i, (first, count) in enumerate(self.folds):
                out_ref[first_row + first : first_row + first + count, self.tiles * LANES :] = left[
                    :count, i * self.rest : (i + 1) * self.rest
                ]

    def payload(self):
        return jax.ShapeDtypeStruct((self.height, LANES), jnp.bfloat16)

    def block(self):
        return jax.ShapeDtypeStruct((self.deep, self.columns), jnp.float32)


def group_sums(rows, same_group):
    high = rows.astype(jnp.bfloat16).astype(jnp.float32)
    rest = rows - high
    middle = rest.astype(jnp.bfloat16).astype(jnp.float32)
    count = rows.shape[0]
    stacked = jnp.concatenate([high, middle, rest - middle], axis=0).astype(jnp.bfloat16)
    sums = jnp.dot(stacked, same_group, preferred_element_type=jnp.float32)
    return sums[:count] + (sums[count : 2 * count] + sums[2 * count :])


def table_sums(packs, rows, same_group):
    return jnp.concatenate(
        [
            group_sums(rows[:, pack.start : pack.stop], same_group[: pack.columns, : pack.columns])
            for pack in packs
        ],
        axis=1,
    )


def position_sums(parts):
    return jnp.concatenate([jnp.sum(part, axis=0, keepdims=True) for part in parts], axis=0)


def doubled_silu_grad(half, turned):
    return (1.0 + turned) + half * (1.0 - turned * turned)


def row(vector, i):
    return vector[i : i + 1]


def eight_sums(block):
    return sum(block[first : first + 8] for first in range(0, block.shape[0], 8))


def squares_sums(samples, positions, step, load, offset):
    sums = []
    for i in range(samples):

        def body(k, total):
            value = load(i, pl.multiple_of(k * step, step), step) + row(offset, i)
            return total + eight_sums(value * value)

        total = lax.fori_loop(0, positions // step, body, jnp.zeros((8, offset.shape[1]), jnp.float32), unroll=UNROLL)
        sums.append(jnp.sum(total, axis=0, keepdims=True))
    return jnp.concatenate(sums, axis=0)


def norm_back(table_mean, samples, positions, step, load, scales, offsets, inverse, incoming, kept_ref, store, stored):
    firsts, seconds = [], []
    zeros = jnp.zeros((8, scales.shape[1]), jnp.float32)
    for i in range(samples):

        def body(k, totals):
            first_row = pl.multiple_of(k * step, step)
            half = load(i, first_row, step) * row(scales, i) + row(offsets, i)
            doubled = incoming(i, first_row, step) * doubled_silu_grad(half, jnp.tanh(half))
            kept_ref[pl.ds(pl.multiple_of(i * positions + first_row, step), step), :] = doubled
            return totals[0] + eight_sums(doubled), totals[1] + eight_sums(doubled * half)

        first, second = lax.fori_loop(0, positions // step, body, (zeros, zeros), unroll=UNROLL)
        firsts.append(jnp.sum(first, axis=0, keepdims=True))
        seconds.append(jnp.sum(second, axis=0, keepdims=True))
    means = table_mean(jnp.concatenate(firsts + seconds, axis=0))
    first, second = 0.5 * means[:samples], means[samples:]
    gain = 0.5 * inverse
    slope = (2.0 * inverse) * second * scales
    level = inverse * (first + 2.0 * offsets * second)
    for i in range(samples):

        def body(k, carry):
            first_row = pl.multiple_of(k * step, step)
            doubled = kept_ref[pl.ds(pl.multiple_of(i * positions + first_row, step), step), :]
            value = load(i, first_row, step)
            store(i, first_row, step, doubled * row(gain, i) - (value * row(slope, i) + row(level, i)))
            return carry

        lax.fori_loop(0, positions // step, body, 0, unroll=UNROLL)
        stored(i)


def sigmoid(values):
    return 0.5 * jnp.tanh(0.5 * values) + 0.5


def cast_kernel(pack, push_ref, params_ref, token_ref, other_token_ref, out_ref, rows_ref):
    rows = pack.rows
    rows_ref[rows // 8 * 8 :, :] = jnp.zeros((pack.deep - rows // 8 * 8, pack.columns), jnp.float32)
    rows_ref[:rows, :] = params_ref[:, 0, pack.start : pack.stop] / push_ref[...]
    pack.write(out_ref, rows_ref[...])


def norm_in_kernel(shards, packs, me_ref, scales_ref, shift_ref, x_hbm, out_grad_hbm, *refs):
    act_ref, mean_ref, inverse_ref, same_group_ref = refs[:4]
    shift_refs, out_grad_refs = refs[4 : 4 + len(packs)], refs[4 + len(packs) : 4 + 2 * len(packs)]
    x_ref, out_grad_ref, sems = refs[4 + 2 * len(packs) :]
    copies = [
        pltpu.make_async_copy(x_hbm, x_ref, sems.at[0]),
        pltpu.make_async_copy(out_grad_hbm, out_grad_ref, sems.at[1]),
    ]
    for copy in copies:
        copy.start()
    samples, positions, channels = x_ref.shape
    rows = channels // shards
    deep = act_ref.shape[0] // shards
    entries = positions * GSIZE
    group_of_row = lax.broadcasted_iota(jnp.int32, same_group_ref.shape, 0) // GSIZE
    group_of_column = lax.broadcasted_iota(jnp.int32, same_group_ref.shape, 1) // GSIZE
    same_group_ref[...] = (group_of_row == group_of_column).astype(jnp.float32).astype(jnp.bfloat16)
    same_group = same_group_ref[...]
    for pack, shift_out in zip(packs, shift_refs):
        shift_out[...] = shift_ref[...].astype(jnp.float32)[:, pack.start : pack.stop]
    copies[0].wait()
    parts = [x_ref[i].astype(jnp.float32) for i in range(samples)]
    mean = table_sums(packs, position_sums(parts), same_group) / entries
    centered = [parts[i] - mean[i : i + 1] for i in range(samples)]
    variance = table_sums(packs, position_sums([part * part for part in centered]), same_group) / entries
    inverse = lax.rsqrt(variance + NORM_EPS)
    mean_ref[...] = mean
    inverse_ref[...] = inverse
    normed = [centered[i] * inverse[i : i + 1] for i in range(samples)]
    act = jnp.concatenate([part * sigmoid(part) for part in normed], axis=0).T
    for block in range(shards):
        slot = jnp.bitwise_xor(me_ref[0], block)
        act_ref[pl.ds(pl.multiple_of(slot * deep, TILE_ROWS), deep), :] = jnp.concatenate(
            [act[block * rows : (block + 1) * rows], jnp.zeros((deep - rows, act.shape[1]), jnp.float32)], axis=0
        ).astype(jnp.bfloat16)
    copies[1].wait()
    for pack, out_grad_out in zip(packs, out_grad_refs):
        for i in range(samples):
            out_grad_out[i] = out_grad_ref[i][:, pack.start : pack.stop]


def mix_kernel(shards, pack, slots, act_ref, shift_ref, out_grad_ref, same_group_ref, *refs):
    weight_refs, token_ref, refs = refs[:shards], refs[shards], refs[shards + 1 :]
    grad_hidden_ref, weight_out_ref = refs[:2]
    made_refs, refs = refs[2 : 2 + len(slots)], refs[2 + len(slots) :]
    weight_ref, kept_ref, hidden_ref, doubled_ref, sems = refs
    samples, positions, columns = out_grad_ref.shape
    entries = positions * GSIZE
    deep = pack.deep
    for slot, shard_ref in enumerate(weight_refs):
        pack.unpack(shard_ref, weight_ref, slot * deep)
    weight_copy = pltpu.make_async_copy(weight_ref, weight_out_ref, sems.at[0])
    weight_copy.start()
    same_group = same_group_ref[:columns, :columns]
    hidden_ref[...] = lax.dot_general(
        act_ref[...], weight_ref[...], (((0,), (0,)), ((), ())), preferred_element_type=jnp.float32
    )

    def table_mean(rows):
        return group_sums(rows, same_group) / entries

    def load(i, first_row, count):
        return hidden_ref[pl.ds(pl.multiple_of(i * positions + first_row, count), count), :]

    def incoming(i, first_row, count):
        return out_grad_ref[i, pl.ds(first_row, count), :].astype(jnp.float32)

    def store(i, first_row, count, grad):
        kept_ref[pl.ds(pl.multiple_of(i * positions + first_row, count), count), :] = grad.astype(jnp.bfloat16)

    shift = shift_ref[...]
    sums = position_sums([hidden_ref[i * positions : (i + 1) * positions, :] for i in range(samples)])
    offset = shift - table_mean(sums + positions * shift)
    squares = squares_sums(samples, positions, math.gcd(positions, ROW_STEP), load, offset)
    inverse = lax.rsqrt(table_mean(squares) + NORM_EPS)
    scales = 0.5 * inverse
    norm_back(
        table_mean,
        samples,
        positions,
        math.gcd(positions, ROW_STEP),
        load,
        scales,
        offset * scales,
        inverse,
        incoming,
        doubled_ref,
        store,
        lambda i: None,
    )
    copy = pltpu.make_async_copy(kept_ref, grad_hidden_ref, sems.at[1])
    copy.start()
    weight_grads(pack, slots, act_ref, kept_ref, made_refs)
    weight_copy.wait()
    copy.wait()


def weight_grads(pack, slots, act_ref, grad_hidden_ref, made_refs):
    deep = pack.deep
    low, high = min(slots), max(slots) + 1
    grad = jnp.dot(act_ref[low * deep : high * deep, :], grad_hidden_ref[...], preferred_element_type=jnp.float32)
    for slot, made_ref in zip(slots, made_refs):
        block = grad[(slot - low) * deep : (slot - low + 1) * deep]
        if slot:
            pack.write(made_ref, block)
        else:
            made_ref[...] = block


def rest_kernel(pack, slots, act_ref, grad_hidden_ref, token_ref, *made_refs):
    weight_grads(pack, slots, act_ref, grad_hidden_ref, made_refs)


def input_grad_kernel(shards, packs, carried, me_ref, mean_ref, inverse_ref, same_group_ref, x_hbm, *refs):
    count = len(packs)
    grad_refs, weight_refs, refs = refs[:count], refs[count : 2 * count], refs[2 * count :]
    carried_hbms, out_ref, carried_refs = refs[:carried], refs[carried], refs[carried + 1 : 2 * carried + 1]
    rows_ref, x_ref, made_ref, act_ref, sems, carried_sems = refs[2 * carried + 1 :]
    copies = [pltpu.make_async_copy(x_hbm, x_ref, sems.at[0])]
    copies[0].start()
    carried_copies = [
        pltpu.make_async_copy(source, target, carried_sems.at[i])
        for i, (source, target) in enumerate(zip(carried_hbms, carried_refs))
    ]
    for copy in carried_copies:
        copy.start()
    samples, positions, channels = x_ref.shape
    entries = positions * GSIZE
    rows = channels // shards
    weights = []
    for index, (pack, weight_ref) in enumerate(zip(packs, weight_refs)):
        for block in range(shards):
            slot = jnp.bitwise_xor(me_ref[0], block)
            rows_ref[block * rows : (block + 1) * rows, : pack.columns] = weight_ref[
                pl.ds(pl.multiple_of(slot * pack.deep, TILE_ROWS), pack.deep), :
            ].astype(jnp.float32)[:rows]
        weights.append(rows_ref[:, : pack.columns].astype(jnp.bfloat16))
    grad_act = 0.0
    for index, (grad_ref, weight) in enumerate(zip(grad_refs, weights)):
        grad_act += lax.dot_general(
            grad_ref[...], weight, (((1,), (1,)), ((), ())), preferred_element_type=jnp.float32
        )
    act_ref[...] = grad_act
    copies[0].wait()
    same_group = same_group_ref[...]
    inverse = inverse_ref[...]

    def table_mean(rows):
        return table_sums(packs, rows, same_group) / entries

    def load(i, first_row, count):
        return x_ref[i, pl.ds(first_row, count), :].astype(jnp.float32)

    def incoming(i, first_row, count):
        return act_ref[pl.ds(pl.multiple_of(i * positions + first_row, count), count), :]

    def store(i, first_row, count, grad):
        made_ref[i, pl.ds(first_row, count), :] = grad.astype(jnp.bfloat16)

    def stored(i):
        copies.append(pltpu.make_async_copy(made_ref.at[i], out_ref.at[i], sems.at[len(copies)]))
        copies[-1].start()

    scales = 0.5 * inverse
    norm_back(
        table_mean, samples, positions, math.gcd(positions, ROW_STEP // 2), load, scales, -mean_ref[...] * scales, inverse, incoming, act_ref, store, stored
    )
    for copy in carried_copies + copies[-samples:]:
        copy.wait()


def merge_kernel(one_ref, other_ref, *refs):
    count = (len(refs) - 1) // 2
    through_refs, out_ref, through_out_refs = refs[:count], refs[count], refs[count + 1 :]
    out_ref[...] = (one_ref[...].astype(jnp.float32) + other_ref[...].astype(jnp.float32)).astype(out_ref.dtype)
    for through_ref, through_out_ref in zip(through_refs, through_out_refs):
        through_out_ref[...] = through_ref[...]


def cut_kernel(packs, *refs):
    count = 3 * len(packs)
    hbm_refs, out_refs = refs[:3], refs[4 : 4 + count]
    row_refs, block_refs, sems = refs[4 + count : 7 + count], refs[7 + count : -1], refs[-1]
    copies = [
        pltpu.make_async_copy(source, target, sems.at[i])
        for i, (source, target) in enumerate(zip(hbm_refs, row_refs))
    ]
    for copy in copies:
        copy.start()
    out_copies = []
    for i, row_ref in enumerate(row_refs):
        copies[i].wait()
        for index, pack in enumerate(packs):
            place = 3 * index + i
            block_refs[place][...] = row_ref[:, 0, pack.start : pack.stop]
            out_copies.append(pltpu.make_async_copy(block_refs[place], out_refs[place], sems.at[3 + place]))
            out_copies[-1].start()
    for copy in out_copies:
        copy.wait()


def adam_kernel(count, pack, spare_value, scales_ref, own_ref, *refs):
    other_refs, refs = refs[:count], refs[count:]
    (params_ref, first_ref, second_ref), (grad_ref, moved_ref, sent_ref) = refs[:3], refs[-3:]
    rows = pack.rows
    total = own_ref[...]
    for other_ref in other_refs:
        total = total + pack.read(other_ref)
    grad_ref[...] = total * scales_ref[2]
    grad = grad_ref[:rows, :]
    first_new = BETA_ONE * first_ref[...] + (1.0 - BETA_ONE) * grad
    second_new = BETA_TWO * second_ref[...] + (1.0 - BETA_TWO) * grad * grad
    update = (scales_ref[0] * first_new) / (jnp.sqrt(second_new * scales_ref[1]) + ADAM_EPS)
    value = scales_ref[3] if spare_value else 0.0
    moved_ref[rows // 8 * 8 :, :] = jnp.full((pack.deep - rows // 8 * 8, pack.columns), value, jnp.float32)
    moved_ref[:rows, :] = params_ref[...] - update
    pack.write(sent_ref, moved_ref[...])


def half_average_kernel(pack, scales_ref, moved_ref, other_ref, mean_ref, push_out_ref):
    other = pack.read(other_ref)
    mean_ref[...] = 0.5 * (moved_ref[...] + other)
    push_out_ref[...] = 0.5 * (scales_ref[3] + other[pack.rows, :1])


def moments_kernel(packs, first_hbm, second_hbm, *refs):
    grad_refs, (first_out, second_out, first_ref, second_ref, sems) = refs[: len(packs)], refs[len(packs) :]
    copies = [
        pltpu.make_async_copy(first_hbm, first_ref, sems.at[0]),
        pltpu.make_async_copy(second_hbm, second_ref, sems.at[1]),
    ]
    for copy in copies:
        copy.start()
    rows = first_ref.shape[0]
    grad = jnp.concatenate([grad_ref[:rows, :] for grad_ref in grad_refs], axis=1)
    copies[0].wait()
    first_out[:, 0, :] = BETA_ONE * first_ref[:, 0, :] + (1.0 - BETA_ONE) * grad
    copies[1].wait()
    second_out[:, 0, :] = BETA_TWO * second_ref[:, 0, :] + (1.0 - BETA_TWO) * grad * grad


def average_kernel(pack, mean_ref, moved_ref, other_ref, out_ref, rows_ref, sem):
    rows = out_ref.shape[0]
    later = 0.5 * (moved_ref[...] + pack.read(other_ref))
    rows_ref[:, 0, :] = jnp.concatenate([mean_ref[...], later], axis=1)[:rows]
    copy = pltpu.make_async_copy(rows_ref, out_ref, sem)
    copy.start()
    copy.wait()


SCALARS = pl.BlockSpec(memory_space=pltpu.SMEM)
BLOCKS = pl.BlockSpec(memory_space=pltpu.VMEM)
TOKEN = pl.BlockSpec(memory_space=pl.ANY)
IN_HBM = pl.BlockSpec(memory_space=pltpu.HBM)


def call(kernel, name, outs, specs, operands, scratch=(), out_specs=None, flops=0, elements=0):
    return pl.pallas_call(
        kernel,
        out_shape=outs,
        in_specs=specs,
        out_specs=out_specs or jax.tree.map(lambda _: BLOCKS, outs),
        scratch_shapes=list(scratch),
        compiler_params=pltpu.CompilerParams(vmem_limit_bytes=VMEM_BYTES),
        cost_estimate=pl.CostEstimate(flops=flops, bytes_accessed=8 * elements, transcendentals=elements),
        name=name,
    )(*operands)


def stay(array):
    return pltpu.with_memory_space_constraint(array, pltpu.HBM)


def moved_on(block, axis, distance):
    size = lax.axis_size(axis)
    return lax.ppermute(block, axis, [(i, (i + distance) % size) for i in range(size)])


def exchanged(block, axis, bit):
    return lax.ppermute(block, axis, [(i, i ^ bit) for i in range(lax.axis_size(axis))])


def lowest_bit(slot):
    return slot & -slot


def hold_kernel(block_ref, token_ref, out_ref):
    out_ref[...] = block_ref[...]


def gathered(piece, shards, token=None):
    held = [piece]
    for slot in range(1, shards):
        bit = lowest_bit(slot)
        held.append(exchanged(held[slot ^ bit], "dp", bit))
        if token is not None and slot == 2:
            shape = jax.ShapeDtypeStruct(piece.shape, piece.dtype)
            held[slot] = call(hold_kernel, "hold", shape, [BLOCKS, IN_HBM], (held[slot], stay(token)))
    return held


def scattered(parts, shards):
    arrived = [[] for _ in parts]
    token, straight = None, []
    for part, held in enumerate(parts):
        last = part == len(parts) - 1
        slots = sorted(range(2, shards), key=lambda slot: (-slot.bit_count(), -slot))
        for slot in slots:
            bit = lowest_bit(slot)
            other = exchanged(held[slot], "dp", bit)
            if slot == bit:
                arrived[part].append(other)
                continue
            if None in held:
                held.update(held.pop(None)(token))
            through = [shares[1] for shares in parts] if last else []
            shapes = [jax.ShapeDtypeStruct(array.shape, array.dtype) for array in (other, *through)]
            made = call(
                merge_kernel,
                "merge",
                tuple(shapes),
                [BLOCKS] * (2 + len(through)),
                (held[slot ^ bit], other, *through),
            )
            held[slot ^ bit], straight, token = made[0], made[1:], made[0]
    for part, piece in enumerate(straight or [shares[1] for shares in parts]):
        arrived[part].append(exchanged(piece, "dp", 1))
    return arrived


def column_cuts(channels):
    half = (channels // GSIZE + 1) // 2 * GSIZE
    return [(0, half), (half, channels)]


def local(
    block_input, time_shift, out_grad, params, first_moment, second_moment, push_weight, step
):
    samples, positions, channels = block_input.shape
    tokens = samples * positions
    shards = lax.axis_size("dp")
    rows = params.shape[1]
    deep = packed_rows(rows)
    me = lax.axis_index("dp").astype(jnp.int32).reshape(1)
    packs = [Packing(rows, start, stop) for start, stop in column_cuts(channels)]
    params, first_moment, second_moment = (
        jnp.transpose(array, (1, 0, 2)) for array in (params, first_moment, second_moment)
    )
    def shards_of(pack, *tokens, late=None):
        piece = call(
            functools.partial(cast_kernel, pack),
            "cast",
            pack.payload(),
            [BLOCKS, BLOCKS, TOKEN, TOKEN],
            (push_weight.reshape(1, 1), params, *tokens),
            scratch=[pltpu.VMEM((deep, pack.columns), jnp.float32)],
            elements=rows * pack.columns,
        )
        return gathered(piece, shards, late)

    level_count = lax.axis_size("replica").bit_length() - 1
    distance_bits = step[0] % level_count
    step_count = (step[0] + 1).astype(jnp.float32)
    scales = jnp.stack(
        [
            LEARN_RATE / (1.0 - jnp.power(BETA_ONE, step_count)),
            1.0 / (1.0 - jnp.power(BETA_TWO, step_count)),
            jnp.float32(1.0 / shards),
            push_weight[0],
        ]
    )

    activation, mean_in, inverse_in, same_group, *pieces = call(
        functools.partial(norm_in_kernel, shards, packs),
        "norm_in",
        (
            jax.ShapeDtypeStruct((shards * deep, tokens), jnp.bfloat16),
            jax.ShapeDtypeStruct((samples, channels), jnp.float32),
            jax.ShapeDtypeStruct((samples, channels), jnp.float32),
            jax.ShapeDtypeStruct((max(pack.columns for pack in packs),) * 2, jnp.bfloat16),
            *(jax.ShapeDtypeStruct((samples, pack.columns), jnp.float32) for pack in packs),
            *(jax.ShapeDtypeStruct((samples, positions, pack.columns), jnp.bfloat16) for pack in packs),
        ),
        [SCALARS, SCALARS, BLOCKS, IN_HBM, IN_HBM],
        (me, scales, time_shift, stay(block_input), stay(out_grad)),
        scratch=[
            pltpu.VMEM(block_input.shape, jnp.bfloat16),
            pltpu.VMEM(out_grad.shape, jnp.bfloat16),
            pltpu.SemaphoreType.DMA((2,)),
        ],
        elements=tokens * channels,
    )

    columns = [pack.columns for pack in packs for _ in range(3)]
    blocks = call(
        functools.partial(cut_kernel, packs),
        "cut",
        tuple(pltpu.HBM((rows, width), jnp.float32) for width in columns),
        [IN_HBM] * 3 + [TOKEN],
        (stay(params), stay(first_moment), stay(second_moment), mean_in),
        scratch=[pltpu.VMEM(params.shape, jnp.float32)] * 3
        + [pltpu.VMEM((rows, width), jnp.float32) for width in columns]
        + [pltpu.SemaphoreType.DMA((3 + len(columns),))],
        out_specs=(IN_HBM,) * len(columns),
        elements=rows * channels,
    )
    weights = [shards_of(packs[0], params, params)]
    weights.append(shards_of(packs[1], weights[0][1], mean_in, late=blocks[-1]))
    hidden_grads, full_weights, parts = [], [], []
    token = mean_in
    shifts, out_grads = pieces[: len(packs)], pieces[len(packs) :]
    for pack, shard_list, shift, out_grad_piece in zip(packs, weights, shifts, out_grads):
        kept = jax.ShapeDtypeStruct if pack is packs[-1] else pltpu.HBM
        kept_spec = BLOCKS if pack is packs[-1] else IN_HBM
        later = range(shards - 1) if pack is packs[-1] and shards > 2 else range(0)
        slots = [slot for slot in range(shards) if slot not in later]

        def made(slots, pack=pack):
            return tuple(pack.payload() if slot else pack.block() for slot in slots)

        grad_hidden, full_weight, *shares = call(
            functools.partial(mix_kernel, shards, pack, slots),
            "mix",
            (kept((tokens, pack.columns), jnp.bfloat16), kept((shards * deep, pack.columns), jnp.bfloat16))
            + made(slots),
            [BLOCKS] * (4 + shards) + [TOKEN],
            (activation, shift, out_grad_piece, same_group, *shard_list, token),
            scratch=[
                pltpu.VMEM((shards * deep, pack.columns), jnp.bfloat16),
                pltpu.VMEM((tokens, pack.columns), jnp.bfloat16),
                pltpu.VMEM((tokens, pack.columns), jnp.float32),
                pltpu.VMEM((tokens, pack.columns), jnp.float32),
                pltpu.SemaphoreType.DMA((2,)),
            ],
            out_specs=(kept_spec,) * 2 + (BLOCKS,) * len(slots),
            flops=4 * tokens * channels * pack.columns,
            elements=tokens * pack.columns,
        )
        shares = dict(zip(slots, shares))
        if later:
            def rest(token, pack=pack, later=tuple(later), outs=made(later), grad_hidden=grad_hidden):
                shares = call(
                    functools.partial(rest_kernel, pack, later),
                    "rest",
                    outs,
                    [BLOCKS] * 2 + [TOKEN],
                    (activation, grad_hidden, token),
                    flops=2 * tokens * channels * pack.columns,
                )
                return dict(zip(later, shares))

            shares[None] = rest
        token = shares[slots[-1]]
        hidden_grads.append(grad_hidden)
        full_weights.append(full_weight)
        parts.append(shares)

    def input_grad(carried, *operands):
        return call(
            functools.partial(input_grad_kernel, shards, packs, len(carried)),
            "input_grad",
            (pltpu.HBM(block_input.shape, jnp.bfloat16),)
            + tuple(jax.ShapeDtypeStruct(array.shape, array.dtype) for array in carried),
            [SCALARS] + [BLOCKS] * 3 + [IN_HBM] + [BLOCKS] * (2 * len(packs)) + [IN_HBM] * len(carried),
            operands[:4] + (stay(operands[4]),) + operands[5:] + tuple(map(stay, carried)),
            scratch=[
                pltpu.VMEM((channels, max(pack.columns for pack in packs)), jnp.float32),
                pltpu.VMEM(block_input.shape, jnp.bfloat16),
                pltpu.VMEM(block_input.shape, jnp.bfloat16),
                pltpu.VMEM((tokens, channels), jnp.float32),
                pltpu.SemaphoreType.DMA((1 + samples,)),
                pltpu.SemaphoreType.DMA((len(carried),)),
            ],
            out_specs=(IN_HBM,) + (BLOCKS,) * len(carried),
            flops=2 * tokens * channels * channels,
            elements=tokens * channels,
        )

    def moments(*grads):
        return call(
            functools.partial(moments_kernel, packs),
            "moments",
            (jax.ShapeDtypeStruct(params.shape, jnp.float32),) * 2,
            [IN_HBM] * 2 + [BLOCKS] * len(packs),
            (stay(first_moment), stay(second_moment), *grads),
            scratch=[pltpu.VMEM(params.shape, jnp.float32)] * 2 + [pltpu.SemaphoreType.DMA((2,))],
            elements=rows * channels,
        )

    def from_behind(finish, *operands):
        def branch(distance):
            return lambda *values: finish(lambda block: moved_on(block, "replica", distance), *values)

        return lax.switch(distance_bits, [branch(1 << power) for power in range(level_count)], *operands)

    grad_input, *early_blocks = input_grad(
        blocks[:3], me, mean_in, inverse_in, same_group, block_input, *hidden_grads, *full_weights
    )
    arrived = scattered(parts, shards)
    owns = [shares[0] for shares in parts]
    early, late = packs

    def adam(pack, own, others, blocks):
        return call(
            functools.partial(adam_kernel, len(others), pack, pack is early),
            "adam",
            (pack.block(), pack.block(), pack.payload()),
            [SCALARS] + [BLOCKS] * (4 + len(others)),
            (scales, own, *others, *blocks),
            elements=rows * pack.columns,
        )

    grad_a, moved_a, sent_a = adam(early, owns[0], arrived[0], early_blocks)

    def finish(move, sent, grad_a, moved_a, own, *operands):
        other_a = move(sent)
        grad_b, moved_b, sent_b = adam(late, own, operands[:-3], operands[-3:])
        other_b = move(sent_b)
        mean, weight = call(
            functools.partial(half_average_kernel, early),
            "half_average",
            (early.block(), jax.ShapeDtypeStruct((1,), jnp.float32)),
            [SCALARS] + [BLOCKS] * 2,
            (scales, moved_a, other_a),
            elements=rows * early.columns,
        )
        averaged = call(
            functools.partial(average_kernel, late),
            "average",
            pltpu.HBM(params.shape, jnp.float32),
            [BLOCKS] * 3,
            (mean, moved_b, other_b),
            scratch=[pltpu.VMEM(params.shape, jnp.float32), pltpu.SemaphoreType.DMA],
            out_specs=IN_HBM,
            elements=rows * channels,
        )
        return (*moments(grad_a, grad_b), averaged, weight)

    first_new, second_new, averaged, new_weight = from_behind(
        finish, sent_a, grad_a, moved_a, owns[1], *arrived[1], *blocks[3:]
    )
    return (
        grad_input,
        *(jnp.transpose(array, (1, 0, 2)) for array in (averaged, first_new, second_new)),
        new_weight,
    )


def solution(mesh):
    placed = (
        P(("replica", "dp"), None, None),
        P(("replica", "dp"), None),
        P(("replica", "dp"), None, None),
        P("replica", "dp", None),
        P("replica", "dp", None),
        P("replica", "dp", None),
        P("replica"),
        P(),
    )
    return jax.shard_map(
        local,
        mesh=mesh,
        in_specs=placed,
        out_specs=(
            P(("replica", "dp"), None, None),
            P("replica", "dp", None),
            P("replica", "dp", None),
            P("replica", "dp", None),
            P("replica"),
        ),
        check_vma=False,
    )
```

```python
import functools
import math

import jax
import jax.numpy as jnp
from jax import lax
from jax.experimental import pallas as pl
from jax.experimental.pallas import tpu as pltpu
from jax.sharding import PartitionSpec as P

GSIZE = 40

NORM_EPS = 1e-05
BETA_ONE = 0.9
BETA_TWO = 0.999
LEARN_RATE = 0.002
ADAM_EPS = 1e-08

LANES = 128
ROW_STEP = 32
UNROLL = 3
TILE_ROWS = 16
VMEM_BYTES = 16 * 1024 * 1024


def padded(rows):
    return -(-rows // TILE_ROWS) * TILE_ROWS


def packed_rows(rows):
    return padded(rows + 1)


class Packing:
    def __init__(self, rows, start, stop):
        self.rows, self.start, self.stop = rows, start, stop
        self.columns = stop - start
        self.deep = packed_rows(rows)
        self.tiles, self.rest = divmod(self.columns, LANES)
        fold = LANES // self.rest if self.rest else 1
        self.fold_rows = padded(-(-self.deep // fold))
        self.folds = [
            (first, min(self.fold_rows, self.deep - first)) for first in range(0, self.deep, self.fold_rows)
        ]
        self.height = self.tiles * self.deep + (self.fold_rows if self.rest else 0)

    def write(self, ref, block):
        for tile in range(self.tiles):
            ref[tile * self.deep : (tile + 1) * self.deep, :] = block[
                :, tile * LANES : (tile + 1) * LANES
            ].astype(ref.dtype)
        if self.rest:
            left = block[:, self.tiles * LANES :]
            parts = []
            for first, count in self.folds:
                part = left[first : first + count]
                if count < self.fold_rows:
                    part = jnp.concatenate(
                        [part, jnp.zeros((self.fold_rows - count, self.rest), part.dtype)], axis=0
                    )
                parts.append(part)
            spare = LANES - self.rest * len(parts)
            if spare:
                parts.append(jnp.zeros((self.fold_rows, spare), left.dtype))
            ref[self.tiles * self.deep :, :] = jnp.concatenate(parts, axis=1).astype(ref.dtype)

    def read(self, ref):
        pieces = [
            ref[tile * self.deep : (tile + 1) * self.deep, :].astype(jnp.float32) for tile in range(self.tiles)
        ]
        if self.rest:
            left = ref[self.tiles * self.deep :, :].astype(jnp.float32)
            parts = [
                left[:count, i * self.rest : (i + 1) * self.rest] for i, (_, count) in enumerate(self.folds)
            ]
            pieces.append(jnp.concatenate(parts, axis=0) if len(parts) > 1 else parts[0])
        return jnp.concatenate(pieces, axis=1) if len(pieces) > 1 else pieces[0]

    def unpack(self, ref, out_ref, first_row):
        for tile in range(self.tiles):
            out_ref[first_row : first_row + self.deep, tile * LANES : (tile + 1) * LANES] = ref[
                tile * self.deep : (tile + 1) * self.deep, :
            ]
        if self.rest:
            left = ref[self.tiles * self.deep :, :]
            for i, (first, count) in enumerate(self.folds):
                out_ref[first_row + first : first_row + first + count, self.tiles * LANES :] = left[
                    :count, i * self.rest : (i + 1) * self.rest
                ]

    def payload(self):
        return jax.ShapeDtypeStruct((self.height, LANES), jnp.bfloat16)

    def block(self):
        return jax.ShapeDtypeStruct((self.deep, self.columns), jnp.float32)


def group_sums(rows, same_group):
    high = rows.astype(jnp.bfloat16).astype(jnp.float32)
    rest = rows - high
    middle = rest.astype(jnp.bfloat16).astype(jnp.float32)
    count = rows.shape[0]
    stacked = jnp.concatenate([high, middle, rest - middle], axis=0).astype(jnp.bfloat16)
    sums = jnp.dot(stacked, same_group, preferred_element_type=jnp.float32)
    return sums[:count] + (sums[count : 2 * count] + sums[2 * count :])


def table_sums(packs, rows, same_group):
    return jnp.concatenate(
        [
            group_sums(rows[:, pack.start : pack.stop], same_group[: pack.columns, : pack.columns])
            for pack in packs
        ],
        axis=1,
    )


def position_sums(parts):
    return jnp.concatenate([jnp.sum(part, axis=0, keepdims=True) for part in parts], axis=0)


def doubled_silu_grad(half, turned):
    return (1.0 + turned) + half * (1.0 - turned * turned)


def row(vector, i):
    return vector[i : i + 1]


def eight_sums(block):
    return sum(block[first : first + 8] for first in range(0, block.shape[0], 8))


def squares_sums(samples, positions, step, load, offset):
    sums = []
    for i in range(samples):

        def body(k, total):
            value = load(i, pl.multiple_of(k * step, step), step) + row(offset, i)
            return total + eight_sums(value * value)

        total = lax.fori_loop(0, positions // step, body, jnp.zeros((8, offset.shape[1]), jnp.float32), unroll=UNROLL)
        sums.append(jnp.sum(total, axis=0, keepdims=True))
    return jnp.concatenate(sums, axis=0)


def norm_back(table_mean, samples, positions, step, load, scales, offsets, inverse, incoming, kept_ref, store, stored):
    firsts, seconds = [], []
    zeros = jnp.zeros((8, scales.shape[1]), jnp.float32)
    for i in range(samples):

        def body(k, totals):
            first_row = pl.multiple_of(k * step, step)
            half = load(i, first_row, step) * row(scales, i) + row(offsets, i)
            doubled = incoming(i, first_row, step) * doubled_silu_grad(half, jnp.tanh(half))
            kept_ref[pl.ds(pl.multiple_of(i * positions + first_row, step), step), :] = doubled
            return totals[0] + eight_sums(doubled), totals[1] + eight_sums(doubled * half)

        first, second = lax.fori_loop(0, positions // step, body, (zeros, zeros), unroll=UNROLL)
        firsts.append(jnp.sum(first, axis=0, keepdims=True))
        seconds.append(jnp.sum(second, axis=0, keepdims=True))
    means = table_mean(jnp.concatenate(firsts + seconds, axis=0))
    first, second = 0.5 * means[:samples], means[samples:]
    gain = 0.5 * inverse
    slope = (2.0 * inverse) * second * scales
    level = inverse * (first + 2.0 * offsets * second)
    for i in range(samples):

        def body(k, carry):
            first_row = pl.multiple_of(k * step, step)
            doubled = kept_ref[pl.ds(pl.multiple_of(i * positions + first_row, step), step), :]
            value = load(i, first_row, step)
            store(i, first_row, step, doubled * row(gain, i) - (value * row(slope, i) + row(level, i)))
            return carry

        lax.fori_loop(0, positions // step, body, 0, unroll=UNROLL)
        stored(i)


def sigmoid(values):
    return 0.5 * jnp.tanh(0.5 * values) + 0.5


def cast_kernel(pack, push_ref, params_ref, token_ref, other_token_ref, out_ref, rows_ref):
    rows = pack.rows
    rows_ref[rows // 8 * 8 :, :] = jnp.zeros((pack.deep - rows // 8 * 8, pack.columns), jnp.float32)
    rows_ref[:rows, :] = params_ref[:, 0, pack.start : pack.stop] / push_ref[...]
    pack.write(out_ref, rows_ref[...])


def norm_in_kernel(shards, packs, me_ref, scales_ref, shift_ref, x_hbm, out_grad_hbm, *refs):
    act_ref, mean_ref, inverse_ref, same_group_ref = refs[:4]
    shift_refs, out_grad_refs = refs[4 : 4 + len(packs)], refs[4 + len(packs) : 4 + 2 * len(packs)]
    x_ref, out_grad_ref, sems = refs[4 + 2 * len(packs) :]
    copies = [
        pltpu.make_async_copy(x_hbm, x_ref, sems.at[0]),
        pltpu.make_async_copy(out_grad_hbm, out_grad_ref, sems.at[1]),
    ]
    for copy in copies:
        copy.start()
    samples, positions, channels = x_ref.shape
    rows = channels // shards
    deep = act_ref.shape[0] // shards
    entries = positions * GSIZE
    group_of_row = lax.broadcasted_iota(jnp.int32, same_group_ref.shape, 0) // GSIZE
    group_of_column = lax.broadcasted_iota(jnp.int32, same_group_ref.shape, 1) // GSIZE
    same_group_ref[...] = (group_of_row == group_of_column).astype(jnp.float32).astype(jnp.bfloat16)
    same_group = same_group_ref[...]
    for pack, shift_out in zip(packs, shift_refs):
        shift_out[...] = shift_ref[...].astype(jnp.float32)[:, pack.start : pack.stop]
    copies[0].wait()
    parts = [x_ref[i].astype(jnp.float32) for i in range(samples)]
    mean = table_sums(packs, position_sums(parts), same_group) / entries
    centered = [parts[i] - mean[i : i + 1] for i in range(samples)]
    variance = table_sums(packs, position_sums([part * part for part in centered]), same_group) / entries
    inverse = lax.rsqrt(variance + NORM_EPS)
    mean_ref[...] = mean
    inverse_ref[...] = inverse
    normed = [centered[i] * inverse[i : i + 1] for i in range(samples)]
    act = jnp.concatenate([part * sigmoid(part) for part in normed], axis=0).T
    for block in range(shards):
        slot = jnp.bitwise_xor(me_ref[0], block)
        act_ref[pl.ds(pl.multiple_of(slot * deep, TILE_ROWS), deep), :] = jnp.concatenate(
            [act[block * rows : (block + 1) * rows], jnp.zeros((deep - rows, act.shape[1]), jnp.float32)], axis=0
        ).astype(jnp.bfloat16)
    copies[1].wait()
    for pack, out_grad_out in zip(packs, out_grad_refs):
        for i in range(samples):
            out_grad_out[i] = out_grad_ref[i][:, pack.start : pack.stop]


def mix_kernel(shards, pack, slots, act_ref, shift_ref, out_grad_ref, same_group_ref, *refs):
    weight_refs, token_ref, refs = refs[:shards], refs[shards], refs[shards + 1 :]
    grad_hidden_ref, weight_out_ref = refs[:2]
    made_refs, refs = refs[2 : 2 + len(slots)], refs[2 + len(slots) :]
    weight_ref, kept_ref, hidden_ref, doubled_ref, sems = refs
    samples, positions, columns = out_grad_ref.shape
    entries = positions * GSIZE
    deep = pack.deep
    for slot, shard_ref in enumerate(weight_refs):
        pack.unpack(shard_ref, weight_ref, slot * deep)
    weight_copy = pltpu.make_async_copy(weight_ref, weight_out_ref, sems.at[0])
    weight_copy.start()
    same_group = same_group_ref[:columns, :columns]
    hidden_ref[...] = lax.dot_general(
        act_ref[...], weight_ref[...], (((0,), (0,)), ((), ())), preferred_element_type=jnp.float32
    )

    def table_mean(rows):
        return group_sums(rows, same_group) / entries

    def load(i, first_row, count):
        return hidden_ref[pl.ds(pl.multiple_of(i * positions + first_row, count), count), :]

    def incoming(i, first_row, count):
        return out_grad_ref[i, pl.ds(first_row, count), :].astype(jnp.float32)

    def store(i, first_row, count, grad):
        kept_ref[pl.ds(pl.multiple_of(i * positions + first_row, count), count), :] = grad.astype(jnp.bfloat16)

    shift = shift_ref[...]
    sums = position_sums([hidden_ref[i * positions : (i + 1) * positions, :] for i in range(samples)])
    offset = shift - table_mean(sums + positions * shift)
    squares = squares_sums(samples, positions, math.gcd(positions, ROW_STEP), load, offset)
    inverse = lax.rsqrt(table_mean(squares) + NORM_EPS)
    scales = 0.5 * inverse
    norm_back(
        table_mean,
        samples,
        positions,
        math.gcd(positions, ROW_STEP),
        load,
        scales,
        offset * scales,
        inverse,
        incoming,
        doubled_ref,
        store,
        lambda i: None,
    )
    copy = pltpu.make_async_copy(kept_ref, grad_hidden_ref, sems.at[1])
    copy.start()
    weight_grads(pack, slots, act_ref, kept_ref, made_refs)
    weight_copy.wait()
    copy.wait()


def weight_grads(pack, slots, act_ref, grad_hidden_ref, made_refs):
    deep = pack.deep
    low, high = min(slots), max(slots) + 1
    grad = jnp.dot(act_ref[low * deep : high * deep, :], grad_hidden_ref[...], preferred_element_type=jnp.float32)
    for slot, made_ref in zip(slots, made_refs):
        block = grad[(slot - low) * deep : (slot - low + 1) * deep]
        if slot:
            pack.write(made_ref, block)
        else:
            made_ref[...] = block


def rest_kernel(pack, slots, act_ref, grad_hidden_ref, token_ref, *made_refs):
    weight_grads(pack, slots, act_ref, grad_hidden_ref, made_refs)


def input_grad_kernel(shards, packs, carried, me_ref, mean_ref, inverse_ref, same_group_ref, x_hbm, *refs):
    count = len(packs)
    grad_refs, weight_refs, refs = refs[:count], refs[count : 2 * count], refs[2 * count :]
    carried_hbms, out_ref, carried_refs = refs[:carried], refs[carried], refs[carried + 1 : 2 * carried + 1]
    rows_ref, x_ref, made_ref, act_ref, sems, carried_sems = refs[2 * carried + 1 :]
    copies = [pltpu.make_async_copy(x_hbm, x_ref, sems.at[0])]
    copies[0].start()
    carried_copies = [
        pltpu.make_async_copy(source, target, carried_sems.at[i])
        for i, (source, target) in enumerate(zip(carried_hbms, carried_refs))
    ]
    for copy in carried_copies:
        copy.start()
    samples, positions, channels = x_ref.shape
    entries = positions * GSIZE
    rows = channels // shards
    weights = []
    for index, (pack, weight_ref) in enumerate(zip(packs, weight_refs)):
        for block in range(shards):
            slot = jnp.bitwise_xor(me_ref[0], block)
            rows_ref[block * rows : (block + 1) * rows, : pack.columns] = weight_ref[
                pl.ds(pl.multiple_of(slot * pack.deep, TILE_ROWS), pack.deep), :
            ].astype(jnp.float32)[:rows]
        weights.append(rows_ref[:, : pack.columns].astype(jnp.bfloat16))
    grad_act = 0.0
    for index, (grad_ref, weight) in enumerate(zip(grad_refs, weights)):
        grad_act += lax.dot_general(
            grad_ref[...], weight, (((1,), (1,)), ((), ())), preferred_element_type=jnp.float32
        )
    act_ref[...] = grad_act
    copies[0].wait()
    same_group = same_group_ref[...]
    inverse = inverse_ref[...]

    def table_mean(rows):
        return table_sums(packs, rows, same_group) / entries

    def load(i, first_row, count):
        return x_ref[i, pl.ds(first_row, count), :].astype(jnp.float32)

    def incoming(i, first_row, count):
        return act_ref[pl.ds(pl.multiple_of(i * positions + first_row, count), count), :]

    def store(i, first_row, count, grad):
        made_ref[i, pl.ds(first_row, count), :] = grad.astype(jnp.bfloat16)

    def stored(i):
        copies.append(pltpu.make_async_copy(made_ref.at[i], out_ref.at[i], sems.at[len(copies)]))
        copies[-1].start()

    scales = 0.5 * inverse
    norm_back(
        table_mean, samples, positions, math.gcd(positions, ROW_STEP // 2), load, scales, -mean_ref[...] * scales, inverse, incoming, act_ref, store, stored
    )
    for copy in carried_copies + copies[-samples:]:
        copy.wait()


def merge_kernel(one_ref, other_ref, *refs):
    count = (len(refs) - 1) // 2
    through_refs, out_ref, through_out_refs = refs[:count], refs[count], refs[count + 1 :]
    out_ref[...] = (one_ref[...].astype(jnp.float32) + other_ref[...].astype(jnp.float32)).astype(out_ref.dtype)
    for through_ref, through_out_ref in zip(through_refs, through_out_refs):
        through_out_ref[...] = through_ref[...]


def cut_kernel(packs, *refs):
    count = 3 * len(packs)
    hbm_refs, out_refs = refs[:3], refs[4 : 4 + count]
    row_refs, block_refs, sems = refs[4 + count : 7 + count], refs[7 + count : -1], refs[-1]
    copies = [
        pltpu.make_async_copy(source, target, sems.at[i])
        for i, (source, target) in enumerate(zip(hbm_refs, row_refs))
    ]
    for copy in copies:
        copy.start()
    out_copies = []
    for i, row_ref in enumerate(row_refs):
        copies[i].wait()
        for index, pack in enumerate(packs):
            place = 3 * index + i
            block_refs[place][...] = row_ref[:, 0, pack.start : pack.stop]
            out_copies.append(pltpu.make_async_copy(block_refs[place], out_refs[place], sems.at[3 + place]))
            out_copies[-1].start()
    for copy in out_copies:
        copy.wait()


def adam_kernel(count, pack, spare_value, scales_ref, own_ref, *refs):
    other_refs, refs = refs[:count], refs[count:]
    (params_ref, first_ref, second_ref), (grad_ref, moved_ref, sent_ref) = refs[:3], refs[-3:]
    rows = pack.rows
    total = own_ref[...]
    for other_ref in other_refs:
        total = total + pack.read(other_ref)
    grad_ref[...] = total * scales_ref[2]
    grad = grad_ref[:rows, :]
    first_new = BETA_ONE * first_ref[...] + (1.0 - BETA_ONE) * grad
    second_new = BETA_TWO * second_ref[...] + (1.0 - BETA_TWO) * grad * grad
    update = (scales_ref[0] * first_new) / (jnp.sqrt(second_new * scales_ref[1]) + ADAM_EPS)
    value = scales_ref[3] if spare_value else 0.0
    moved_ref[rows // 8 * 8 :, :] = jnp.full((pack.deep - rows // 8 * 8, pack.columns), value, jnp.float32)
    moved_ref[:rows, :] = params_ref[...] - update
    pack.write(sent_ref, moved_ref[...])


def half_average_kernel(pack, moved_ref, other_ref, mean_ref, push_out_ref):
    mean = 0.5 * (moved_ref[...] + pack.read(other_ref))
    mean_ref[...] = mean
    push_out_ref[...] = mean[pack.rows, :1]


def moments_kernel(packs, first_hbm, second_hbm, *refs):
    grad_refs, (first_out, second_out, first_ref, second_ref, sems) = refs[: len(packs)], refs[len(packs) :]
    copies = [
        pltpu.make_async_copy(first_hbm, first_ref, sems.at[0]),
        pltpu.make_async_copy(second_hbm, second_ref, sems.at[1]),
    ]
    for copy in copies:
        copy.start()
    rows = first_ref.shape[0]
    grad = jnp.concatenate([grad_ref[:rows, :] for grad_ref in grad_refs], axis=1)
    copies[0].wait()
    first_out[:, 0, :] = BETA_ONE * first_ref[:, 0, :] + (1.0 - BETA_ONE) * grad
    copies[1].wait()
    second_out[:, 0, :] = BETA_TWO * second_ref[:, 0, :] + (1.0 - BETA_TWO) * grad * grad


def average_kernel(pack, mean_ref, moved_ref, other_ref, out_ref, rows_ref, sem):
    rows = out_ref.shape[0]
    later = 0.5 * (moved_ref[...] + pack.read(other_ref))
    rows_ref[:, 0, :] = jnp.concatenate([mean_ref[...], later], axis=1)[:rows]
    copy = pltpu.make_async_copy(rows_ref, out_ref, sem)
    copy.start()
    copy.wait()


SCALARS = pl.BlockSpec(memory_space=pltpu.SMEM)
BLOCKS = pl.BlockSpec(memory_space=pltpu.VMEM)
TOKEN = pl.BlockSpec(memory_space=pl.ANY)
IN_HBM = pl.BlockSpec(memory_space=pltpu.HBM)


def call(kernel, name, outs, specs, operands, scratch=(), out_specs=None, flops=0, elements=0):
    return pl.pallas_call(
        kernel,
        out_shape=outs,
        in_specs=specs,
        out_specs=out_specs or jax.tree.map(lambda _: BLOCKS, outs),
        scratch_shapes=list(scratch),
        compiler_params=pltpu.CompilerParams(vmem_limit_bytes=VMEM_BYTES),
        cost_estimate=pl.CostEstimate(flops=flops, bytes_accessed=8 * elements, transcendentals=elements),
        name=name,
    )(*operands)


def stay(array):
    return pltpu.with_memory_space_constraint(array, pltpu.HBM)


def moved_on(block, axis, distance):
    size = lax.axis_size(axis)
    return lax.ppermute(block, axis, [(i, (i + distance) % size) for i in range(size)])


def exchanged(block, axis, bit):
    return lax.ppermute(block, axis, [(i, i ^ bit) for i in range(lax.axis_size(axis))])


def lowest_bit(slot):
    return slot & -slot


def hold_kernel(block_ref, token_ref, out_ref):
    out_ref[...] = block_ref[...]


def gathered(piece, shards, token=None):
    held = [piece]
    for slot in range(1, shards):
        bit = lowest_bit(slot)
        held.append(exchanged(held[slot ^ bit], "dp", bit))
        if token is not None and slot == 2:
            shape = jax.ShapeDtypeStruct(piece.shape, piece.dtype)
            held[slot] = call(hold_kernel, "hold", shape, [BLOCKS, IN_HBM], (held[slot], stay(token)))
    return held


def scattered(parts, shards):
    arrived = [[] for _ in parts]
    token, straight = None, []
    for part, held in enumerate(parts):
        last = part == len(parts) - 1
        slots = sorted(range(2, shards), key=lambda slot: (-slot.bit_count(), -slot))
        for slot in slots:
            bit = lowest_bit(slot)
            other = exchanged(held[slot], "dp", bit)
            if slot == bit:
                arrived[part].append(other)
                continue
            if None in held:
                held.update(held.pop(None)(token))
            through = [shares[1] for shares in parts] if last else []
            shapes = [jax.ShapeDtypeStruct(array.shape, array.dtype) for array in (other, *through)]
            made = call(
                merge_kernel,
                "merge",
                tuple(shapes),
                [BLOCKS] * (2 + len(through)),
                (held[slot ^ bit], other, *through),
            )
            held[slot ^ bit], straight, token = made[0], made[1:], made[0]
    for part, piece in enumerate(straight or [shares[1] for shares in parts]):
        arrived[part].append(exchanged(piece, "dp", 1))
    return arrived


def column_cuts(channels):
    half = (channels // GSIZE + 1) // 2 * GSIZE
    return [(0, half), (half, channels)]


def local(
    block_input, time_shift, out_grad, params, first_moment, second_moment, push_weight, step
):
    samples, positions, channels = block_input.shape
    tokens = samples * positions
    shards = lax.axis_size("dp")
    rows = params.shape[1]
    deep = packed_rows(rows)
    me = lax.axis_index("dp").astype(jnp.int32).reshape(1)
    packs = [Packing(rows, start, stop) for start, stop in column_cuts(channels)]
    params, first_moment, second_moment = (
        jnp.transpose(array, (1, 0, 2)) for array in (params, first_moment, second_moment)
    )
    def shards_of(pack, *tokens, late=None):
        piece = call(
            functools.partial(cast_kernel, pack),
            "cast",
            pack.payload(),
            [BLOCKS, BLOCKS, TOKEN, TOKEN],
            (push_weight.reshape(1, 1), params, *tokens),
            scratch=[pltpu.VMEM((deep, pack.columns), jnp.float32)],
            elements=rows * pack.columns,
        )
        return gathered(piece, shards, late)

    level_count = lax.axis_size("replica").bit_length() - 1
    distance_bits = step[0] % level_count
    step_count = (step[0] + 1).astype(jnp.float32)
    scales = jnp.stack(
        [
            LEARN_RATE / (1.0 - jnp.power(BETA_ONE, step_count)),
            1.0 / (1.0 - jnp.power(BETA_TWO, step_count)),
            jnp.float32(1.0 / shards),
            push_weight[0],
        ]
    )

    activation, mean_in, inverse_in, same_group, *pieces = call(
        functools.partial(norm_in_kernel, shards, packs),
        "norm_in",
        (
            jax.ShapeDtypeStruct((shards * deep, tokens), jnp.bfloat16),
            jax.ShapeDtypeStruct((samples, channels), jnp.float32),
            jax.ShapeDtypeStruct((samples, channels), jnp.float32),
            jax.ShapeDtypeStruct((max(pack.columns for pack in packs),) * 2, jnp.bfloat16),
            *(jax.ShapeDtypeStruct((samples, pack.columns), jnp.float32) for pack in packs),
            *(jax.ShapeDtypeStruct((samples, positions, pack.columns), jnp.bfloat16) for pack in packs),
        ),
        [SCALARS, SCALARS, BLOCKS, IN_HBM, IN_HBM],
        (me, scales, time_shift, stay(block_input), stay(out_grad)),
        scratch=[
            pltpu.VMEM(block_input.shape, jnp.bfloat16),
            pltpu.VMEM(out_grad.shape, jnp.bfloat16),
            pltpu.SemaphoreType.DMA((2,)),
        ],
        elements=tokens * channels,
    )

    columns = [pack.columns for pack in packs for _ in range(3)]
    blocks = call(
        functools.partial(cut_kernel, packs),
        "cut",
        tuple(pltpu.HBM((rows, width), jnp.float32) for width in columns),
        [IN_HBM] * 3 + [TOKEN],
        (stay(params), stay(first_moment), stay(second_moment), mean_in),
        scratch=[pltpu.VMEM(params.shape, jnp.float32)] * 3
        + [pltpu.VMEM((rows, width), jnp.float32) for width in columns]
        + [pltpu.SemaphoreType.DMA((3 + len(columns),))],
        out_specs=(IN_HBM,) * len(columns),
        elements=rows * channels,
    )
    weights = [shards_of(packs[0], params, params)]
    weights.append(shards_of(packs[1], weights[0][1], mean_in, late=blocks[-1]))
    hidden_grads, full_weights, parts = [], [], []
    token = mean_in
    shifts, out_grads = pieces[: len(packs)], pieces[len(packs) :]
    for pack, shard_list, shift, out_grad_piece in zip(packs, weights, shifts, out_grads):
        kept = jax.ShapeDtypeStruct if pack is packs[-1] else pltpu.HBM
        kept_spec = BLOCKS if pack is packs[-1] else IN_HBM
        later = range(shards - 1) if pack is packs[-1] and shards > 2 else range(0)
        slots = [slot for slot in range(shards) if slot not in later]

        def made(slots, pack=pack):
            return tuple(pack.payload() if slot else pack.block() for slot in slots)

        grad_hidden, full_weight, *shares = call(
            functools.partial(mix_kernel, shards, pack, slots),
            "mix",
            (kept((tokens, pack.columns), jnp.bfloat16), kept((shards * deep, pack.columns), jnp.bfloat16))
            + made(slots),
            [BLOCKS] * (4 + shards) + [TOKEN],
            (activation, shift, out_grad_piece, same_group, *shard_list, token),
            scratch=[
                pltpu.VMEM((shards * deep, pack.columns), jnp.bfloat16),
                pltpu.VMEM((tokens, pack.columns), jnp.bfloat16),
                pltpu.VMEM((tokens, pack.columns), jnp.float32),
                pltpu.VMEM((tokens, pack.columns), jnp.float32),
                pltpu.SemaphoreType.DMA((2,)),
            ],
            out_specs=(kept_spec,) * 2 + (BLOCKS,) * len(slots),
            flops=4 * tokens * channels * pack.columns,
            elements=tokens * pack.columns,
        )
        shares = dict(zip(slots, shares))
        if later:
            def rest(token, pack=pack, later=tuple(later), outs=made(later), grad_hidden=grad_hidden):
                shares = call(
                    functools.partial(rest_kernel, pack, later),
                    "rest",
                    outs,
                    [BLOCKS] * 2 + [TOKEN],
                    (activation, grad_hidden, token),
                    flops=2 * tokens * channels * pack.columns,
                )
                return dict(zip(later, shares))

            shares[None] = rest
        token = shares[slots[-1]]
        hidden_grads.append(grad_hidden)
        full_weights.append(full_weight)
        parts.append(shares)

    def input_grad(carried, *operands):
        return call(
            functools.partial(input_grad_kernel, shards, packs, len(carried)),
            "input_grad",
            (pltpu.HBM(block_input.shape, jnp.bfloat16),)
            + tuple(jax.ShapeDtypeStruct(array.shape, array.dtype) for array in carried),
            [SCALARS] + [BLOCKS] * 3 + [IN_HBM] + [BLOCKS] * (2 * len(packs)) + [IN_HBM] * len(carried),
            operands[:4] + (stay(operands[4]),) + operands[5:] + tuple(map(stay, carried)),
            scratch=[
                pltpu.VMEM((channels, max(pack.columns for pack in packs)), jnp.float32),
                pltpu.VMEM(block_input.shape, jnp.bfloat16),
                pltpu.VMEM(block_input.shape, jnp.bfloat16),
                pltpu.VMEM((tokens, channels), jnp.float32),
                pltpu.SemaphoreType.DMA((1 + samples,)),
                pltpu.SemaphoreType.DMA((len(carried),)),
            ],
            out_specs=(IN_HBM,) + (BLOCKS,) * len(carried),
            flops=2 * tokens * channels * channels,
            elements=tokens * channels,
        )

    def moments(*grads):
        return call(
            functools.partial(moments_kernel, packs),
            "moments",
            (jax.ShapeDtypeStruct(params.shape, jnp.float32),) * 2,
            [IN_HBM] * 2 + [BLOCKS] * len(packs),
            (stay(first_moment), stay(second_moment), *grads),
            scratch=[pltpu.VMEM(params.shape, jnp.float32)] * 2 + [pltpu.SemaphoreType.DMA((2,))],
            elements=rows * channels,
        )

    def from_behind(finish, *operands):
        def branch(distance):
            return lambda *values: finish(lambda block: moved_on(block, "replica", distance), *values)

        return lax.switch(distance_bits, [branch(1 << power) for power in range(level_count)], *operands)

    grad_input, *early_blocks = input_grad(
        blocks[:3], me, mean_in, inverse_in, same_group, block_input, *hidden_grads, *full_weights
    )
    arrived = scattered(parts, shards)
    owns = [shares[0] for shares in parts]
    early, late = packs

    def adam(pack, own, others, blocks):
        return call(
            functools.partial(adam_kernel, len(others), pack, pack is early),
            "adam",
            (pack.block(), pack.block(), pack.payload()),
            [SCALARS] + [BLOCKS] * (4 + len(others)),
            (scales, own, *others, *blocks),
            elements=rows * pack.columns,
        )

    grad_a, moved_a, sent_a = adam(early, owns[0], arrived[0], early_blocks)

    def finish(move, sent, grad_a, moved_a, own, *operands):
        other_a = move(sent)
        grad_b, moved_b, sent_b = adam(late, own, operands[:-3], operands[-3:])
        other_b = move(sent_b)
        mean, weight = call(
            functools.partial(half_average_kernel, early),
            "half_average",
            (early.block(), jax.ShapeDtypeStruct((1,), jnp.float32)),
            [BLOCKS] * 2,
            (moved_a, other_a),
            elements=rows * early.columns,
        )
        averaged = call(
            functools.partial(average_kernel, late),
            "average",
            pltpu.HBM(params.shape, jnp.float32),
            [BLOCKS] * 3,
            (mean, moved_b, other_b),
            scratch=[pltpu.VMEM(params.shape, jnp.float32), pltpu.SemaphoreType.DMA],
            out_specs=IN_HBM,
            elements=rows * channels,
        )
        return (*moments(grad_a, grad_b), averaged, weight)

    first_new, second_new, averaged, new_weight = from_behind(
        finish, sent_a, grad_a, moved_a, owns[1], *arrived[1], *blocks[3:]
    )
    return (
        grad_input,
        *(jnp.transpose(array, (1, 0, 2)) for array in (averaged, first_new, second_new)),
        new_weight,
    )


def solution(mesh):
    placed = (
        P(("replica", "dp"), None, None),
        P(("replica", "dp"), None),
        P(("replica", "dp"), None, None),
        P("replica", "dp", None),
        P("replica", "dp", None),
        P("replica", "dp", None),
        P("replica"),
        P(),
    )
    return jax.shard_map(
        local,
        mesh=mesh,
        in_specs=placed,
        out_specs=(
            P(("replica", "dp"), None, None),
            P("replica", "dp", None),
            P("replica", "dp", None),
            P("replica", "dp", None),
            P("replica"),
        ),
        check_vma=False,
    )
```
